32 devices in a mesh: phase: 8 (over y, x, core), space: 4 (over z).
Axes of the slice: x: 2, y: 2, z: 4, core: 2. Of those that a mesh axis runs over, the one named last changes fastest.
Arguments:
- volume: bfloat16 [8, 16, 4, 32, 256], P('phase', 'space'), may hold values from -6 to 6
- gain_first: float32 [256], replicated, may hold values from 0.25 to 1.75
- phase_qkv: bfloat16 [256, 768], replicated, may hold values from -0.375 to 0.375
- phase_out: bfloat16 [256, 256], replicated, may hold values from -0.375 to 0.375
- bin_phase: int32 [8], replicated, may hold values from 0 to 7, each once
- phase_bias: float32 [8, 8], replicated, may hold values from -4 to 304
- gain_second: float32 [256], replicated, may hold values from 0.25 to 1.75
- window_qkv: bfloat16 [256, 768], replicated, may hold values from -0.375 to 0.375
- window_out: bfloat16 [256, 256], replicated, may hold values from -0.375 to 0.375
- window_corner: int32 [8, 3], replicated, may hold values from -3 to 0
- window_bias: float32 [8, 64], replicated, may hold values from -4 to 304
- gain_third: float32 [256], replicated, may hold values from 0.25 to 1.75
- mlp_up: bfloat16 [256, 1024], replicated, may hold values from -0.375 to 0.375
- mlp_down: bfloat16 [1024, 256], replicated, may hold values from -0.1875 to 0.1875
Outputs:
- layer_out: bfloat16 [8, 16, 4, 32, 256], P('phase', 'space')
The draws below stay inside these ranges and needn't reach their ends.
Inputs may be any that keep to these rules, and one draw needn't show every extreme that they name: `bin_phase`: each phase 0 to 7 is held by exactly one bin. `window_corner`: head h's window covers corner to corner + 3 along each dimension.
All inputs are finite; a program needn't handle non-finite values.
Results may differ from the reference program's by a relative error of at most 0.012.
Values may be sent and summed in bfloat16 or wider, within the bound.
No kernel may reach another device: no remote copies, remote signals or barrier semaphores. Data moves between devices by JAX's collectives and lax.ppermute only.
A program may use at most 128 MiB of HBM per device.

```python
import math
import jax
import jax.numpy as jnp
from jax import lax

D = 256
HEADS = 8
FF = 1024
GX = 4
GY = 32
BINS = 8
NZ = 16


def bias_table(key, row_count, col_count):
    fourth = jax.random.fold_in(key, 3)
    return jnp.clip(jax.random.normal(fourth, (row_count, col_count)), -4.0, 4.0)


def draw_phase_bias(key, part):
    return bias_table(jax.random.fold_in(key, 11), HEADS, BINS).astype(jnp.float32)


def draw_window_bias(key, part):
    return bias_table(jax.random.fold_in(key, 23), HEADS, 64).astype(jnp.float32)


def with_ends(array, key, least, largest):
    place = [jax.random.randint(jax.random.fold_in(key, axis), (), 0, length) for axis, length in enumerate(array.shape)]
    longest = array.shape.index(max(array.shape))
    beside = place[:longest] + [(place[longest] + 1) % array.shape[longest]] + place[longest + 1:]
    return array.at[tuple(place)].set(least).at[tuple(beside)].set(largest)


def block_scale(rng, extent, cuts, low, high):
    level, own = 1.0, jax.random.fold_in(rng, 6)
    for axis_at, blocks in cuts:
        heights = jnp.exp(jax.random.uniform(jax.random.fold_in(own, axis_at), (blocks,), jnp.float32, low / len(cuts), high / len(cuts)))
        level = level * jnp.repeat(heights, extent[axis_at] // blocks).reshape([-1 if axis == axis_at else 1 for axis in range(len(extent))])
    return level


def gaussian(stream_key, dims, scale, reach, shards=(), kind=jnp.bfloat16):
    loudness = block_scale(stream_key, dims, shards, -0.22, 0.18) if shards else 1.0
    entries = jax.random.normal(stream_key, dims, jnp.float32) * scale * loudness
    return jnp.minimum(jnp.maximum(entries, -reach), reach).astype(kind)


def setup_inputs(seed: int = 0) -> dict:
    splits = jax.random.split(jax.random.key(seed), 15)
    volume = gaussian(splits[0], (BINS, NZ, GX, GY, D), 1.0, 6.0, ((0, 8), (1, 4)))
    gain_first = jnp.clip(1.0 + 0.15 * jax.random.normal(splits[1], (D,), jnp.float32), 0.25, 1.75)
    phase_qkv = gaussian(splits[2], (D, 3 * D), D ** -0.5, 0.375)
    phase_out = gaussian(splits[3], (D, D), D ** -0.5, 0.375)
    bin_phase = jax.random.permutation(splits[4], BINS).astype(jnp.int32)
    phase_bias = draw_phase_bias(jax.random.fold_in(splits[14], 71), 0)
    gain_second = jnp.clip(1.0 + 0.15 * jax.random.normal(splits[6], (D,), jnp.float32), 0.25, 1.75)
    window_qkv = gaussian(splits[7], (D, 3 * D), D ** -0.5, 0.375)
    window_out = gaussian(splits[8], (D, D), D ** -0.5, 0.375)
    window_corner = with_ends(jax.random.randint(splits[9], (HEADS, 3), -3, 1), jax.random.fold_in(splits[9], 1), -3, 0).astype(jnp.int32)
    window_bias = draw_window_bias(jax.random.fold_in(splits[14], 71), 0)
    gain_third = jnp.clip(1.0 + 0.15 * jax.random.normal(splits[11], (D,), jnp.float32), 0.25, 1.75)
    mlp_up = gaussian(splits[12], (D, FF), D ** -0.5, 0.375)
    mlp_down = gaussian(splits[13], (FF, D), FF ** -0.5, 0.1875)
    return {"volume": volume, "gain_first": gain_first, "phase_qkv": phase_qkv, "phase_out": phase_out, "bin_phase": bin_phase, "phase_bias": phase_bias, "gain_second": gain_second, "window_qkv": window_qkv, "window_out": window_out, "window_corner": window_corner, "window_bias": window_bias, "gain_third": gain_third, "mlp_up": mlp_up, "mlp_down": mlp_down}


EPSILON = 1e-06

def rms_norm(values, gain):
    mean_sq = lax.optimization_barrier(jnp.mean(values * values, axis=-1, keepdims=True))
    return values * lax.rsqrt(mean_sq + EPSILON) * gain

def head_matrix(model_width, head_count):
    column = lax.broadcasted_iota(jnp.int32, (model_width, head_count), 0) // (model_width // head_count)
    target = lax.broadcasted_iota(jnp.int32, (model_width, head_count), 1)
    return (column == target).astype(jnp.float32)

def window_attend(queries, keys_ext, window_corner, window_bias, z_first, depth):
    planes, extent_x, extent_y, model_width = queries.shape
    head_count = window_corner.shape[0]
    head_dim = model_width // head_count
    score_scale = 1.0 / math.sqrt(head_dim)
    padded = jnp.pad(keys_ext, ((0, 0), (3, 3), (3, 3), (0, 0)))
    corner = window_corner.astype(jnp.int32)
    key_parts = []
    value_parts = []
    for member in range(head_count):
        anchor = ((corner[member, 0] + 3).astype(jnp.int32), (corner[member, 1] + 3).astype(jnp.int32), (corner[member, 2] + 3).astype(jnp.int32))
        key_start = jnp.asarray(member * head_dim, dtype=jnp.int32)
        value_start = jnp.asarray(model_width + member * head_dim, dtype=jnp.int32)
        sizes_here = (planes + 3, extent_x + 3, extent_y + 3, head_dim)
        key_parts.append(lax.dynamic_slice(padded, anchor + (key_start,), sizes_here))
        value_parts.append(lax.dynamic_slice(padded, anchor + (value_start,), sizes_here))
    key_shift = jnp.concatenate(key_parts, axis=3)
    value_shift = jnp.concatenate(value_parts, axis=3)
    summer = head_matrix(model_width, head_count)
    z_index = z_first + lax.broadcasted_iota(jnp.int32, (planes, 1, 1, 1), 0) + corner[:, 0]
    x_index = lax.broadcasted_iota(jnp.int32, (1, extent_x, 1, 1), 1) + corner[:, 1]
    y_index = lax.broadcasted_iota(jnp.int32, (1, 1, extent_y, 1), 2) + corner[:, 2]
    query_float = queries.astype(jnp.float32)
    score_list = []
    for neighbor in range(64):
        step_z, step_x, step_y = (neighbor // 16, neighbor // 4 % 4, neighbor % 4)
        keys_here = key_shift[step_z:step_z + planes, step_x:step_x + extent_x, step_y:step_y + extent_y]
        raw_score = jnp.dot(query_float * keys_here.astype(jnp.float32), summer, precision=lax.Precision.HIGHEST) * score_scale + window_bias[:, neighbor]
        inside = (z_index + step_z >= 0) & (z_index + step_z < depth) & (x_index + step_x >= 0) & (x_index + step_x < extent_x) & (y_index + step_y >= 0) & (y_index + step_y < extent_y)
        score_list.append(jnp.where(inside, raw_score, -1e+30))
    weights = jax.nn.softmax(jnp.stack(score_list), axis=0).astype(jnp.bfloat16)
    accumulated = jnp.zeros(queries.shape, jnp.float32)
    for neighbor in range(64):
        step_z, step_x, step_y = (neighbor // 16, neighbor // 4 % 4, neighbor % 4)
        values_here = value_shift[step_z:step_z + planes, step_x:step_x + extent_x, step_y:step_y + extent_y]
        spread = jnp.dot(weights[neighbor].astype(jnp.float32), summer.T, precision=lax.Precision.HIGHEST)
        accumulated = accumulated + spread * values_here.astype(jnp.float32)
    return accumulated.astype(jnp.bfloat16)

def reference(volume, gain_first, phase_qkv, phase_out, bin_phase, phase_bias, gain_second, window_qkv, window_out, window_corner, window_bias, gain_third, mlp_up, mlp_down):
    bin_count, depth, extent_x, extent_y, model_width = volume.shape
    head_count = window_corner.shape[0]
    head_dim = model_width // head_count
    score_scale = 1.0 / math.sqrt(head_dim)
    stream = volume.astype(jnp.float32).reshape(-1, model_width)
    normed_one = rms_norm(stream, gain_first).astype(jnp.bfloat16)
    triple = jnp.dot(normed_one, phase_qkv, preferred_element_type=jnp.float32).astype(jnp.bfloat16)
    triple = triple.reshape(bin_count, -1, 3 * model_width)
    token_count = triple.shape[1]
    queries = triple[..., :model_width].astype(jnp.float32).reshape(bin_count, token_count, head_count, head_dim)
    key_all = triple[..., model_width:2 * model_width].astype(jnp.float32).reshape(bin_count, token_count, head_count, head_dim)
    value_all = triple[..., 2 * model_width:].astype(jnp.float32).reshape(bin_count, token_count, head_count, head_dim)
    phase_gap = (bin_phase[None, :] - bin_phase[:, None]) % bin_count
    onehot = (phase_gap[:, :, None] == jnp.arange(bin_count, dtype=jnp.int32)[None, None, :]).astype(jnp.float32)
    bias_all = jnp.einsum('bck,hk->bch', onehot, phase_bias.astype(jnp.float32), precision=lax.Precision.HIGHEST)

    def per_bin(member):
        query_bin, bias_bin = member
        scores = jnp.einsum('phd,cphd->chp', query_bin, key_all) * score_scale + bias_bin[:, :, None]
        rounded = jax.nn.softmax(scores, axis=0).astype(jnp.bfloat16)
        rounded = lax.optimization_barrier(rounded)
        return jnp.einsum('chp,cphd->phd', rounded.astype(jnp.float32), value_all).astype(jnp.bfloat16)
    phase_mixed = lax.map(per_bin, (queries, bias_all)).reshape(-1, model_width)
    residual_one = stream + jnp.dot(phase_mixed, phase_out, preferred_element_type=jnp.float32)
    normed_two = rms_norm(residual_one, gain_second).astype(jnp.bfloat16)
    triple_two = jnp.dot(normed_two, window_qkv, preferred_element_type=jnp.float32).astype(jnp.bfloat16)
    triple_two = triple_two.reshape(bin_count, depth, extent_x, extent_y, 3 * model_width)

    def per_volume(block):
        keys_ext = jnp.pad(block[..., model_width:], ((3, 3), (0, 0), (0, 0), (0, 0)))
        return window_attend(block[..., :model_width], keys_ext, window_corner, window_bias, 0, depth)
    windowed = lax.map(per_volume, triple_two).reshape(-1, model_width)
    residual_two = residual_one + jnp.dot(windowed, window_out, preferred_element_type=jnp.float32)
    normed_three = rms_norm(residual_two, gain_third).astype(jnp.bfloat16)
    hidden = jax.nn.gelu(jnp.dot(normed_three, mlp_up, preferred_element_type=jnp.float32), approximate=True).astype(jnp.bfloat16)
    layer_out = residual_two + jnp.dot(hidden, mlp_down, preferred_element_type=jnp.float32)
    return layer_out.astype(jnp.bfloat16).reshape(volume.shape)
```

```python
import functools
import math

import jax
import jax.numpy as jnp
from jax import lax
from jax.experimental import pallas as pl
from jax.experimental.pallas import tpu as pltpu
from jax.sharding import PartitionSpec as P

EPSILON = 1e-06
LOG2E = math.log2(math.e)
NEG = -1e30
SPAN = 4
REACH = SPAN - 1
ROWS = 16
VMEM_LIMIT = 56 * 1024 * 1024

NT = (((1,), (1,)), ((), ()))
TN = (((0,), (0,)), ((), ()))


def mm(a, b, dims=(((1,), (0,)), ((), ()))):
    return lax.dot_general(a, b, dims, preferred_element_type=jnp.float32)


def rms(values, gain):
    mean_sq = jnp.mean(values * values, axis=-1, keepdims=True)
    return (values * lax.rsqrt(mean_sq + EPSILON) * gain).astype(jnp.bfloat16)


def prep_kernel(
    bins,
    extent_x,
    extent_y,
    bin_phase,
    corner,
    window_bias,
    phase_bias,
    phase_qkv,
    window_qkv,
    phase_qv,
    window_qv,
    phase_table,
    window_table,
):
    width = phase_qkv.shape[0]
    heads = phase_bias.shape[0]
    for source, target in ((phase_qkv, phase_qv), (window_qkv, window_qv)):
        target[:width] = source[:, :width].T
        target[width:] = source[:, 2 * width :].T
    me = lax.axis_index("phase")
    tile = ROWS * bins
    slot = lax.broadcasted_iota(jnp.int32, (heads, tile), 1) // ROWS
    query_phase = jnp.zeros((heads, tile), jnp.int32)
    for member in range(bins):
        query_phase = jnp.where(slot == member, bin_phase[me ^ member], query_phase)
    same = (
        lax.broadcasted_iota(jnp.int32, (ROWS, tile), 0)
        == lax.broadcasted_iota(jnp.int32, (ROWS, tile), 1) % ROWS
    )
    bias = phase_bias[...] * LOG2E
    for member in range(bins):
        gap = bin_phase[me ^ member] - query_phase
        gap = jnp.where(gap < 0, gap + bins, gap)
        value = jnp.zeros((heads, tile), jnp.float32)
        for step in range(bins):
            value = jnp.where(gap == step, bias[:, step : step + 1], value)
        for head in range(heads):
            phase_table[
                head // 2,
                member * ROWS : (member + 1) * ROWS,
                (head % 2) * tile : (head % 2 + 1) * tile,
            ] = jnp.where(same, value[head : head + 1], NEG)
    plane = extent_x * extent_y
    shape = (extent_y, plane)
    lane = lax.broadcasted_iota(jnp.int32, shape, 1)
    lane_x = lane // extent_y
    delta_y = lax.broadcasted_iota(jnp.int32, shape, 0) - lane % extent_y
    for head in range(heads):
        first_x = corner[head, 1]
        first_y = corner[head, 2]
        y_masks = [delta_y == first_y + step for step in range(SPAN)]
        for step_z in range(SPAN):
            strips = []
            for step_x in range(SPAN):
                strip = jnp.full(shape, NEG, jnp.float32)
                for step_y in range(SPAN):
                    entry = window_bias[head, (step_z * SPAN + step_x) * SPAN + step_y] * LOG2E
                    strip = jnp.where(y_masks[step_y], entry, strip)
                strips.append(strip)
            for key_x in range(extent_x):
                block = jnp.full(shape, NEG, jnp.float32)
                for step_x in range(SPAN):
                    block = jnp.where(
                        lane_x == key_x - first_x - step_x, strips[step_x], block
                    )
                start = step_z * plane + key_x * extent_y
                window_table[
                    head // 2,
                    start : start + extent_y,
                    (head % 2) * plane : (head % 2 + 1) * plane,
                ] = block


def pair_attend(keys, queries, values, table, head_dim):
    count = queries.shape[1] // 2
    scores = mm(keys, queries) + table
    top = jnp.max(scores, axis=0, keepdims=True)
    weights = jnp.exp2(scores - top).astype(jnp.bfloat16)
    mixed = mm(values, weights)
    inverse = 1.0 / mixed[2 * head_dim : 2 * head_dim + 1]
    return jnp.concatenate(
        [
            mixed[:head_dim, :count] * inverse[:, :count],
            mixed[head_dim : 2 * head_dim, count:] * inverse[:, count:],
        ],
        axis=0,
    ).astype(jnp.bfloat16)


def block_diagonal(queries, base, head_dim, group):
    count = queries.shape[1]
    frame = base // group * group
    columns = []
    for member in range(2):
        first = base + member * head_dim - frame
        parts = []
        if first:
            parts.append(jnp.zeros((first, count), queries.dtype))
        parts.append(queries[frame + first : frame + first + head_dim])
        rest = group - first - head_dim
        if rest:
            parts.append(jnp.zeros((rest, count), queries.dtype))
        columns.append(jnp.concatenate(parts, axis=0))
    return jnp.concatenate(columns, axis=1)


def phase_kernel(bins, heads, *refs):
    blocks = refs[: bins // 2]
    gain, qkv, qv, table, out_weight = refs[bins // 2 : bins // 2 + 5]
    outs = refs[bins // 2 + 5 :]
    chunk, width = blocks[0].shape[1:]
    head_dim = width // heads
    scale = LOG2E / math.sqrt(head_dim)
    tile = ROWS * bins
    tiles = chunk // ROWS
    stream = jnp.concatenate(
        [
            blocks[slot // 2][slot % 2, step * ROWS : (step + 1) * ROWS]
            for step in range(tiles)
            for slot in range(bins)
        ],
        axis=0,
    ).astype(jnp.float32)
    normed = rms(stream, gain[...])
    keys = mm(normed, qkv[:, width : 2 * width]).astype(jnp.bfloat16)
    both = mm(qv[...], normed, NT)
    queries = (both[:width] * scale).astype(jnp.bfloat16)
    values = both[width:].astype(jnp.bfloat16)
    ones = jnp.ones((ROWS, tile), jnp.bfloat16)
    group = 128
    for step in range(tiles):
        span = slice(step * tile, (step + 1) * tile)
        parts = []
        for pair in range(heads // 2):
            base = pair * 2 * head_dim
            frame = base // group * group
            parts.append(
                pair_attend(
                    keys[span, frame : frame + group],
                    block_diagonal(queries[:, span], base, head_dim, group),
                    jnp.concatenate([values[base : base + 2 * head_dim, span], ones], axis=0),
                    table[pair],
                    head_dim,
                )
            )
        mixed = jnp.concatenate(parts, axis=0)
        result = (stream[span] + mm(mixed, out_weight[...], TN)).astype(jnp.bfloat16)
        for slot in range(bins):
            outs[slot // 2][slot % 2, step * ROWS : (step + 1) * ROWS] = result[
                slot * ROWS : (slot + 1) * ROWS
            ]


def window_kernel(
    plane,
    corner,
    own,
    low,
    high,
    gain_second,
    qkv,
    qv,
    table,
    out_weight,
    gain_third,
    mlp_up,
    mlp_down,
    out,
    key_store,
    value_store,
):
    tokens, width = own.shape
    planes = tokens // plane
    heads = corner.shape[0]
    head_dim = width // heads
    scale = LOG2E / math.sqrt(head_dim)
    reach = REACH * plane
    group = 128
    gain = gain_second[...]
    stream = own[...].astype(jnp.float32)
    normed = jnp.concatenate(
        [
            rms(low[...].astype(jnp.float32), gain),
            rms(stream, gain),
            rms(high[...].astype(jnp.float32), gain),
        ],
        axis=0,
    )
    key_store[...] = mm(normed, qkv[:, width : 2 * width]).astype(jnp.bfloat16)
    value_store[...] = mm(qv[width:], normed, NT).astype(jnp.bfloat16)
    queries = (mm(qv[:width], normed[reach : reach + tokens], NT) * scale).astype(jnp.bfloat16)
    z_first = lax.axis_index("space") * planes
    depth = lax.axis_size("space") * planes
    span = (planes + REACH) * plane
    reach_keys = SPAN * plane
    lane = lax.broadcasted_iota(jnp.int32, (1, group), 1)
    lane_head = lax.broadcasted_iota(jnp.int32, (1, 2 * plane), 1) // plane
    ones = jnp.ones((ROWS, span), jnp.bfloat16)
    pair_keys = []
    pair_values = []
    for pair in range(heads // 2):
        base = pair * 2 * head_dim
        frame = base // group * group
        first = [
            pl.multiple_of((corner[2 * pair + member, 0] + REACH) * plane, plane)
            for member in range(2)
        ]
        left = key_store[pl.ds(first[0], span), frame : frame + group]
        right = key_store[pl.ds(first[1], span), frame : frame + group]
        is_left = (lane < base + head_dim - frame).astype(jnp.bfloat16)
        pair_keys.append(left * is_left + right * (1 - is_left))
        pair_values.append(
            jnp.concatenate(
                [
                    value_store[
                        base + member * head_dim : base + (member + 1) * head_dim,
                        pl.ds(first[member], span),
                    ]
                    for member in range(2)
                ]
                + [ones],
                axis=0,
            )
        )
    for at in range(planes):
        here = slice(at * plane, (at + 1) * plane)
        parts = []
        for pair in range(heads // 2):
            base = pair * 2 * head_dim
            penalties = []
            for step in range(SPAN):
                outside = []
                for member in range(2):
                    z = z_first + at + step + corner[2 * pair + member, 0]
                    outside.append(jnp.where((z >= 0) & (z < depth), 0.0, NEG))
                penalties.append(
                    jnp.broadcast_to(
                        jnp.where(lane_head == 0, outside[0], outside[1]), (plane, 2 * plane)
                    )
                )
            parts.append(
                pair_attend(
                    pair_keys[pair][at * plane : at * plane + reach_keys],
                    block_diagonal(queries[:, here], base, head_dim, group),
                    pair_values[pair][:, at * plane : at * plane + reach_keys],
                    table[pair] + jnp.concatenate(penalties, axis=0),
                    head_dim,
                )
            )
        mixed = jnp.concatenate(parts, axis=0)
        residual = stream[here] + mm(mixed, out_weight[...], TN)
        hidden = jax.nn.gelu(mm(rms(residual, gain_third[...]), mlp_up[...]), approximate=True)
        out[here] = (residual + mm(hidden.astype(jnp.bfloat16), mlp_down[...])).astype(out.dtype)


VMEM = pl.BlockSpec(memory_space=pltpu.VMEM)
SMEM = pl.BlockSpec(memory_space=pltpu.SMEM)


def call(kernel, specs, shapes, args, scratch=(), flops=0, bytes_accessed=0):
    return pl.pallas_call(
        kernel,
        in_specs=specs,
        out_specs=[VMEM] * len(shapes),
        out_shape=[jax.ShapeDtypeStruct(shape, dtype) for shape, dtype in shapes],
        scratch_shapes=list(scratch),
        compiler_params=pltpu.CompilerParams(vmem_limit_bytes=VMEM_LIMIT),
        cost_estimate=pl.CostEstimate(
            flops=flops, bytes_accessed=bytes_accessed, transcendentals=0
        ),
    )(*args)


def local(
    volume,
    gain_first,
    phase_qkv,
    phase_out,
    bin_phase,
    phase_bias,
    gain_second,
    window_qkv,
    window_out,
    window_corner,
    window_bias,
    gain_third,
    mlp_up,
    mlp_down,
):
    planes, extent_x, extent_y, width = volume.shape[1:]
    plane = extent_x * extent_y
    tokens = planes * plane
    heads = window_corner.shape[0]
    bins = lax.axis_size("phase")
    half = bins // 2
    chunk = tokens // bins
    tile = ROWS * bins
    me = lax.axis_index("phase")
    bf16, f32 = jnp.bfloat16, jnp.float32

    def swap(block, mask):
        return lax.ppermute(block, "phase", [(i, i ^ mask) for i in range(bins)])

    own = volume.reshape(tokens, width)
    twin = swap(own, 1)

    def piece(mask):
        start = (me ^ mask) * chunk
        return jnp.stack(
            [lax.dynamic_slice_in_dim(source, start, chunk, axis=0) for source in (own, twin)]
        )

    blocks = [piece(0)] + [swap(piece(2 * step), 2 * step) for step in range(1, half)]

    phase_qv, window_qv, phase_table, window_table = call(
        functools.partial(prep_kernel, bins, extent_x, extent_y),
        [SMEM, SMEM, SMEM, VMEM, VMEM, VMEM],
        [
            ((2 * width, width), bf16),
            ((2 * width, width), bf16),
            ((heads // 2, tile, 2 * tile), f32),
            ((heads // 2, SPAN * plane, 2 * plane), f32),
        ],
        [bin_phase, window_corner, window_bias, phase_bias, phase_qkv, window_qkv],
        flops=2 * 10**9,
        bytes_accessed=4 * 2**20,
    )
    results = call(
        functools.partial(phase_kernel, bins, heads),
        [VMEM] * (half + 5),
        [((2, chunk, width), bf16)] * half,
        [*blocks, gain_first.reshape(1, width), phase_qkv, phase_qv, phase_table, phase_out],
        flops=2 * tokens * width * 5 * width,
        bytes_accessed=2**20,
    )
    got = [results[0]] + [swap(results[step], 2 * step) for step in range(1, half)]
    mine = jnp.stack([block[0] for block in got])
    theirs = swap(jnp.stack([block[1] for block in got]), 1)
    slots = jnp.stack([mine, theirs], axis=1).reshape(bins, chunk, width)
    residual = jnp.concatenate(
        [lax.dynamic_index_in_dim(slots, me ^ slot, 0, keepdims=True) for slot in range(bins)]
    ).reshape(planes, plane, width)

    count = lax.axis_size("space")
    place = lax.axis_index("space")
    first = 1 - place % 2
    even = [(i, i ^ 1) for i in range(count) if i ^ 1 < count]
    odd = [(i, ((i + 1) ^ 1) - 1) for i in range(count) if 0 <= ((i + 1) ^ 1) - 1 < count]
    inner = lax.ppermute(
        lax.dynamic_slice_in_dim(residual, first * (planes - REACH), REACH, axis=0), "space", even
    )
    outer = lax.ppermute(
        lax.dynamic_slice_in_dim(residual, (1 - first) * (planes - REACH), REACH, axis=0),
        "space",
        odd,
    )
    is_even = place % 2 == 0
    low = jnp.where(is_even, outer, inner)
    high = jnp.where(is_even, inner, outer)
    reach = REACH * plane
    ext = tokens + 2 * reach
    (out,) = call(
        functools.partial(window_kernel, plane),
        [SMEM] + [VMEM] * 11,
        [((tokens, width), bf16)],
        [
            window_corner,
            residual.reshape(tokens, width),
            low.reshape(reach, width),
            high.reshape(reach, width),
            gain_second.reshape(1, width),
            window_qkv,
            window_qv,
            window_table,
            window_out,
            gain_third.reshape(1, width),
            mlp_up,
            mlp_down,
        ],
        scratch=[pltpu.VMEM((ext, width), bf16), pltpu.VMEM((width, ext), bf16)],
        flops=2 * tokens * width * 14 * width,
        bytes_accessed=2**22,
    )
    return out.reshape(volume.shape)


def solution(mesh):
    split = P("phase", "space", None, None, None)
    in_specs = (split,) + (P(),) * 13
    return jax.shard_map(local, mesh=mesh, in_specs=in_specs, out_specs=split, check_vma=False)
```

```python
import functools
import math

import jax
import jax.numpy as jnp
from jax import lax
from jax.experimental import pallas as pl
from jax.experimental.pallas import tpu as pltpu
from jax.sharding import PartitionSpec as P

EPSILON = 1e-06
LOG2E = math.log2(math.e)
NEG = -1e30
SPAN = 4
REACH = SPAN - 1
ROWS = 16
MIB = 2**20

NT = (((1,), (1,)), ((), ()))
TN = (((0,), (0,)), ((), ()))


def mm(a, b, dims=(((1,), (0,)), ((), ()))):
    return lax.dot_general(a, b, dims, preferred_element_type=jnp.float32)


def rms(values, gain):
    mean_sq = jnp.mean(values * values, axis=-1, keepdims=True)
    return (values * lax.rsqrt(mean_sq + EPSILON) * gain).astype(jnp.bfloat16)


def prep_kernel(
    bins,
    extent_x,
    extent_y,
    bin_phase_at,
    corner_at,
    window_bias_at,
    phase_bias_at,
    phase_qkv_at,
    _,
    phase_weights,
    phase_table,
    window_table,
    bin_phase,
    corner,
    window_bias,
    phase_bias,
    phase_qkv,
    sems,
):
    copies = [
        pltpu.make_async_copy(source, target, sems.at[index])
        for index, (source, target) in enumerate(
            (
                (bin_phase_at, bin_phase),
                (corner_at, corner),
                (window_bias_at, window_bias),
                (phase_bias_at, phase_bias),
                (phase_qkv_at, phase_qkv),
            )
        )
    ]
    for copy in copies:
        copy.start()
    for copy in copies:
        copy.wait()
    width = phase_qkv.shape[0]
    heads = phase_bias.shape[0]
    phase_weights[:width] = phase_qkv[:, :width].T
    phase_weights[width : 2 * width] = phase_qkv[:, 2 * width :].T
    phase_weights[2 * width :] = phase_qkv[:, width : 2 * width]
    me = lax.axis_index("phase")
    tile = ROWS * bins
    slot = lax.broadcasted_iota(jnp.int32, (heads, tile), 1) // ROWS
    query_phase = jnp.zeros((heads, tile), jnp.int32)
    for member in range(bins):
        query_phase = jnp.where(slot == member, bin_phase[me ^ member], query_phase)
    same = (
        lax.broadcasted_iota(jnp.int32, (ROWS, tile), 0)
        == lax.broadcasted_iota(jnp.int32, (ROWS, tile), 1) % ROWS
    )
    bias = phase_bias[...] * LOG2E
    for member in range(bins):
        gap = bin_phase[me ^ member] - query_phase
        gap = jnp.where(gap < 0, gap + bins, gap)
        value = jnp.zeros((heads, tile), jnp.float32)
        for step in range(bins):
            value = jnp.where(gap == step, bias[:, step : step + 1], value)
        for head in range(heads):
            phase_table[
                head // 2,
                member * ROWS : (member + 1) * ROWS,
                (head % 2) * tile : (head % 2 + 1) * tile,
            ] = jnp.where(same, value[head : head + 1], NEG)
    plane = extent_x * extent_y
    shape = (extent_y, plane)
    lane = lax.broadcasted_iota(jnp.int32, shape, 1)
    lane_x = lane // extent_y
    delta_y = lax.broadcasted_iota(jnp.int32, shape, 0) - lane % extent_y
    for head in range(heads):
        first_x = corner[1, head]
        first_y = corner[2, head]
        y_masks = [delta_y == first_y + step for step in range(SPAN)]
        for step_z in range(SPAN):
            strips = []
            for step_x in range(SPAN):
                strip = jnp.full(shape, NEG, jnp.float32)
                for step_y in range(SPAN):
                    entry = window_bias[head, (step_z * SPAN + step_x) * SPAN + step_y] * LOG2E
                    strip = jnp.where(y_masks[step_y], entry, strip)
                strips.append(strip)
            for key_x in range(extent_x):
                block = jnp.full(shape, NEG, jnp.float32)
                for step_x in range(SPAN):
                    block = jnp.where(
                        lane_x == key_x - first_x - step_x, strips[step_x], block
                    )
                start = step_z * plane + key_x * extent_y
                window_table[
                    head // 2,
                    start : start + extent_y,
                    (head % 2) * plane : (head % 2 + 1) * plane,
                ] = block


def score(keys, queries, table):
    scores = mm(keys, queries) + table
    return scores, jnp.max(scores, axis=0, keepdims=True)


def soften(scores, top):
    return jnp.exp2(scores - top).astype(jnp.bfloat16)


def blend(values, weights, head_dim):
    count = weights.shape[1] // 2
    mixed = mm(values, weights)
    inverse = 1.0 / mixed[2 * head_dim : 2 * head_dim + 1]
    return jnp.concatenate(
        [
            mixed[:head_dim, :count] * inverse[:, :count],
            mixed[head_dim : 2 * head_dim, count:] * inverse[:, count:],
        ],
        axis=0,
    ).astype(jnp.bfloat16)


def run_pipeline(units, first, second, third, after):
    held = first(units[0])
    weights = None
    for index, unit in enumerate(units):
        following = first(units[index + 1]) if index + 1 < len(units) else None
        now = second(held)
        if index:
            third(units[index - 1], weights)
            after(index - 1)
        weights = now
        held = following
    third(units[-1], weights)
    after(len(units) - 1)


def block_diagonal(queries, base, head_dim, group, extra=None):
    count = queries.shape[1]
    first = base % group
    left = queries[base : base + head_dim]
    right = queries[base + head_dim : base + 2 * head_dim]
    zero = jnp.zeros((head_dim, count), queries.dtype)
    body = jnp.concatenate(
        [jnp.concatenate([left, zero], axis=1), jnp.concatenate([zero, right], axis=1)], axis=0
    )
    spare = group - 2 * head_dim
    if extra is None:
        pad = jnp.zeros((spare, 2 * count), queries.dtype)
    else:
        pad = jnp.concatenate(
            [extra, jnp.zeros((spare - ROWS, 2 * count), queries.dtype)], axis=0
        )
    return jnp.concatenate([body, pad] if first == 0 else [pad, body], axis=0)


def phase_kernel(bins, heads, *refs):
    blocks = refs[: bins // 2]
    gain, weights_in, table, out_weight = refs[bins // 2 : bins // 2 + 4]
    outs = refs[bins // 2 + 4 :]
    chunk, width = blocks[0].shape[1:]
    head_dim = width // heads
    scale = LOG2E / math.sqrt(head_dim)
    tile = ROWS * bins
    tiles = chunk // ROWS
    pairs = heads // 2
    group = 128
    stream = jnp.concatenate(
        [
            blocks[slot // 2][slot % 2, step * ROWS : (step + 1) * ROWS]
            for step in range(tiles)
            for slot in range(bins)
        ],
        axis=0,
    ).astype(jnp.float32)
    normed = rms(stream, gain[...])
    keys = mm(normed, weights_in[2 * width :]).astype(jnp.bfloat16)
    both = mm(weights_in[: 2 * width], normed, NT)
    queries = (both[:width] * scale).astype(jnp.bfloat16)
    values = both[width:].astype(jnp.bfloat16)
    ones = jnp.ones((ROWS, tile), jnp.bfloat16)
    units = [(step, pair) for step in range(tiles) for pair in range(pairs)]
    parts = []

    def first(unit):
        step, pair = unit
        span = slice(step * tile, (step + 1) * tile)
        base = pair * 2 * head_dim
        frame = base // group * group
        return score(
            keys[span, frame : frame + group],
            block_diagonal(queries[:, span], base, head_dim, group),
            table[pair],
        )

    def third(unit, weights):
        step, pair = unit
        span = slice(step * tile, (step + 1) * tile)
        base = pair * 2 * head_dim
        stack = jnp.concatenate([values[base : base + 2 * head_dim, span], ones], axis=0)
        parts.append(blend(stack, weights, head_dim))

    def after(index):
        if index % pairs != pairs - 1:
            return
        step = index // pairs
        mixed = jnp.concatenate(parts[step * pairs :], axis=0)
        span = slice(step * tile, (step + 1) * tile)
        result = (stream[span] + mm(mixed, out_weight[...], TN)).astype(jnp.bfloat16)
        for slot in range(bins):
            outs[slot // 2][slot % 2, step * ROWS : (step + 1) * ROWS] = result[
                slot * ROWS : (slot + 1) * ROWS
            ]

    run_pipeline(units, first, lambda held: soften(*held), third, after)


def gather_kernel(plane, half, *refs):
    got, twins = refs[:half], refs[half : 2 * half]
    residual, inner, outer = refs[2 * half :]
    me = lax.axis_index("phase")
    chunk = got[0].shape[1]
    for step in range(half):
        for part, source in enumerate((got[step], twins[step])):
            start = pl.multiple_of((me ^ (2 * step + part)) * chunk, ROWS)
            residual[pl.ds(start, chunk)] = source[part]
    reach = inner.shape[0]
    extra = residual.shape[0] - reach
    odd = lax.axis_index("space") % 2
    inner[...] = residual[pl.ds(pl.multiple_of((1 - odd) * extra, plane), reach)]
    outer[...] = residual[pl.ds(pl.multiple_of(odd * extra, plane), reach)]


def window_kernel(
    plane,
    corner,
    own,
    inner,
    outer,
    gain_second,
    qkv,
    table,
    out_weight,
    gain_third,
    mlp_up,
    mlp_down,
    out,
    key_store,
    value_store,
    pair_store,
):
    tokens, width = own.shape
    planes = tokens // plane
    heads = corner.shape[1]
    pairs = heads // 2
    head_dim = width // heads
    scale = LOG2E / math.sqrt(head_dim)
    reach = REACH * plane
    group = 128
    gain = gain_second[...]
    place = lax.axis_index("space")
    is_even = place % 2 == 0
    stream = own[...].astype(jnp.float32)
    own_normed = rms(stream, gain)
    key_weight = qkv[:, width : 2 * width]
    value_weight = qkv[:, 2 * width :].T
    query_weight = qkv[:, :width].T

    def project(normed, start, count):
        key_store[pl.ds(start, count)] = mm(normed, key_weight).astype(jnp.bfloat16)
        value_store[:, pl.ds(start, count)] = mm(value_weight, normed, NT).astype(jnp.bfloat16)

    project(own_normed, reach, tokens)
    queries = (mm(query_weight, own_normed, NT) * scale).astype(jnp.bfloat16)
    for source, at_end in ((inner, is_even), (outer, jnp.logical_not(is_even))):
        start = pl.multiple_of(jnp.where(at_end, reach + tokens, 0), plane)
        project(rms(source[...].astype(jnp.float32), gain), start, reach)
    z_first = place * planes
    depth = lax.axis_size("space") * planes
    span = (planes + REACH) * plane
    reach_keys = SPAN * plane
    lane = lax.broadcasted_iota(jnp.int32, (1, group), 1)
    ones = jnp.ones((ROWS, span), jnp.bfloat16)
    row = lax.broadcasted_iota(jnp.int32, (ROWS, 2 * plane), 0)
    lane_head = lax.broadcasted_iota(jnp.int32, (ROWS, 2 * plane), 1) // plane
    block_out = jnp.where(row == lane_head, NEG, 0.0).astype(jnp.bfloat16)
    pair_values = []
    for pair in range(pairs):
        base = pair * 2 * head_dim
        frame = base // group * group
        spare = 2 * head_dim if base == frame else 0
        first_z = [corner[0, 2 * pair + member] for member in range(2)]
        start = [pl.multiple_of((z + REACH) * plane, plane) for z in first_z]
        keep = [
            (
                (lane >= base + member * head_dim - frame)
                & (lane < base + (member + 1) * head_dim - frame)
            ).astype(jnp.bfloat16)
            for member in range(2)
        ]
        for at in range(planes + REACH):
            flags = jnp.zeros((1, group), jnp.float32)
            for member in range(2):
                z = z_first + at + first_z[member]
                flag = jnp.where((z >= 0) & (z < depth), 0.0, 1.0)
                flags = jnp.where(lane == spare + member, flag, flags)
            rows = [pl.ds(pl.multiple_of(start[m] + at * plane, plane), plane) for m in range(2)]
            pair_store[pair, at * plane : (at + 1) * plane] = (
                key_store[rows[0], frame : frame + group] * keep[0]
                + key_store[rows[1], frame : frame + group] * keep[1]
                + flags.astype(jnp.bfloat16)
            )
        pair_values.append(
            jnp.concatenate(
                [
                    value_store[
                        base + member * head_dim : base + (member + 1) * head_dim,
                        pl.ds(start[member], span),
                    ]
                    for member in range(2)
                ]
                + [ones],
                axis=0,
            )
        )
    units = [(at, pair) for at in range(planes) for pair in range(pairs)]
    parts = []
    residuals = {}
    hiddens = {}

    def first(unit):
        at, pair = unit
        here = slice(at * plane, (at + 1) * plane)
        return score(
            pair_store[pair, at * plane : at * plane + reach_keys],
            block_diagonal(queries[:, here], pair * 2 * head_dim, head_dim, group, block_out),
            table[pair],
        )

    def third(unit, weights):
        at, pair = unit
        values = pair_values[pair][:, at * plane : at * plane + reach_keys]
        parts.append(blend(values, weights, head_dim))

    def mix(at):
        mixed = jnp.concatenate(parts[at * pairs : (at + 1) * pairs], axis=0)
        here = slice(at * plane, (at + 1) * plane)
        residuals[at] = stream[here] + mm(mixed, out_weight[...], TN)

    def expand(at):
        hidden = mm(rms(residuals[at], gain_third[...]), mlp_up[...])
        hiddens[at] = jax.nn.gelu(hidden, approximate=True).astype(jnp.bfloat16)

    def finish(at):
        here = slice(at * plane, (at + 1) * plane)
        out[here] = (residuals[at] + mm(hiddens[at], mlp_down[...])).astype(out.dtype)

    def after(index):
        at, stage = index // pairs, index % pairs
        if stage == pairs - 1:
            mix(at)
        if at and stage == 0:
            expand(at - 1)
        if at and stage == 1:
            finish(at - 1)

    run_pipeline(units, first, lambda held: soften(*held), third, after)
    expand(planes - 1)
    finish(planes - 1)


VMEM = pl.BlockSpec(memory_space=pltpu.VMEM)
SMEM = pl.BlockSpec(memory_space=pltpu.SMEM)
ANY = pl.BlockSpec(memory_space=pl.ANY)
HBM = pl.BlockSpec(memory_space=pltpu.HBM)


def call(kernel, specs, shapes, args, limit, scratch=(), flops=0, bytes_accessed=0):
    return pl.pallas_call(
        kernel,
        in_specs=specs,
        out_specs=[VMEM] * len(shapes),
        out_shape=[jax.ShapeDtypeStruct(shape, dtype) for shape, dtype in shapes],
        scratch_shapes=list(scratch),
        compiler_params=pltpu.CompilerParams(vmem_limit_bytes=limit * MIB),
        cost_estimate=pl.CostEstimate(
            flops=flops, bytes_accessed=bytes_accessed, transcendentals=0
        ),
    )(*args)


def local(
    volume,
    gain_first,
    phase_qkv,
    phase_out,
    bin_phase,
    phase_bias,
    gain_second,
    window_qkv,
    window_out,
    window_corner,
    window_bias,
    gain_third,
    mlp_up,
    mlp_down,
):
    planes, extent_x, extent_y, width = volume.shape[1:]
    plane = extent_x * extent_y
    tokens = planes * plane
    heads = window_corner.shape[0]
    bins = lax.axis_size("phase")
    half = bins // 2
    chunk = tokens // bins
    tile = ROWS * bins
    me = lax.axis_index("phase")
    bf16, f32 = jnp.bfloat16, jnp.float32

    def swap(block, mask):
        return lax.ppermute(block, "phase", [(i, i ^ mask) for i in range(bins)])

    own = volume.reshape(tokens, width)
    twin = swap(own, 1)

    def piece(mask):
        start = (me ^ mask) * chunk
        return jnp.stack(
            [lax.dynamic_slice_in_dim(source, start, chunk, axis=0) for source in (own, twin)]
        )

    pieces = [piece(2 * step) for step in range(half)]
    blocks = pieces[:1] + [swap(pieces[step], 2 * step) for step in range(1, half)]
    corner = window_corner.T

    phase_weights, phase_table, window_table = call(
        functools.partial(prep_kernel, bins, extent_x, extent_y),
        [HBM] * 5 + [ANY],
        [
            ((3 * width, width), bf16),
            ((heads // 2, tile, 2 * tile), f32),
            ((heads // 2, SPAN * plane, 2 * plane), f32),
        ],
        [
            *(
                pltpu.with_memory_space_constraint(array, pltpu.HBM)
                for array in (bin_phase, corner, window_bias, phase_bias, phase_qkv)
            ),
            pieces[-1],
        ],
        12,
        scratch=[
            pltpu.SMEM(bin_phase.shape, jnp.int32),
            pltpu.SMEM(corner.shape, jnp.int32),
            pltpu.SMEM(window_bias.shape, f32),
            pltpu.VMEM(phase_bias.shape, f32),
            pltpu.VMEM(phase_qkv.shape, bf16),
            pltpu.SemaphoreType.DMA((5,)),
        ],
        flops=2 * 10**9,
        bytes_accessed=4 * 2**20,
    )
    results = call(
        functools.partial(phase_kernel, bins, heads),
        [VMEM] * (half + 4),
        [((2, chunk, width), bf16)] * half,
        [*blocks, gain_first.reshape(1, width), phase_weights, phase_table, phase_out],
        12,
        flops=2 * tokens * width * 5 * width,
        bytes_accessed=2**20,
    )
    got = [results[0]] + [swap(results[step], 2 * step) for step in range(1, half)]
    twins = [swap(block, 1) for block in got]
    reach = REACH * plane
    ext = tokens + 2 * reach
    residual, inner, outer = call(
        functools.partial(gather_kernel, plane, half),
        [VMEM] * (2 * half),
        [((tokens, width), bf16), ((reach, width), bf16), ((reach, width), bf16)],
        [*got, *twins],
        4,
    )
    count = lax.axis_size("space")
    even = [(i, i ^ 1) for i in range(count) if i ^ 1 < count]
    odd = [(i, ((i + 1) ^ 1) - 1) for i in range(count) if 0 <= ((i + 1) ^ 1) - 1 < count]
    inner = lax.ppermute(inner, "space", even)
    outer = lax.ppermute(outer, "space", odd)
    (out,) = call(
        functools.partial(window_kernel, plane),
        [SMEM] + [VMEM] * 10,
        [((tokens, width), bf16)],
        [
            corner,
            residual,
            inner,
            outer,
            gain_second.reshape(1, width),
            window_qkv,
            window_table,
            window_out,
            gain_third.reshape(1, width),
            mlp_up,
            mlp_down,
        ],
        24,
        scratch=[
            pltpu.VMEM((ext, width), bf16),
            pltpu.VMEM((width, ext), bf16),
            pltpu.VMEM((heads // 2, (planes + REACH) * plane, 128), bf16),
        ],
        flops=2 * tokens * width * 14 * width,
        bytes_accessed=2**22,
    )
    return out.reshape(volume.shape)


def solution(mesh):
    split = P("phase", "space", None, None, None)
    in_specs = (split,) + (P(),) * 13
    return jax.shard_map(local, mesh=mesh, in_specs=in_specs, out_specs=split, check_vma=False)
```

```python
import functools
import math

import jax
import jax.numpy as jnp
from jax import lax
from jax.experimental import pallas as pl
from jax.experimental.pallas import tpu as pltpu
from jax.sharding import PartitionSpec as P

EPSILON = 1e-06
LOG2E = math.log2(math.e)
NEG = -1e30
SPAN = 4
REACH = SPAN - 1
ROWS = 16
MIB = 2**20
GELU_LINEAR = math.sqrt(2.0 / math.pi)
GELU_CUBIC = 0.044715 * GELU_LINEAR

NT = (((1,), (1,)), ((), ()))
TN = (((0,), (0,)), ((), ()))


def mm(a, b, dims=(((1,), (0,)), ((), ()))):
    return lax.dot_general(a, b, dims, preferred_element_type=jnp.float32)


def rms(values, gain):
    mean_sq = jnp.mean(values * values, axis=-1, keepdims=True)
    return (values * lax.rsqrt(mean_sq + EPSILON) * gain).astype(jnp.bfloat16)


def prep_kernel(
    bins,
    extent_x,
    extent_y,
    bin_phase_at,
    corner_at,
    window_bias_at,
    phase_bias_at,
    phase_qkv_at,
    _,
    phase_weights,
    phase_table,
    window_table,
    bin_phase,
    corner,
    window_bias,
    phase_bias,
    phase_qkv,
    sems,
):
    copies = [
        pltpu.make_async_copy(source, target, sems.at[index])
        for index, (source, target) in enumerate(
            (
                (bin_phase_at, bin_phase),
                (corner_at, corner),
                (window_bias_at, window_bias),
                (phase_bias_at, phase_bias),
                (phase_qkv_at, phase_qkv),
            )
        )
    ]
    for copy in copies:
        copy.start()
    for copy in copies:
        copy.wait()
    width = phase_qkv.shape[0]
    heads = phase_bias.shape[0]
    phase_weights[:width] = phase_qkv[:, :width].T
    phase_weights[width : 2 * width] = phase_qkv[:, 2 * width :].T
    phase_weights[2 * width :] = phase_qkv[:, width : 2 * width]
    me = lax.axis_index("phase")
    tile = ROWS * bins
    slot = lax.broadcasted_iota(jnp.int32, (heads, tile), 1) // ROWS
    query_phase = jnp.zeros((heads, tile), jnp.int32)
    for member in range(bins):
        query_phase = jnp.where(slot == member, bin_phase[me ^ member], query_phase)
    same = (
        lax.broadcasted_iota(jnp.int32, (ROWS, tile), 0)
        == lax.broadcasted_iota(jnp.int32, (ROWS, tile), 1) % ROWS
    )
    bias = phase_bias[...] * LOG2E
    for member in range(bins):
        gap = bin_phase[me ^ member] - query_phase
        gap = jnp.where(gap < 0, gap + bins, gap)
        value = jnp.zeros((heads, tile), jnp.float32)
        for step in range(bins):
            value = jnp.where(gap == step, bias[:, step : step + 1], value)
        for head in range(heads):
            phase_table[
                head // 2,
                member * ROWS : (member + 1) * ROWS,
                (head % 2) * tile : (head % 2 + 1) * tile,
            ] = jnp.where(same, value[head : head + 1], NEG)
    plane = extent_x * extent_y
    window_table[:, SPAN * plane :] = jnp.full(
        (heads // 2, plane, 2 * plane), NEG, window_table.dtype
    )
    shape = (extent_y, plane)
    lane = lax.broadcasted_iota(jnp.int32, shape, 1)
    lane_x = lane // extent_y
    delta_y = lax.broadcasted_iota(jnp.int32, shape, 0) - lane % extent_y
    for head in range(heads):
        first_x = corner[1, head]
        first_y = corner[2, head]
        y_masks = [delta_y == first_y + step for step in range(SPAN)]
        for step_z in range(SPAN):
            strips = []
            for step_x in range(SPAN):
                strip = jnp.full(shape, NEG, jnp.float32)
                for step_y in range(SPAN):
                    entry = window_bias[head, (step_z * SPAN + step_x) * SPAN + step_y] * LOG2E
                    strip = jnp.where(y_masks[step_y], entry, strip)
                strips.append(strip)
            for key_x in range(extent_x):
                block = jnp.full(shape, NEG, jnp.float32)
                for step_x in range(SPAN):
                    block = jnp.where(
                        lane_x == key_x - first_x - step_x, strips[step_x], block
                    )
                start = step_z * plane + key_x * extent_y
                window_table[
                    head // 2,
                    start : start + extent_y,
                    (head % 2) * plane : (head % 2 + 1) * plane,
                ] = block


def score_steps(keys, queries, tiles, store):
    pieces = []
    tops = []
    for start, stop, table in tiles:
        piece = mm(keys[start:stop], queries) + table
        pieces.append(piece)
        tops.append(jnp.max(piece.reshape(-1, 8, piece.shape[1]), axis=0))
        yield
    top = functools.reduce(jnp.maximum, tops)
    store["pieces"] = pieces
    store["top"] = jnp.max(top, axis=0, keepdims=True)


def soften_steps(store):
    weights = []
    for piece in store.pop("pieces"):
        weights.append(jnp.exp2((piece - store["top"]).astype(jnp.bfloat16)))
        yield
    store["weights"] = jnp.concatenate(weights, axis=0) if len(weights) > 1 else weights[0]


def blend(mixed, head_dim):
    count = mixed.shape[1] // 2
    inverse = 1.0 / mixed[2 * head_dim : 2 * head_dim + 1]
    return jnp.concatenate(
        [
            mixed[:head_dim, :count] * inverse[:, :count],
            mixed[head_dim : 2 * head_dim, count:] * inverse[:, count:],
        ],
        axis=0,
    ).astype(jnp.bfloat16)


def interleave(*steps):
    running = list(steps)
    while running:
        for step in list(running):
            try:
                next(step)
            except StopIteration:
                running.remove(step)


def run_pipeline(units, size, first, second, third, side):
    groups = [units[start : start + size] for start in range(0, len(units), size)]
    stores = {unit: {} for unit in units}

    def steps(action, index):
        if not 0 <= index < len(groups):
            return []
        return [action(unit, stores[unit]) for unit in groups[index]]

    interleave(*steps(first, 0))
    for index in range(len(groups)):
        interleave(
            *steps(first, index + 1),
            *steps(second, index),
            *steps(third, index - 1),
            side(index),
        )
    interleave(*steps(third, len(groups) - 1))


def block_diagonal(queries, base, head_dim, group):
    count = queries.shape[1]
    first = base % group
    left = queries[base : base + head_dim]
    right = queries[base + head_dim : base + 2 * head_dim]
    zero = jnp.zeros((head_dim, count), queries.dtype)
    body = jnp.concatenate(
        [jnp.concatenate([left, zero], axis=1), jnp.concatenate([zero, right], axis=1)], axis=0
    )
    pad = jnp.zeros((group - 2 * head_dim, 2 * count), queries.dtype)
    return jnp.concatenate([body, pad] if first == 0 else [pad, body], axis=0)


def phase_kernel(bins, heads, *refs):
    blocks = refs[: bins // 2]
    gain, weights_in, table, out_weight = refs[bins // 2 : bins // 2 + 4]
    outs = refs[bins // 2 + 4 :]
    chunk, width = blocks[0].shape[1:]
    head_dim = width // heads
    scale = LOG2E / math.sqrt(head_dim)
    tile = ROWS * bins
    tiles = chunk // ROWS
    pairs = heads // 2
    group = 128
    stream = jnp.concatenate(
        [
            blocks[slot // 2][slot % 2, step * ROWS : (step + 1) * ROWS]
            for step in range(tiles)
            for slot in range(bins)
        ],
        axis=0,
    ).astype(jnp.float32)
    normed = rms(stream, gain[...])
    keys = mm(normed, weights_in[2 * width :]).astype(jnp.bfloat16)
    both = mm(weights_in[: 2 * width], normed, NT)
    queries = (both[:width] * scale).astype(jnp.bfloat16)
    values = both[width:].astype(jnp.bfloat16)
    ones = jnp.ones((ROWS, tile), jnp.bfloat16)
    units = [(step, pair) for step in range(tiles) for pair in range(pairs)]
    parts = []

    def first(unit, store):
        step, pair = unit
        span = slice(step * tile, (step + 1) * tile)
        base = pair * 2 * head_dim
        frame = base // group * group
        return score_steps(
            keys[span, frame : frame + group],
            block_diagonal(queries[:, span], base, head_dim, group),
            [(0, tile, table[pair])],
            store,
        )

    def third(unit, store):
        step, pair = unit
        span = slice(step * tile, (step + 1) * tile)
        base = pair * 2 * head_dim
        stack = jnp.concatenate([values[base : base + 2 * head_dim, span], ones], axis=0)
        parts.append(blend(mm(stack, store.pop("weights")), head_dim))
        yield

    def finish(step):
        mixed = jnp.concatenate(parts[step * pairs : (step + 1) * pairs], axis=0)
        span = slice(step * tile, (step + 1) * tile)
        result = (stream[span] + mm(mixed, out_weight[...], TN)).astype(jnp.bfloat16)
        for slot in range(bins):
            outs[slot // 2][slot % 2, step * ROWS : (step + 1) * ROWS] = result[
                slot * ROWS : (slot + 1) * ROWS
            ]

    size = pairs

    def side(index):
        if index * size >= pairs and index * size % pairs == 0:
            yield
            finish(index * size // pairs - 1)

    run_pipeline(units, size, first, lambda _, store: soften_steps(store), third, side)
    finish(tiles - 1)


def pack_kernel(*refs):
    give = refs[-1]
    chunk = refs[0].shape[1]
    for step, source in enumerate(refs[:-1]):
        give[step * chunk : (step + 1) * chunk] = source[1]


def gather_kernel(plane, half, *refs):
    got = refs[:half]
    twin, residual, inner, outer = refs[half:]
    me = lax.axis_index("phase")
    chunk = got[0].shape[1]
    for step in range(half):
        start = pl.multiple_of((me ^ (2 * step)) * chunk, ROWS)
        residual[pl.ds(start, chunk)] = got[step][0]
        start = pl.multiple_of((me ^ (2 * step + 1)) * chunk, ROWS)
        residual[pl.ds(start, chunk)] = twin[step * chunk : (step + 1) * chunk]
    reach = inner.shape[0]
    extra = residual.shape[0] - reach
    odd = lax.axis_index("space") % 2
    inner[...] = residual[pl.ds(pl.multiple_of((1 - odd) * extra, plane), reach)]
    outer[...] = residual[pl.ds(pl.multiple_of(odd * extra, plane), reach)]


def frame_of(keys, pair, head_dim, group):
    frame = pair * 2 * head_dim // group * group
    return keys[:, frame : frame + group]


def table_tiles(table, corner, pair, at, members, plane, z_first, depth):
    tiles = []
    for index, member in enumerate(members):
        z = z_first + member - REACH
        halves = []
        for side in range(2):
            step = member - REACH - at - corner[0, 2 * pair + side]
            inside = (step >= 0) & (step < SPAN) & (z >= 0) & (z < depth)
            start = pl.multiple_of(jnp.where(inside, step, SPAN) * plane, plane)
            halves.append(table[pair, pl.ds(start, plane), side * plane : (side + 1) * plane])
        tiles.append((index * plane, (index + 1) * plane, jnp.concatenate(halves, axis=1)))
    return tiles


def inside_kernel(
    plane, corner, own, gain_second, qkv, table, queries_out, values_out,
    part_mixed, part_top, part_sum
):
    tokens, width = own.shape
    planes = tokens // plane
    heads = corner.shape[1]
    pairs = heads // 2
    head_dim = width // heads
    scale = LOG2E / math.sqrt(head_dim)
    group = 128
    members = list(range(REACH, REACH + planes))
    z_first = lax.axis_index("space") * planes
    depth = lax.axis_size("space") * planes
    normed = rms(own[...].astype(jnp.float32), gain_second[...])
    keys = mm(normed, qkv[:, width : 2 * width]).astype(jnp.bfloat16)
    value_weight = qkv[:, 2 * width :].T
    values_out[...] = value_weight
    values = mm(value_weight, normed, NT).astype(jnp.bfloat16)
    queries = (mm(qkv[:, :width].T, normed, NT) * scale).astype(jnp.bfloat16)
    queries_out[...] = queries
    ones = jnp.ones((ROWS, tokens), jnp.bfloat16)
    frames = [frame_of(keys, pair, head_dim, group) for pair in range(pairs)]
    stacks = [
        jnp.concatenate([values[pair * 2 * head_dim : (pair + 1) * 2 * head_dim], ones], axis=0)
        for pair in range(pairs)
    ]
    units = [(at, pair) for at in range(planes) for pair in range(pairs)]

    def first(unit, store):
        at, pair = unit
        return score_steps(
            frames[pair],
            block_diagonal(
                queries[:, at * plane : (at + 1) * plane],
                pair * 2 * head_dim,
                head_dim,
                group,
            ),
            table_tiles(table, corner, pair, at, members, plane, z_first, depth),
            store,
        )

    def third(unit, store):
        at, pair = unit
        mixed = mm(stacks[pair], store.pop("weights"))
        base = pair * 2 * head_dim
        part_mixed[at, base : base + head_dim] = mixed[:head_dim, :plane]
        part_mixed[at, base + head_dim : base + 2 * head_dim] = mixed[
            head_dim : 2 * head_dim, plane:
        ]
        part_top[at, pair : pair + 1] = store["top"]
        part_sum[at, pair : pair + 1] = mixed[2 * head_dim : 2 * head_dim + 1]
        yield

    run_pipeline(units, 2, first, lambda _, store: soften_steps(store), third, lambda _: iter(()))


def outside_kernel(
    plane,
    corner,
    own,
    inner,
    outer,
    gain_second,
    qkv,
    table,
    queries,
    value_weight,
    part_mixed,
    part_top,
    part_sum,
    out_weight,
    gain_third,
    mlp_up,
    mlp_down,
    out,
    key_store,
    value_store,
):
    tokens, width = own.shape
    planes = tokens // plane
    heads = corner.shape[1]
    pairs = heads // 2
    head_dim = width // heads
    reach = REACH * plane
    group = 128
    gain = gain_second[...]
    place = lax.axis_index("space")
    is_even = place % 2 == 0
    z_first = place * planes
    depth = lax.axis_size("space") * planes
    key_weight = qkv[:, width : 2 * width]
    for source, at_end in ((inner, is_even), (outer, jnp.logical_not(is_even))):
        normed = rms(source[...].astype(jnp.float32), gain)
        rows = pl.ds(pl.multiple_of(jnp.where(at_end, reach, 0), plane), reach)
        key_store[rows] = mm(normed, key_weight).astype(jnp.bfloat16)
        value_store[:, rows] = mm(value_weight[...], normed, NT).astype(jnp.bfloat16)
    rim = list(range(REACH)) + list(range(REACH + planes, 2 * REACH + planes))
    ones = jnp.ones((ROWS, 2 * reach), jnp.bfloat16)
    frames = [frame_of(key_store, pair, head_dim, group) for pair in range(pairs)]
    stacks = [
        jnp.concatenate([value_store[pair * 2 * head_dim : (pair + 1) * 2 * head_dim], ones], axis=0)
        for pair in range(pairs)
    ]
    units = [(at, pair) for at in range(planes) for pair in range(pairs)]

    def span(at):
        return min(at, REACH), REACH + max(0, at + SPAN - planes)

    def first(unit, store):
        at, pair = unit
        start, stop = span(at)
        return score_steps(
            frames[pair][start * plane : stop * plane],
            block_diagonal(
                queries[:, at * plane : (at + 1) * plane],
                pair * 2 * head_dim,
                head_dim,
                group,
            ),
            table_tiles(table, corner, pair, at, rim[start:stop], plane, z_first, depth),
            store,
        )

    def second(unit, store):
        at, pair = unit
        before = part_top[at, pair : pair + 1]
        store["top"] = jnp.maximum(store["top"], before)
        store["ratio"] = jnp.exp2(before - store["top"])
        return soften_steps(store)

    parts = []

    def third(unit, store):
        at, pair = unit
        start, stop = span(at)
        mixed = mm(stacks[pair][:, start * plane : stop * plane], store.pop("weights"))
        ratio = store["ratio"]
        total = mixed[2 * head_dim : 2 * head_dim + 1] + ratio * part_sum[at, pair : pair + 1]
        inverse = 1.0 / total
        ratio = ratio * inverse
        halves = []
        for side in range(2):
            rows = slice(side * head_dim, (side + 1) * head_dim)
            lanes = slice(side * plane, (side + 1) * plane)
            base = (pair * 2 + side) * head_dim
            halves.append(
                mixed[rows, lanes] * inverse[:, lanes]
                + part_mixed[at, base : base + head_dim] * ratio[:, lanes]
            )
        parts.append(jnp.concatenate(halves, axis=0).astype(jnp.bfloat16))
        yield

    run_pipeline(units, 2, first, second, third, lambda _: iter(()))
    mixed = [jnp.concatenate(parts[at * pairs : (at + 1) * pairs], axis=0) for at in range(planes)]
    columns = width
    block = 2 * plane

    def mlp_steps(start):
        here = slice(start * plane, start * plane + block)
        joined = jnp.concatenate(mixed[start : start + 2], axis=1) if 2 > 1 else mixed[start]
        residual = own[here].astype(jnp.float32) + mm(joined, out_weight[...], TN)
        normed = rms(residual, gain_third[...])
        yield
        hiddens = []
        for first_column in range(0, mlp_up.shape[1], columns):
            hidden = mm(normed, mlp_up[:, first_column : first_column + columns])
            hiddens.append(gelu(hidden.astype(jnp.bfloat16)))
            yield
        hidden = jnp.concatenate(hiddens, axis=1)
        out[here] = (residual + mm(hidden, mlp_down[...])).astype(out.dtype)

    interleave(*(mlp_steps(start) for start in range(0, planes, 2)))


def gelu(values):
    half = values * 0.5
    cubic = values * (GELU_LINEAR + GELU_CUBIC * (values * values))
    return half + half * jnp.tanh(cubic)


VMEM = pl.BlockSpec(memory_space=pltpu.VMEM)
SMEM = pl.BlockSpec(memory_space=pltpu.SMEM)
ANY = pl.BlockSpec(memory_space=pl.ANY)
HBM = pl.BlockSpec(memory_space=pltpu.HBM)


def call(kernel, specs, shapes, args, limit, scratch=(), flops=0, bytes_accessed=0):
    return pl.pallas_call(
        kernel,
        in_specs=specs,
        out_specs=[VMEM] * len(shapes),
        out_shape=[jax.ShapeDtypeStruct(shape, dtype) for shape, dtype in shapes],
        scratch_shapes=list(scratch),
        compiler_params=pltpu.CompilerParams(vmem_limit_bytes=limit * MIB),
        cost_estimate=pl.CostEstimate(
            flops=flops, bytes_accessed=bytes_accessed, transcendentals=0
        ),
    )(*args)


def local(
    volume,
    gain_first,
    phase_qkv,
    phase_out,
    bin_phase,
    phase_bias,
    gain_second,
    window_qkv,
    window_out,
    window_corner,
    window_bias,
    gain_third,
    mlp_up,
    mlp_down,
):
    planes, extent_x, extent_y, width = volume.shape[1:]
    plane = extent_x * extent_y
    tokens = planes * plane
    heads = window_corner.shape[0]
    bins = lax.axis_size("phase")
    half = bins // 2
    chunk = tokens // bins
    tile = ROWS * bins
    me = lax.axis_index("phase")
    bf16, f32 = jnp.bfloat16, jnp.float32

    def swap(block, mask):
        return lax.ppermute(block, "phase", [(i, i ^ mask) for i in range(bins)])

    own = volume.reshape(tokens, width)
    twin = swap(own, 1)

    def piece(mask):
        start = (me ^ mask) * chunk
        return jnp.stack(
            [lax.dynamic_slice_in_dim(source, start, chunk, axis=0) for source in (own, twin)]
        )

    pieces = [piece(2 * step) for step in range(half)]
    blocks = pieces[:1] + [swap(pieces[step], 2 * step) for step in range(1, half)]
    corner = window_corner.T

    phase_weights, phase_table, window_table = call(
        functools.partial(prep_kernel, bins, extent_x, extent_y),
        [HBM] * 5 + [ANY],
        [
            ((3 * width, width), bf16),
            ((heads // 2, tile, 2 * tile), f32),
            ((heads // 2, (SPAN + 1) * plane, 2 * plane), f32),
        ],
        [
            *(
                pltpu.with_memory_space_constraint(array, pltpu.HBM)
                for array in (bin_phase, corner, window_bias, phase_bias, phase_qkv)
            ),
            pieces[-1],
        ],
        12,
        scratch=[
            pltpu.SMEM(bin_phase.shape, jnp.int32),
            pltpu.SMEM(corner.shape, jnp.int32),
            pltpu.SMEM(window_bias.shape, f32),
            pltpu.VMEM(phase_bias.shape, f32),
            pltpu.VMEM(phase_qkv.shape, bf16),
            pltpu.SemaphoreType.DMA((5,)),
        ],
        flops=2 * 10**9,
        bytes_accessed=4 * 2**20,
    )
    results = call(
        functools.partial(phase_kernel, bins, heads),
        [VMEM] * (half + 4),
        [((2, chunk, width), bf16)] * half,
        [*blocks, gain_first.reshape(1, width), phase_weights, phase_table, phase_out],
        12,
        flops=2 * tokens * width * 5 * width,
        bytes_accessed=2**20,
    )
    got = [results[0]] + [swap(results[step], 2 * step) for step in range(1, half)]
    (give,) = call(
        pack_kernel, [VMEM] * half, [((half * chunk, width), bf16)], [*got], 4
    )
    twin = swap(give, 1)
    reach = REACH * plane
    residual, inner, outer = call(
        functools.partial(gather_kernel, plane, half),
        [VMEM] * (half + 1),
        [((tokens, width), bf16), ((reach, width), bf16), ((reach, width), bf16)],
        [*got, twin],
        4,
    )
    count = lax.axis_size("space")
    even = [(i, i ^ 1) for i in range(count) if i ^ 1 < count]
    odd = [(i, ((i + 1) ^ 1) - 1) for i in range(count) if 0 <= ((i + 1) ^ 1) - 1 < count]
    inner = lax.ppermute(inner, "space", even)
    outer = lax.ppermute(outer, "space", odd)
    gain = gain_second.reshape(1, width)
    pairs = heads // 2
    partial = call(
        functools.partial(inside_kernel, plane),
        [SMEM] + [VMEM] * 4,
        [
            ((width, tokens), bf16),
            ((width, width), bf16),
            ((planes, width, plane), f32),
            ((planes, pairs, 2 * plane), f32),
            ((planes, pairs, 2 * plane), f32),
        ],
        [corner, residual, gain, window_qkv, window_table],
        16,
        flops=2 * tokens * width * 14 * width,
        bytes_accessed=2**22,
    )
    (out,) = call(
        functools.partial(outside_kernel, plane),
        [SMEM] + [VMEM] * 15,
        [((tokens, width), bf16)],
        [
            corner,
            residual,
            inner,
            outer,
            gain,
            window_qkv,
            window_table,
            *partial,
            window_out,
            gain_third.reshape(1, width),
            mlp_up,
            mlp_down,
        ],
        20,
        scratch=[pltpu.VMEM((2 * reach, width), bf16), pltpu.VMEM((width, 2 * reach), bf16)],
        flops=2 * tokens * width * 14 * width,
        bytes_accessed=2**22,
    )
    return out.reshape(volume.shape)


def solution(mesh):
    split = P("phase", "space", None, None, None)
    in_specs = (split,) + (P(),) * 13
    return jax.shard_map(local, mesh=mesh, in_specs=in_specs, out_specs=split, check_vma=False)
```

```python
import functools
import math

import jax
import jax.numpy as jnp
from jax import lax
from jax.experimental import pallas as pl
from jax.experimental.pallas import tpu as pltpu
from jax.sharding import PartitionSpec as P

EPSILON = 1e-06
LOG2E = math.log2(math.e)
NEG = -1e30
SPAN = 4
REACH = SPAN - 1
ROWS = 16
MIB = 2**20
GELU_LINEAR = math.sqrt(2.0 / math.pi)
GELU_CUBIC = 0.044715 * GELU_LINEAR

NT = (((1,), (1,)), ((), ()))
TN = (((0,), (0,)), ((), ()))


def mm(a, b, dims=(((1,), (0,)), ((), ()))):
    return lax.dot_general(a, b, dims, preferred_element_type=jnp.float32)


def rms(values, gain):
    mean_sq = jnp.mean(values * values, axis=-1, keepdims=True)
    return (values * lax.rsqrt(mean_sq + EPSILON) * gain).astype(jnp.bfloat16)


def prep_kernel(
    masks,
    extent_x,
    extent_y,
    bin_phase_at,
    corner_at,
    window_bias_at,
    phase_bias_at,
    phase_qkv_at,
    _,
    phase_weights,
    phase_table,
    window_table,
    bin_phase,
    corner,
    window_bias,
    phase_bias,
    phase_qkv,
    sems,
):
    copies = [
        pltpu.make_async_copy(source, target, sems.at[index])
        for index, (source, target) in enumerate(
            (
                (bin_phase_at, bin_phase),
                (corner_at, corner),
                (window_bias_at, window_bias),
                (phase_bias_at, phase_bias),
                (phase_qkv_at, phase_qkv),
            )
        )
    ]
    for copy in copies:
        copy.start()
    for copy in copies:
        copy.wait()
    width = phase_qkv.shape[0]
    heads = phase_bias.shape[0]
    phase_weights[:width] = phase_qkv[:, :width].T
    phase_weights[width : 2 * width] = phase_qkv[:, 2 * width :].T
    phase_weights[2 * width :] = phase_qkv[:, width : 2 * width]
    me = lax.axis_index("phase")
    bins = len(masks)
    tile = ROWS * bins
    slot = lax.broadcasted_iota(jnp.int32, (heads, tile), 1) // ROWS
    query_phase = jnp.zeros((heads, tile), jnp.int32)
    for member, mask in enumerate(masks):
        query_phase = jnp.where(slot == member, bin_phase[me ^ mask], query_phase)
    same = (
        lax.broadcasted_iota(jnp.int32, (ROWS, tile), 0)
        == lax.broadcasted_iota(jnp.int32, (ROWS, tile), 1) % ROWS
    )
    bias = phase_bias[...] * LOG2E
    for member, mask in enumerate(masks):
        gap = bin_phase[me ^ mask] - query_phase
        gap = jnp.where(gap < 0, gap + bins, gap)
        value = jnp.zeros((heads, tile), jnp.float32)
        for step in range(bins):
            value = jnp.where(gap == step, bias[:, step : step + 1], value)
        for head in range(heads):
            phase_table[
                head // 2,
                member * ROWS : (member + 1) * ROWS,
                (head % 2) * tile : (head % 2 + 1) * tile,
            ] = jnp.where(same, value[head : head + 1], NEG)
    plane = extent_x * extent_y
    window_table[:, SPAN * plane :] = jnp.full(
        (heads // 2, plane, 2 * plane), NEG, window_table.dtype
    )
    shape = (extent_y, plane)
    lane = lax.broadcasted_iota(jnp.int32, shape, 1)
    lane_x = lane // extent_y
    delta_y = lax.broadcasted_iota(jnp.int32, shape, 0) - lane % extent_y
    for head in range(heads):
        first_x = corner[1, head]
        first_y = corner[2, head]
        y_masks = [delta_y == first_y + step for step in range(SPAN)]
        for step_z in range(SPAN):
            strips = []
            for step_x in range(SPAN):
                strip = jnp.full(shape, NEG, jnp.float32)
                for step_y in range(SPAN):
                    entry = window_bias[head, (step_z * SPAN + step_x) * SPAN + step_y] * LOG2E
                    strip = jnp.where(y_masks[step_y], entry, strip)
                strips.append(strip)
            for key_x in range(extent_x):
                block = jnp.full(shape, NEG, jnp.float32)
                for step_x in range(SPAN):
                    block = jnp.where(
                        lane_x == key_x - first_x - step_x, strips[step_x], block
                    )
                start = step_z * plane + key_x * extent_y
                window_table[
                    head // 2,
                    start : start + extent_y,
                    (head % 2) * plane : (head % 2 + 1) * plane,
                ] = block


def score_steps(keys, queries, tiles, store):
    pieces = []
    tops = []
    for start, stop, table in tiles:
        piece = mm(keys[start:stop], queries) + table
        pieces.append(piece)
        tops.append(jnp.max(piece.reshape(-1, 8, piece.shape[1]), axis=0))
        yield
    top = functools.reduce(jnp.maximum, tops)
    store["pieces"] = pieces
    store["top"] = jnp.max(top, axis=0, keepdims=True)


def soften_steps(store):
    weights = []
    for piece in store.pop("pieces"):
        weights.append(jnp.exp2((piece - store["top"]).astype(jnp.bfloat16)))
        yield
    store["weights"] = jnp.concatenate(weights, axis=0) if len(weights) > 1 else weights[0]


def blend(mixed, head_dim):
    count = mixed.shape[1] // 2
    inverse = 1.0 / mixed[2 * head_dim : 2 * head_dim + 1]
    return jnp.concatenate(
        [
            mixed[:head_dim, :count] * inverse[:, :count],
            mixed[head_dim : 2 * head_dim, count:] * inverse[:, count:],
        ],
        axis=0,
    ).astype(jnp.bfloat16)


def interleave(*steps):
    running = list(steps)
    while running:
        for step in list(running):
            try:
                next(step)
            except StopIteration:
                running.remove(step)


def run_pipeline(units, size, first, second, third, side):
    groups = [units[start : start + size] for start in range(0, len(units), size)]
    stores = {unit: {} for unit in units}

    def steps(action, index):
        if not 0 <= index < len(groups):
            return []
        return [action(unit, stores[unit]) for unit in groups[index]]

    interleave(*steps(first, 0))
    for index in range(len(groups)):
        interleave(
            *steps(first, index + 1),
            *steps(second, index),
            *steps(third, index - 1),
            side(index),
        )
    interleave(*steps(third, len(groups) - 1))


def block_diagonal(queries, base, head_dim, group):
    count = queries.shape[1]
    first = base % group
    left = queries[base : base + head_dim]
    right = queries[base + head_dim : base + 2 * head_dim]
    zero = jnp.zeros((head_dim, count), queries.dtype)
    body = jnp.concatenate(
        [jnp.concatenate([left, zero], axis=1), jnp.concatenate([zero, right], axis=1)], axis=0
    )
    pad = jnp.zeros((group - 2 * head_dim, 2 * count), queries.dtype)
    return jnp.concatenate([body, pad] if first == 0 else [pad, body], axis=0)


def phase_kernel(bins, heads, *refs):
    blocks = refs[: bins // 2]
    gain, weights_in, table, out_weight = refs[bins // 2 : bins // 2 + 4]
    outs = refs[bins // 2 + 4 :]
    chunk, width = blocks[0].shape[1:]
    head_dim = width // heads
    scale = LOG2E / math.sqrt(head_dim)
    tile = ROWS * bins
    tiles = chunk // ROWS
    pairs = heads // 2
    group = 128
    stream = jnp.concatenate(
        [
            blocks[slot // 2][slot % 2, step * ROWS : (step + 1) * ROWS]
            for step in range(tiles)
            for slot in range(bins)
        ],
        axis=0,
    ).astype(jnp.float32)
    normed = rms(stream, gain[...])
    keys = mm(normed, weights_in[2 * width :]).astype(jnp.bfloat16)
    both = mm(weights_in[: 2 * width], normed, NT)
    queries = (both[:width] * scale).astype(jnp.bfloat16)
    values = both[width:].astype(jnp.bfloat16)
    ones = jnp.ones((ROWS, tile), jnp.bfloat16)
    units = [(step, pair) for step in range(tiles) for pair in range(pairs)]
    parts = []

    def first(unit, store):
        step, pair = unit
        span = slice(step * tile, (step + 1) * tile)
        base = pair * 2 * head_dim
        frame = base // group * group
        return score_steps(
            keys[span, frame : frame + group],
            block_diagonal(queries[:, span], base, head_dim, group),
            [(0, tile, table[pair])],
            store,
        )

    def third(unit, store):
        step, pair = unit
        span = slice(step * tile, (step + 1) * tile)
        base = pair * 2 * head_dim
        stack = jnp.concatenate([values[base : base + 2 * head_dim, span], ones], axis=0)
        parts.append(blend(mm(stack, store.pop("weights")), head_dim))
        yield

    def finish(step):
        mixed = jnp.concatenate(parts[step * pairs : (step + 1) * pairs], axis=0)
        span = slice(step * tile, (step + 1) * tile)
        result = (stream[span] + mm(mixed, out_weight[...], TN)).astype(jnp.bfloat16)
        for slot in range(bins):
            outs[slot // 2][slot % 2, step * ROWS : (step + 1) * ROWS] = result[
                slot * ROWS : (slot + 1) * ROWS
            ]

    size = pairs

    def side(index):
        if index * size >= pairs and index * size % pairs == 0:
            yield
            finish(index * size // pairs - 1)

    run_pipeline(units, size, first, lambda _, store: soften_steps(store), third, side)
    finish(tiles - 1)


def pack_kernel(*refs):
    give = refs[-1]
    chunk = refs[0].shape[1]
    for step, source in enumerate(refs[:-1]):
        give[step * chunk : (step + 1) * chunk] = source[1]


def gather_kernel(plane, masks, *refs):
    half = len(masks) // 2
    got = refs[:half]
    twin, residual, inner, outer = refs[half:]
    me = lax.axis_index("phase")
    chunk = got[0].shape[1]
    for step in range(half):
        start = pl.multiple_of((me ^ masks[2 * step]) * chunk, ROWS)
        residual[pl.ds(start, chunk)] = got[step][0]
        start = pl.multiple_of((me ^ masks[2 * step + 1]) * chunk, ROWS)
        residual[pl.ds(start, chunk)] = twin[step * chunk : (step + 1) * chunk]
    reach = inner.shape[0]
    extra = residual.shape[0] - reach
    odd = lax.axis_index("space") % 2
    inner[...] = residual[pl.ds(pl.multiple_of((1 - odd) * extra, plane), reach)]
    outer[...] = residual[pl.ds(pl.multiple_of(odd * extra, plane), reach)]


def frame_of(keys, pair, head_dim, group):
    frame = pair * 2 * head_dim // group * group
    return keys[:, frame : frame + group]


def table_tiles(table, corner, pair, at, members, plane, z_first, depth):
    tiles = []
    for index, member in enumerate(members):
        z = z_first + member - REACH
        halves = []
        for side in range(2):
            step = member - REACH - at - corner[0, 2 * pair + side]
            inside = (step >= 0) & (step < SPAN) & (z >= 0) & (z < depth)
            start = pl.multiple_of(jnp.where(inside, step, SPAN) * plane, plane)
            halves.append(table[pair, pl.ds(start, plane), side * plane : (side + 1) * plane])
        tiles.append((index * plane, (index + 1) * plane, jnp.concatenate(halves, axis=1)))
    return tiles


def inside_kernel(
    plane, corner, own, gain_second, qkv, table, queries_out, values_out,
    part_mixed, part_top, part_sum
):
    tokens, width = own.shape
    planes = tokens // plane
    heads = corner.shape[1]
    pairs = heads // 2
    head_dim = width // heads
    scale = LOG2E / math.sqrt(head_dim)
    group = 128
    members = list(range(REACH, REACH + planes))
    z_first = lax.axis_index("space") * planes
    depth = lax.axis_size("space") * planes
    normed = rms(own[...].astype(jnp.float32), gain_second[...])
    keys = mm(normed, qkv[:, width : 2 * width]).astype(jnp.bfloat16)
    value_weight = qkv[:, 2 * width :].T
    values_out[...] = value_weight
    values = mm(value_weight, normed, NT).astype(jnp.bfloat16)
    queries = (mm(qkv[:, :width].T, normed, NT) * scale).astype(jnp.bfloat16)
    queries_out[...] = queries
    ones = jnp.ones((ROWS, tokens), jnp.bfloat16)
    frames = [frame_of(keys, pair, head_dim, group) for pair in range(pairs)]
    stacks = [
        jnp.concatenate([values[pair * 2 * head_dim : (pair + 1) * 2 * head_dim], ones], axis=0)
        for pair in range(pairs)
    ]
    units = [(at, pair) for at in range(planes) for pair in range(pairs)]

    def first(unit, store):
        at, pair = unit
        return score_steps(
            frames[pair],
            block_diagonal(
                queries[:, at * plane : (at + 1) * plane],
                pair * 2 * head_dim,
                head_dim,
                group,
            ),
            table_tiles(table, corner, pair, at, members, plane, z_first, depth),
            store,
        )

    def third(unit, store):
        at, pair = unit
        mixed = mm(stacks[pair], store.pop("weights"))
        base = pair * 2 * head_dim
        part_mixed[at, base : base + head_dim] = mixed[:head_dim, :plane]
        part_mixed[at, base + head_dim : base + 2 * head_dim] = mixed[
            head_dim : 2 * head_dim, plane:
        ]
        part_top[at, pair : pair + 1] = store["top"]
        part_sum[at, pair : pair + 1] = mixed[2 * head_dim : 2 * head_dim + 1]
        yield

    run_pipeline(units, 2, first, lambda _, store: soften_steps(store), third, lambda _: iter(()))


def outside_kernel(
    plane,
    corner,
    own,
    inner,
    outer,
    gain_second,
    qkv,
    table,
    queries,
    value_weight,
    part_mixed,
    part_top,
    part_sum,
    out_weight,
    gain_third,
    mlp_up,
    mlp_down,
    out,
    key_store,
    value_store,
):
    tokens, width = own.shape
    planes = tokens // plane
    heads = corner.shape[1]
    pairs = heads // 2
    head_dim = width // heads
    reach = REACH * plane
    group = 128
    gain = gain_second[...]
    place = lax.axis_index("space")
    is_even = place % 2 == 0
    z_first = place * planes
    depth = lax.axis_size("space") * planes
    key_weight = qkv[:, width : 2 * width]
    for source, at_end in ((inner, is_even), (outer, jnp.logical_not(is_even))):
        normed = rms(source[...].astype(jnp.float32), gain)
        rows = pl.ds(pl.multiple_of(jnp.where(at_end, reach, 0), plane), reach)
        key_store[rows] = mm(normed, key_weight).astype(jnp.bfloat16)
        value_store[:, rows] = mm(value_weight[...], normed, NT).astype(jnp.bfloat16)
    rim = list(range(REACH)) + list(range(REACH + planes, 2 * REACH + planes))
    ones = jnp.ones((ROWS, 2 * reach), jnp.bfloat16)
    frames = [frame_of(key_store, pair, head_dim, group) for pair in range(pairs)]
    stacks = [
        jnp.concatenate([value_store[pair * 2 * head_dim : (pair + 1) * 2 * head_dim], ones], axis=0)
        for pair in range(pairs)
    ]
    units = [(at, pair) for at in range(planes) for pair in range(pairs)]

    def span(at):
        return min(at, REACH), REACH + max(0, at + SPAN - planes)

    def first(unit, store):
        at, pair = unit
        start, stop = span(at)
        return score_steps(
            frames[pair][start * plane : stop * plane],
            block_diagonal(
                queries[:, at * plane : (at + 1) * plane],
                pair * 2 * head_dim,
                head_dim,
                group,
            ),
            table_tiles(table, corner, pair, at, rim[start:stop], plane, z_first, depth),
            store,
        )

    def second(unit, store):
        at, pair = unit
        before = part_top[at, pair : pair + 1]
        store["top"] = jnp.maximum(store["top"], before)
        store["ratio"] = jnp.exp2(before - store["top"])
        return soften_steps(store)

    parts = []

    def third(unit, store):
        at, pair = unit
        start, stop = span(at)
        mixed = mm(stacks[pair][:, start * plane : stop * plane], store.pop("weights"))
        ratio = store["ratio"]
        total = mixed[2 * head_dim : 2 * head_dim + 1] + ratio * part_sum[at, pair : pair + 1]
        inverse = 1.0 / total
        ratio = ratio * inverse
        halves = []
        for side in range(2):
            rows = slice(side * head_dim, (side + 1) * head_dim)
            lanes = slice(side * plane, (side + 1) * plane)
            base = (pair * 2 + side) * head_dim
            halves.append(
                mixed[rows, lanes] * inverse[:, lanes]
                + part_mixed[at, base : base + head_dim] * ratio[:, lanes]
            )
        parts.append(jnp.concatenate(halves, axis=0).astype(jnp.bfloat16))
        yield

    run_pipeline(units, 2, first, second, third, lambda _: iter(()))
    mixed = [jnp.concatenate(parts[at * pairs : (at + 1) * pairs], axis=0) for at in range(planes)]
    columns = width
    block = 2 * plane

    def mlp_steps(start):
        here = slice(start * plane, start * plane + block)
        joined = jnp.concatenate(mixed[start : start + 2], axis=1) if 2 > 1 else mixed[start]
        residual = own[here].astype(jnp.float32) + mm(joined, out_weight[...], TN)
        normed = rms(residual, gain_third[...])
        yield
        hiddens = []
        for first_column in range(0, mlp_up.shape[1], columns):
            hidden = mm(normed, mlp_up[:, first_column : first_column + columns])
            hiddens.append(gelu(hidden.astype(jnp.bfloat16)))
            yield
        hidden = jnp.concatenate(hiddens, axis=1)
        out[here] = (residual + mm(hidden, mlp_down[...])).astype(out.dtype)

    interleave(*(mlp_steps(start) for start in range(0, planes, 2)))


def gelu(values):
    half = values * 0.5
    cubic = values * (GELU_LINEAR + GELU_CUBIC * (values * values))
    return half + half * jnp.tanh(cubic)


VMEM = pl.BlockSpec(memory_space=pltpu.VMEM)
SMEM = pl.BlockSpec(memory_space=pltpu.SMEM)
ANY = pl.BlockSpec(memory_space=pl.ANY)
HBM = pl.BlockSpec(memory_space=pltpu.HBM)


def call(kernel, specs, shapes, args, limit, scratch=(), flops=0, bytes_accessed=0):
    return pl.pallas_call(
        kernel,
        in_specs=specs,
        out_specs=[VMEM] * len(shapes),
        out_shape=[jax.ShapeDtypeStruct(shape, dtype) for shape, dtype in shapes],
        scratch_shapes=list(scratch),
        compiler_params=pltpu.CompilerParams(vmem_limit_bytes=limit * MIB),
        cost_estimate=pl.CostEstimate(
            flops=flops, bytes_accessed=bytes_accessed, transcendentals=0
        ),
    )(*args)


def local(
    volume,
    gain_first,
    phase_qkv,
    phase_out,
    bin_phase,
    phase_bias,
    gain_second,
    window_qkv,
    window_out,
    window_corner,
    window_bias,
    gain_third,
    mlp_up,
    mlp_down,
):
    planes, extent_x, extent_y, width = volume.shape[1:]
    plane = extent_x * extent_y
    tokens = planes * plane
    heads = window_corner.shape[0]
    bins = lax.axis_size("phase")
    half = bins // 2
    chunk = tokens // bins
    tile = ROWS * bins
    me = lax.axis_index("phase")
    bf16, f32 = jnp.bfloat16, jnp.float32

    def swap(block, mask):
        return lax.ppermute(block, "phase", [(i, i ^ mask) for i in range(bins)])

    own = volume.reshape(tokens, width)
    twin = swap(own, 1)

    def piece(mask):
        start = (me ^ mask) * chunk
        return jnp.stack(
            [lax.dynamic_slice_in_dim(source, start, chunk, axis=0) for source in (own, twin)]
        )

    masks = [0, 1] + [2 * step + part for step in range(half - 1, 0, -1) for part in range(2)]
    pieces = [piece(mask) for mask in masks[::2]]
    blocks = pieces[:1] + [swap(pieces[step], masks[2 * step]) for step in range(1, half)]
    corner = window_corner.T

    phase_weights, phase_table, window_table = call(
        functools.partial(prep_kernel, masks, extent_x, extent_y),
        [HBM] * 5 + [ANY],
        [
            ((3 * width, width), bf16),
            ((heads // 2, tile, 2 * tile), f32),
            ((heads // 2, (SPAN + 1) * plane, 2 * plane), f32),
        ],
        [
            *(
                pltpu.with_memory_space_constraint(array, pltpu.HBM)
                for array in (bin_phase, corner, window_bias, phase_bias, phase_qkv)
            ),
            pieces[-1],
        ],
        12,
        scratch=[
            pltpu.SMEM(bin_phase.shape, jnp.int32),
            pltpu.SMEM(corner.shape, jnp.int32),
            pltpu.SMEM(window_bias.shape, f32),
            pltpu.VMEM(phase_bias.shape, f32),
            pltpu.VMEM(phase_qkv.shape, bf16),
            pltpu.SemaphoreType.DMA((5,)),
        ],
        flops=2 * 10**9,
        bytes_accessed=4 * 2**20,
    )
    results = call(
        functools.partial(phase_kernel, bins, heads),
        [VMEM] * (half + 4),
        [((2, chunk, width), bf16)] * half,
        [*blocks, gain_first.reshape(1, width), phase_weights, phase_table, phase_out],
        12,
        flops=2 * tokens * width * 5 * width,
        bytes_accessed=2**20,
    )
    got = [results[0]] + [swap(results[step], masks[2 * step]) for step in range(1, half)]
    (give,) = call(
        pack_kernel, [VMEM] * half, [((half * chunk, width), bf16)], [*got], 4
    )
    twin = swap(give, 1)
    reach = REACH * plane
    residual, inner, outer = call(
        functools.partial(gather_kernel, plane, masks),
        [VMEM] * (half + 1),
        [((tokens, width), bf16), ((reach, width), bf16), ((reach, width), bf16)],
        [*got, twin],
        4,
    )
    count = lax.axis_size("space")

    def partners(shift):
        pairs = []
        for i in range(bins):
            for place in range(count):
                other = ((place + shift) ^ 1) - shift
                target = (i, other) if 0 <= other < count else (i ^ 1, place)
                pairs.append((i * count + place, target[0] * count + target[1]))
        return pairs

    inner = lax.ppermute(inner, ("phase", "space"), partners(0))
    outer = lax.ppermute(outer, ("phase", "space"), partners(1))
    gain = gain_second.reshape(1, width)
    pairs = heads // 2
    partial = call(
        functools.partial(inside_kernel, plane),
        [SMEM] + [VMEM] * 4,
        [
            ((width, tokens), bf16),
            ((width, width), bf16),
            ((planes, width, plane), f32),
            ((planes, pairs, 2 * plane), f32),
            ((planes, pairs, 2 * plane), f32),
        ],
        [corner, residual, gain, window_qkv, window_table],
        16,
        flops=2 * tokens * width * 14 * width,
        bytes_accessed=2**22,
    )
    (out,) = call(
        functools.partial(outside_kernel, plane),
        [SMEM] + [VMEM] * 15,
        [((tokens, width), bf16)],
        [
            corner,
            residual,
            inner,
            outer,
            gain,
            window_qkv,
            window_table,
            *partial,
            window_out,
            gain_third.reshape(1, width),
            mlp_up,
            mlp_down,
        ],
        20,
        scratch=[pltpu.VMEM((2 * reach, width), bf16), pltpu.VMEM((width, 2 * reach), bf16)],
        flops=2 * tokens * width * 14 * width,
        bytes_accessed=2**22,
    )
    return out.reshape(volume.shape)


def solution(mesh):
    split = P("phase", "space", None, None, None)
    in_specs = (split,) + (P(),) * 13
    return jax.shard_map(local, mesh=mesh, in_specs=in_specs, out_specs=split, check_vma=False)
```

```python
import functools
import math

import jax
import jax.numpy as jnp
from jax import lax
from jax.experimental import pallas as pl
from jax.experimental.pallas import tpu as pltpu
from jax.sharding import PartitionSpec as P

EPSILON = 1e-06
LOG2E = math.log2(math.e)
NEG = -1e30
SPAN = 4
REACH = SPAN - 1
ROWS = 16
MIB = 2**20
GELU_LINEAR = math.sqrt(2.0 / math.pi)
GELU_CUBIC = 0.044715 * GELU_LINEAR

NT = (((1,), (1,)), ((), ()))
TN = (((0,), (0,)), ((), ()))


def mm(a, b, dims=(((1,), (0,)), ((), ()))):
    return lax.dot_general(a, b, dims, preferred_element_type=jnp.float32)


def rms(values, gain):
    mean_sq = jnp.mean(values * values, axis=-1, keepdims=True)
    return (values * lax.rsqrt(mean_sq + EPSILON) * gain).astype(jnp.bfloat16)


def prep_kernel(
    masks,
    extent_x,
    extent_y,
    bin_phase_at,
    corner_at,
    window_bias_at,
    phase_bias_at,
    phase_qkv_at,
    _,
    phase_weights,
    phase_table,
    window_table,
    bin_phase,
    corner,
    window_bias,
    phase_bias,
    phase_qkv,
    sems,
):
    copies = [
        pltpu.make_async_copy(source, target, sems.at[index])
        for index, (source, target) in enumerate(
            (
                (bin_phase_at, bin_phase),
                (corner_at, corner),
                (window_bias_at, window_bias),
                (phase_bias_at, phase_bias),
                (phase_qkv_at, phase_qkv),
            )
        )
    ]
    for copy in copies:
        copy.start()
    for copy in copies:
        copy.wait()
    width = phase_qkv.shape[0]
    heads = phase_bias.shape[0]
    phase_weights[:width] = phase_qkv[:, :width].T
    phase_weights[width : 2 * width] = phase_qkv[:, 2 * width :].T
    phase_weights[2 * width :] = phase_qkv[:, width : 2 * width]
    me = lax.axis_index("phase")
    bins = len(masks)
    tile = ROWS * bins
    slot = lax.broadcasted_iota(jnp.int32, (heads, tile), 1) // ROWS
    query_phase = jnp.zeros((heads, tile), jnp.int32)
    for member, mask in enumerate(masks):
        query_phase = jnp.where(slot == member, bin_phase[me ^ mask], query_phase)
    same = (
        lax.broadcasted_iota(jnp.int32, (ROWS, tile), 0)
        == lax.broadcasted_iota(jnp.int32, (ROWS, tile), 1) % ROWS
    )
    bias = phase_bias[...] * LOG2E
    for member, mask in enumerate(masks):
        gap = bin_phase[me ^ mask] - query_phase
        gap = jnp.where(gap < 0, gap + bins, gap)
        value = jnp.zeros((heads, tile), jnp.float32)
        for step in range(bins):
            value = jnp.where(gap == step, bias[:, step : step + 1], value)
        for head in range(heads):
            phase_table[
                head // 2,
                member * ROWS : (member + 1) * ROWS,
                (head % 2) * tile : (head % 2 + 1) * tile,
            ] = jnp.where(same, value[head : head + 1], NEG)
    plane = extent_x * extent_y
    window_table[:, SPAN * plane :] = jnp.full(
        (heads // 2, plane, 2 * plane), NEG, window_table.dtype
    )
    shape = (extent_y, plane)
    lane = lax.broadcasted_iota(jnp.int32, shape, 1)
    lane_x = lane // extent_y
    delta_y = lax.broadcasted_iota(jnp.int32, shape, 0) - lane % extent_y
    for head in range(heads):
        first_x = corner[1, head]
        first_y = corner[2, head]
        y_masks = [delta_y == first_y + step for step in range(SPAN)]
        for step_z in range(SPAN):
            strips = []
            for step_x in range(SPAN):
                strip = jnp.full(shape, NEG, jnp.float32)
                for step_y in range(SPAN):
                    entry = window_bias[head, (step_z * SPAN + step_x) * SPAN + step_y] * LOG2E
                    strip = jnp.where(y_masks[step_y], entry, strip)
                strips.append(strip)
            for key_x in range(extent_x):
                block = jnp.full(shape, NEG, jnp.float32)
                for step_x in range(SPAN):
                    block = jnp.where(
                        lane_x == key_x - first_x - step_x, strips[step_x], block
                    )
                start = step_z * plane + key_x * extent_y
                window_table[
                    head // 2,
                    start : start + extent_y,
                    (head % 2) * plane : (head % 2 + 1) * plane,
                ] = block


def score_steps(keys, queries, tiles, store):
    pieces = []
    tops = []
    whole = mm(keys, queries)
    for start, stop, table in tiles:
        piece = whole[start:stop] + table
        pieces.append(piece)
        tops.append(jnp.max(piece.reshape(-1, 8, piece.shape[1]), axis=0))
        yield
    top = functools.reduce(jnp.maximum, tops)
    store["pieces"] = pieces
    store["top"] = jnp.max(top, axis=0, keepdims=True)


def soften_steps(store):
    weights = []
    for piece in store.pop("pieces"):
        weights.append(jnp.exp2((piece - store["top"]).astype(jnp.bfloat16)))
        yield
    store["weights"] = jnp.concatenate(weights, axis=0) if len(weights) > 1 else weights[0]


def blend(mixed, head_dim):
    count = mixed.shape[1] // 2
    inverse = 1.0 / mixed[2 * head_dim : 2 * head_dim + 1]
    return jnp.concatenate(
        [
            mixed[:head_dim, :count] * inverse[:, :count],
            mixed[head_dim : 2 * head_dim, count:] * inverse[:, count:],
        ],
        axis=0,
    ).astype(jnp.bfloat16)


def interleave(*steps):
    running = list(steps)
    while running:
        for step in list(running):
            try:
                next(step)
            except StopIteration:
                running.remove(step)


def run_pipeline(units, size, first, second, third, side):
    groups = [units[start : start + size] for start in range(0, len(units), size)]
    stores = {unit: {} for unit in units}

    def steps(action, index):
        if not 0 <= index < len(groups):
            return []
        return [action(unit, stores[unit]) for unit in groups[index]]

    interleave(*steps(first, 0))
    for index in range(len(groups)):
        interleave(
            *steps(first, index + 1),
            *steps(second, index),
            *steps(third, index - 1),
            side(index),
        )
    interleave(*steps(third, len(groups) - 1))


def block_diagonal(queries, base, head_dim, group):
    count = queries.shape[1]
    first = base % group
    left = queries[base : base + head_dim]
    right = queries[base + head_dim : base + 2 * head_dim]
    zero = jnp.zeros((head_dim, count), queries.dtype)
    body = jnp.concatenate(
        [jnp.concatenate([left, zero], axis=1), jnp.concatenate([zero, right], axis=1)], axis=0
    )
    pad = jnp.zeros((group - 2 * head_dim, 2 * count), queries.dtype)
    return jnp.concatenate([body, pad] if first == 0 else [pad, body], axis=0)


def phase_kernel(bins, heads, *refs):
    blocks = refs[: bins // 2]
    gain, weights_in, table, out_weight = refs[bins // 2 : bins // 2 + 4]
    outs = refs[bins // 2 + 4 :]
    chunk, width = blocks[0].shape[1:]
    head_dim = width // heads
    scale = LOG2E / math.sqrt(head_dim)
    tile = ROWS * bins
    tiles = chunk // ROWS
    pairs = heads // 2
    group = 128
    stream = jnp.concatenate(
        [
            blocks[slot // 2][slot % 2, step * ROWS : (step + 1) * ROWS]
            for step in range(tiles)
            for slot in range(bins)
        ],
        axis=0,
    ).astype(jnp.float32)
    normed = rms(stream, gain[...])
    keys = mm(normed, weights_in[2 * width :]).astype(jnp.bfloat16)
    both = mm(weights_in[: 2 * width], normed, NT)
    queries = (both[:width] * scale).astype(jnp.bfloat16)
    values = both[width:].astype(jnp.bfloat16)
    ones = jnp.ones((ROWS, tile), jnp.bfloat16)
    units = [(step, pair) for step in range(tiles) for pair in range(pairs)]
    parts = []

    def first(unit, store):
        step, pair = unit
        span = slice(step * tile, (step + 1) * tile)
        base = pair * 2 * head_dim
        frame = base // group * group
        return score_steps(
            keys[span, frame : frame + group],
            block_diagonal(queries[:, span], base, head_dim, group),
            [(0, tile, table[pair])],
            store,
        )

    def third(unit, store):
        step, pair = unit
        span = slice(step * tile, (step + 1) * tile)
        base = pair * 2 * head_dim
        stack = jnp.concatenate([values[base : base + 2 * head_dim, span], ones], axis=0)
        parts.append(blend(mm(stack, store.pop("weights")), head_dim))
        yield

    def finish(steps):
        mixed = jnp.concatenate(
            [
                jnp.concatenate(parts[step * pairs : (step + 1) * pairs], axis=0)
                for step in steps
            ],
            axis=1,
        )
        span = slice(steps[0] * tile, (steps[-1] + 1) * tile)
        result = (stream[span] + mm(mixed, out_weight[...], TN)).astype(jnp.bfloat16)
        for index, step in enumerate(steps):
            for slot in range(bins):
                start = index * tile + slot * ROWS
                outs[slot // 2][slot % 2, step * ROWS : (step + 1) * ROWS] = result[
                    start : start + ROWS
                ]

    run_pipeline(
        units,
        len(units),
        first,
        lambda _, store: soften_steps(store),
        third,
        lambda _: iter(()),
    )
    finish(range(tiles))


def pack_kernel(*refs):
    give = refs[-1]
    chunk = refs[0].shape[1]
    for step, source in enumerate(refs[:-1]):
        give[step * chunk : (step + 1) * chunk] = source[1]


def gather_kernel(plane, masks, *refs):
    half = len(masks) // 2
    got = refs[:half]
    twin, residual, inner, outer = refs[half:]
    me = lax.axis_index("phase")
    chunk = got[0].shape[1]
    for step in range(half):
        start = pl.multiple_of((me ^ masks[2 * step]) * chunk, ROWS)
        residual[pl.ds(start, chunk)] = got[step][0]
        start = pl.multiple_of((me ^ masks[2 * step + 1]) * chunk, ROWS)
        residual[pl.ds(start, chunk)] = twin[step * chunk : (step + 1) * chunk]
    reach = inner.shape[0]
    extra = residual.shape[0] - reach
    odd = lax.axis_index("space") % 2
    inner[...] = residual[pl.ds(pl.multiple_of((1 - odd) * extra, plane), reach)]
    outer[...] = residual[pl.ds(pl.multiple_of(odd * extra, plane), reach)]


def frame_of(keys, pair, head_dim, group):
    frame = pair * 2 * head_dim // group * group
    return keys[:, frame : frame + group]


def table_tiles(table, corner, pair, at, members, plane, z_first, depth):
    tiles = []
    for index, member in enumerate(members):
        z = z_first + member - REACH
        halves = []
        for side in range(2):
            step = member - REACH - at - corner[0, 2 * pair + side]
            inside = (step >= 0) & (step < SPAN) & (z >= 0) & (z < depth)
            start = pl.multiple_of(jnp.where(inside, step, SPAN) * plane, plane)
            halves.append(table[pair, pl.ds(start, plane), side * plane : (side + 1) * plane])
        tiles.append((index * plane, (index + 1) * plane, jnp.concatenate(halves, axis=1)))
    return tiles


def inside_kernel(
    plane, corner, own, gain_second, qkv, table, queries_out, values_out,
    part_mixed, part_top, part_sum
):
    tokens, width = own.shape
    planes = tokens // plane
    heads = corner.shape[1]
    pairs = heads // 2
    head_dim = width // heads
    scale = LOG2E / math.sqrt(head_dim)
    group = 128
    members = list(range(REACH, REACH + planes))
    z_first = lax.axis_index("space") * planes
    depth = lax.axis_size("space") * planes
    normed = rms(own[...].astype(jnp.float32), gain_second[...])
    keys = mm(normed, qkv[:, width : 2 * width]).astype(jnp.bfloat16)
    value_weight = qkv[:, 2 * width :].T
    values_out[...] = value_weight
    values = mm(value_weight, normed, NT).astype(jnp.bfloat16)
    queries = (mm(qkv[:, :width].T, normed, NT) * scale).astype(jnp.bfloat16)
    queries_out[...] = queries
    ones = jnp.ones((ROWS, tokens), jnp.bfloat16)
    frames = [frame_of(keys, pair, head_dim, group) for pair in range(pairs)]
    stacks = [
        jnp.concatenate([values[pair * 2 * head_dim : (pair + 1) * 2 * head_dim], ones], axis=0)
        for pair in range(pairs)
    ]
    units = [(at, pair) for at in range(planes) for pair in range(pairs)]

    def first(unit, store):
        at, pair = unit
        return score_steps(
            frames[pair],
            block_diagonal(
                queries[:, at * plane : (at + 1) * plane],
                pair * 2 * head_dim,
                head_dim,
                group,
            ),
            table_tiles(table, corner, pair, at, members, plane, z_first, depth),
            store,
        )

    def third(unit, store):
        at, pair = unit
        mixed = mm(stacks[pair], store.pop("weights"))
        base = pair * 2 * head_dim
        part_mixed[at, base : base + head_dim] = mixed[:head_dim, :plane]
        part_mixed[at, base + head_dim : base + 2 * head_dim] = mixed[
            head_dim : 2 * head_dim, plane:
        ]
        part_top[at, pair : pair + 1] = store["top"]
        part_sum[at, pair : pair + 1] = mixed[2 * head_dim : 2 * head_dim + 1]
        yield

    run_pipeline(units, 2, first, lambda _, store: soften_steps(store), third, lambda _: iter(()))


def outside_kernel(
    plane,
    corner,
    own,
    inner,
    outer,
    gain_second,
    qkv,
    table,
    queries,
    value_weight,
    part_mixed,
    part_top,
    part_sum,
    out_weight,
    gain_third,
    mlp_up,
    mlp_down,
    out,
    key_store,
    value_store,
):
    tokens, width = own.shape
    planes = tokens // plane
    heads = corner.shape[1]
    pairs = heads // 2
    head_dim = width // heads
    reach = REACH * plane
    group = 128
    gain = gain_second[...]
    place = lax.axis_index("space")
    is_even = place % 2 == 0
    z_first = place * planes
    depth = lax.axis_size("space") * planes
    key_weight = qkv[:, width : 2 * width]
    for source, at_end in ((inner, is_even), (outer, jnp.logical_not(is_even))):
        normed = rms(source[...].astype(jnp.float32), gain)
        rows = pl.ds(pl.multiple_of(jnp.where(at_end, reach, 0), plane), reach)
        key_store[rows] = mm(normed, key_weight).astype(jnp.bfloat16)
        value_store[:, rows] = mm(value_weight[...], normed, NT).astype(jnp.bfloat16)
    rim = list(range(REACH)) + list(range(REACH + planes, 2 * REACH + planes))
    ones = jnp.ones((ROWS, 2 * reach), jnp.bfloat16)
    frames = [frame_of(key_store, pair, head_dim, group) for pair in range(pairs)]
    stacks = [
        jnp.concatenate([value_store[pair * 2 * head_dim : (pair + 1) * 2 * head_dim], ones], axis=0)
        for pair in range(pairs)
    ]
    units = [(at, pair) for at in range(planes) for pair in range(pairs)]

    def span(at):
        return min(at, REACH), REACH + max(0, at + SPAN - planes)

    def first(unit, store):
        at, pair = unit
        start, stop = span(at)
        return score_steps(
            frames[pair][start * plane : stop * plane],
            block_diagonal(
                queries[:, at * plane : (at + 1) * plane],
                pair * 2 * head_dim,
                head_dim,
                group,
            ),
            table_tiles(table, corner, pair, at, rim[start:stop], plane, z_first, depth),
            store,
        )

    def second(unit, store):
        at, pair = unit
        before = part_top[at, pair : pair + 1]
        store["top"] = jnp.maximum(store["top"], before)
        store["ratio"] = jnp.exp2(before - store["top"])
        return soften_steps(store)

    parts = []

    def third(unit, store):
        at, pair = unit
        start, stop = span(at)
        mixed = mm(stacks[pair][:, start * plane : stop * plane], store.pop("weights"))
        ratio = store["ratio"]
        total = mixed[2 * head_dim : 2 * head_dim + 1] + ratio * part_sum[at, pair : pair + 1]
        inverse = 1.0 / total
        ratio = ratio * inverse
        halves = []
        for side in range(2):
            rows = slice(side * head_dim, (side + 1) * head_dim)
            lanes = slice(side * plane, (side + 1) * plane)
            base = (pair * 2 + side) * head_dim
            halves.append(
                mixed[rows, lanes] * inverse[:, lanes]
                + part_mixed[at, base : base + head_dim] * ratio[:, lanes]
            )
        parts.append(jnp.concatenate(halves, axis=0).astype(jnp.bfloat16))
        yield

    run_pipeline(units, 2, first, second, third, lambda _: iter(()))
    mixed = [jnp.concatenate(parts[at * pairs : (at + 1) * pairs], axis=0) for at in range(planes)]
    columns = width
    block = 2 * plane

    def mlp_steps(start):
        here = slice(start * plane, start * plane + block)
        joined = jnp.concatenate(mixed[start : start + 2], axis=1) if 2 > 1 else mixed[start]
        residual = own[here].astype(jnp.float32) + mm(joined, out_weight[...], TN)
        normed = rms(residual, gain_third[...])
        yield
        hiddens = []
        for first_column in range(0, mlp_up.shape[1], columns):
            hidden = mm(normed, mlp_up[:, first_column : first_column + columns])
            hiddens.append(gelu(hidden.astype(jnp.bfloat16)))
            yield
        hidden = jnp.concatenate(hiddens, axis=1)
        out[here] = (residual + mm(hidden, mlp_down[...])).astype(out.dtype)

    interleave(*(mlp_steps(start) for start in range(0, planes, 2)))


def gelu(values):
    half = values * 0.5
    cubic = values * (GELU_LINEAR + GELU_CUBIC * (values * values))
    return half + half * jnp.tanh(cubic)


VMEM = pl.BlockSpec(memory_space=pltpu.VMEM)
SMEM = pl.BlockSpec(memory_space=pltpu.SMEM)
ANY = pl.BlockSpec(memory_space=pl.ANY)
HBM = pl.BlockSpec(memory_space=pltpu.HBM)


def call(kernel, specs, shapes, args, limit, scratch=(), flops=0, bytes_accessed=0):
    return pl.pallas_call(
        kernel,
        in_specs=specs,
        out_specs=[VMEM] * len(shapes),
        out_shape=[jax.ShapeDtypeStruct(shape, dtype) for shape, dtype in shapes],
        scratch_shapes=list(scratch),
        compiler_params=pltpu.CompilerParams(vmem_limit_bytes=limit * MIB),
        cost_estimate=pl.CostEstimate(
            flops=flops, bytes_accessed=bytes_accessed, transcendentals=0
        ),
    )(*args)


def local(
    volume,
    gain_first,
    phase_qkv,
    phase_out,
    bin_phase,
    phase_bias,
    gain_second,
    window_qkv,
    window_out,
    window_corner,
    window_bias,
    gain_third,
    mlp_up,
    mlp_down,
):
    planes, extent_x, extent_y, width = volume.shape[1:]
    plane = extent_x * extent_y
    tokens = planes * plane
    heads = window_corner.shape[0]
    bins = lax.axis_size("phase")
    half = bins // 2
    chunk = tokens // bins
    tile = ROWS * bins
    me = lax.axis_index("phase")
    bf16, f32 = jnp.bfloat16, jnp.float32

    def swap(block, mask):
        return lax.ppermute(block, "phase", [(i, i ^ mask) for i in range(bins)])

    own = volume.reshape(tokens, width)
    twin = swap(own, 1)

    def piece(mask):
        start = (me ^ mask) * chunk
        return jnp.stack(
            [lax.dynamic_slice_in_dim(source, start, chunk, axis=0) for source in (own, twin)]
        )

    masks = [0, 1] + [2 * step + part for step in range(half - 1, 0, -1) for part in range(2)]
    pieces = [piece(mask) for mask in masks[::2]]
    blocks = pieces[:1] + [swap(pieces[step], masks[2 * step]) for step in range(1, half)]
    corner = window_corner.T

    phase_weights, phase_table, window_table = call(
        functools.partial(prep_kernel, masks, extent_x, extent_y),
        [HBM] * 5 + [ANY],
        [
            ((3 * width, width), bf16),
            ((heads // 2, tile, 2 * tile), f32),
            ((heads // 2, (SPAN + 1) * plane, 2 * plane), f32),
        ],
        [
            *(
                pltpu.with_memory_space_constraint(array, pltpu.HBM)
                for array in (bin_phase, corner, window_bias, phase_bias, phase_qkv)
            ),
            pieces[-1],
        ],
        12,
        scratch=[
            pltpu.SMEM(bin_phase.shape, jnp.int32),
            pltpu.SMEM(corner.shape, jnp.int32),
            pltpu.SMEM(window_bias.shape, f32),
            pltpu.VMEM(phase_bias.shape, f32),
            pltpu.VMEM(phase_qkv.shape, bf16),
            pltpu.SemaphoreType.DMA((5,)),
        ],
        flops=2 * 10**9,
        bytes_accessed=4 * 2**20,
    )
    results = call(
        functools.partial(phase_kernel, bins, heads),
        [VMEM] * (half + 4),
        [((2, chunk, width), bf16)] * half,
        [*blocks, gain_first.reshape(1, width), phase_weights, phase_table, phase_out],
        12,
        flops=2 * tokens * width * 5 * width,
        bytes_accessed=2**20,
    )
    got = [results[0]] + [swap(results[step], masks[2 * step]) for step in range(1, half)]
    (give,) = call(
        pack_kernel, [VMEM] * half, [((half * chunk, width), bf16)], [*got], 4
    )
    twin = swap(give, 1)
    reach = REACH * plane
    residual, inner, outer = call(
        functools.partial(gather_kernel, plane, masks),
        [VMEM] * (half + 1),
        [((tokens, width), bf16), ((reach, width), bf16), ((reach, width), bf16)],
        [*got, twin],
        4,
    )
    count = lax.axis_size("space")

    def partners(shift):
        pairs = []
        for i in range(bins):
            for place in range(count):
                other = ((place + shift) ^ 1) - shift
                target = (i, other) if 0 <= other < count else (i ^ 1, place)
                pairs.append((i * count + place, target[0] * count + target[1]))
        return pairs

    inner = lax.ppermute(inner, ("phase", "space"), partners(0))
    outer = lax.ppermute(outer, ("phase", "space"), partners(1))
    gain = gain_second.reshape(1, width)
    pairs = heads // 2
    partial = call(
        functools.partial(inside_kernel, plane),
        [SMEM] + [VMEM] * 4,
        [
            ((width, tokens), bf16),
            ((width, width), bf16),
            ((planes, width, plane), f32),
            ((planes, pairs, 2 * plane), f32),
            ((planes, pairs, 2 * plane), f32),
        ],
        [corner, residual, gain, window_qkv, window_table],
        16,
        flops=2 * tokens * width * 14 * width,
        bytes_accessed=2**22,
    )
    (out,) = call(
        functools.partial(outside_kernel, plane),
        [SMEM] + [VMEM] * 15,
        [((tokens, width), bf16)],
        [
            corner,
            residual,
            inner,
            outer,
            gain,
            window_qkv,
            window_table,
            *partial,
            window_out,
            gain_third.reshape(1, width),
            mlp_up,
            mlp_down,
        ],
        20,
        scratch=[pltpu.VMEM((2 * reach, width), bf16), pltpu.VMEM((width, 2 * reach), bf16)],
        flops=2 * tokens * width * 14 * width,
        bytes_accessed=2**22,
    )
    return out.reshape(volume.shape)


def solution(mesh):
    split = P("phase", "space", None, None, None)
    in_specs = (split,) + (P(),) * 13
    return jax.shard_map(local, mesh=mesh, in_specs=in_specs, out_specs=split, check_vma=False)
```

```python
import functools
import math

import jax
import jax.numpy as jnp
from jax import lax
from jax.experimental import pallas as pl
from jax.experimental.pallas import tpu as pltpu
from jax.sharding import PartitionSpec as P

EPSILON = 1e-06
LOG2E = math.log2(math.e)
NEG = -1e30
SPAN = 4
REACH = SPAN - 1
ROWS = 16
MIB = 2**20
GELU_LINEAR = math.sqrt(2.0 / math.pi)
GELU_CUBIC = 0.044715 * GELU_LINEAR

NT = (((1,), (1,)), ((), ()))
TN = (((0,), (0,)), ((), ()))


def mm(a, b, dims=(((1,), (0,)), ((), ()))):
    return lax.dot_general(a, b, dims, preferred_element_type=jnp.float32)


def rms(values, gain):
    mean_sq = jnp.mean(values * values, axis=-1, keepdims=True)
    return (values * lax.rsqrt(mean_sq + EPSILON) * gain).astype(jnp.bfloat16)


def prep_kernel(
    masks,
    extent_x,
    extent_y,
    bin_phase_at,
    corner_at,
    window_bias_at,
    phase_bias_at,
    phase_qkv_at,
    _,
    phase_weights,
    phase_table,
    window_table,
    bin_phase,
    corner,
    window_bias,
    phase_bias,
    phase_qkv,
    sems,
):
    copies = [
        pltpu.make_async_copy(source, target, sems.at[index])
        for index, (source, target) in enumerate(
            (
                (bin_phase_at, bin_phase),
                (corner_at, corner),
                (window_bias_at, window_bias),
                (phase_bias_at, phase_bias),
                (phase_qkv_at, phase_qkv),
            )
        )
    ]
    for copy in copies:
        copy.start()
    for copy in copies:
        copy.wait()
    width = phase_qkv.shape[0]
    heads = phase_bias.shape[0]
    phase_weights[:width] = phase_qkv[:, :width].T
    phase_weights[width : 2 * width] = phase_qkv[:, 2 * width :].T
    phase_weights[2 * width :] = phase_qkv[:, width : 2 * width]
    me = lax.axis_index("phase")
    bins = len(masks)
    tile = ROWS * bins
    slot = lax.broadcasted_iota(jnp.int32, (heads, tile), 1) // ROWS
    query_phase = jnp.zeros((heads, tile), jnp.int32)
    for member, mask in enumerate(masks):
        query_phase = jnp.where(slot == member, bin_phase[me ^ mask], query_phase)
    same = (
        lax.broadcasted_iota(jnp.int32, (ROWS, tile), 0)
        == lax.broadcasted_iota(jnp.int32, (ROWS, tile), 1) % ROWS
    )
    bias = phase_bias[...] * LOG2E
    for member, mask in enumerate(masks):
        gap = bin_phase[me ^ mask] - query_phase
        gap = jnp.where(gap < 0, gap + bins, gap)
        value = jnp.zeros((heads, tile), jnp.float32)
        for step in range(bins):
            value = jnp.where(gap == step, bias[:, step : step + 1], value)
        for head in range(heads):
            phase_table[
                head // 2,
                member * ROWS : (member + 1) * ROWS,
                (head % 2) * tile : (head % 2 + 1) * tile,
            ] = jnp.where(same, value[head : head + 1], NEG)
    plane = extent_x * extent_y
    window_table[:, SPAN * plane :] = jnp.full(
        (heads // 2, plane, 2 * plane), NEG, window_table.dtype
    )
    shape = (extent_y, plane)
    lane = lax.broadcasted_iota(jnp.int32, shape, 1)
    lane_x = lane // extent_y
    delta_y = lax.broadcasted_iota(jnp.int32, shape, 0) - lane % extent_y
    for head in range(heads):
        first_x = corner[1, head]
        first_y = corner[2, head]
        y_masks = [delta_y == first_y + step for step in range(SPAN)]
        for step_z in range(SPAN):
            strips = []
            for step_x in range(SPAN):
                strip = jnp.full(shape, NEG, jnp.float32)
                for step_y in range(SPAN):
                    entry = window_bias[head, (step_z * SPAN + step_x) * SPAN + step_y] * LOG2E
                    strip = jnp.where(y_masks[step_y], entry, strip)
                strips.append(strip)
            for key_x in range(extent_x):
                block = jnp.full(shape, NEG, jnp.float32)
                for step_x in range(SPAN):
                    block = jnp.where(
                        lane_x == key_x - first_x - step_x, strips[step_x], block
                    )
                start = step_z * plane + key_x * extent_y
                window_table[
                    head // 2,
                    start : start + extent_y,
                    (head % 2) * plane : (head % 2 + 1) * plane,
                ] = block


def score_steps(keys, queries, tiles, store):
    pieces = []
    tops = []
    whole = mm(keys, queries)
    for start, stop, table in tiles:
        piece = whole[start:stop] + table
        pieces.append(piece)
        tops.append(jnp.max(piece.reshape(-1, 8, piece.shape[1]), axis=0))
        yield
    top = functools.reduce(jnp.maximum, tops)
    store["pieces"] = pieces
    store["top"] = jnp.max(top, axis=0, keepdims=True)


def soften_steps(store):
    weights = []
    for piece in store.pop("pieces"):
        weights.append(jnp.exp2((piece - store["top"]).astype(jnp.bfloat16)))
        yield
    store["weights"] = jnp.concatenate(weights, axis=0) if len(weights) > 1 else weights[0]


def blend(mixed, head_dim):
    count = mixed.shape[1] // 2
    inverse = 1.0 / mixed[2 * head_dim : 2 * head_dim + 1]
    return jnp.concatenate(
        [
            mixed[:head_dim, :count] * inverse[:, :count],
            mixed[head_dim : 2 * head_dim, count:] * inverse[:, count:],
        ],
        axis=0,
    ).astype(jnp.bfloat16)


def interleave(*steps):
    running = list(steps)
    while running:
        for step in list(running):
            try:
                next(step)
            except StopIteration:
                running.remove(step)


def run_pipeline(units, size, first, second, third, side):
    groups = [units[start : start + size] for start in range(0, len(units), size)]
    stores = {unit: {} for unit in units}

    def steps(action, index):
        if not 0 <= index < len(groups):
            return []
        return [action(unit, stores[unit]) for unit in groups[index]]

    interleave(*steps(first, 0))
    for index in range(len(groups)):
        interleave(
            *steps(first, index + 1),
            *steps(second, index),
            *steps(third, index - 1),
            side(index),
        )
    interleave(*steps(third, len(groups) - 1))


def block_diagonal(queries, base, head_dim, group):
    count = queries.shape[1]
    first = base % group
    left = queries[base : base + head_dim]
    right = queries[base + head_dim : base + 2 * head_dim]
    zero = jnp.zeros((head_dim, count), queries.dtype)
    body = jnp.concatenate(
        [jnp.concatenate([left, zero], axis=1), jnp.concatenate([zero, right], axis=1)], axis=0
    )
    pad = jnp.zeros((group - 2 * head_dim, 2 * count), queries.dtype)
    return jnp.concatenate([body, pad] if first == 0 else [pad, body], axis=0)


def phase_kernel(bins, heads, *refs):
    blocks = refs[: bins // 2]
    gain, weights_in, table, out_weight = refs[bins // 2 : bins // 2 + 4]
    passed, *kept = refs[bins // 2 + 4 :]
    chunk, width = blocks[0].shape[1:]
    head_dim = width // heads
    scale = LOG2E / math.sqrt(head_dim)
    tile = ROWS * bins
    tiles = chunk // ROWS
    pairs = heads // 2
    group = 128
    stream = jnp.concatenate(
        [
            blocks[slot // 2][slot % 2, step * ROWS : (step + 1) * ROWS]
            for step in range(tiles)
            for slot in range(bins)
        ],
        axis=0,
    ).astype(jnp.float32)
    normed = rms(stream, gain[...])
    keys = mm(normed, weights_in[2 * width :]).astype(jnp.bfloat16)
    both = mm(weights_in[: 2 * width], normed, NT)
    queries = (both[:width] * scale).astype(jnp.bfloat16)
    values = both[width:].astype(jnp.bfloat16)
    ones = jnp.ones((ROWS, tile), jnp.bfloat16)
    units = [(step, pair) for step in range(tiles) for pair in range(pairs)]
    parts = []

    def first(unit, store):
        step, pair = unit
        span = slice(step * tile, (step + 1) * tile)
        base = pair * 2 * head_dim
        frame = base // group * group
        return score_steps(
            keys[span, frame : frame + group],
            block_diagonal(queries[:, span], base, head_dim, group),
            [(0, tile, table[pair])],
            store,
        )

    def third(unit, store):
        step, pair = unit
        span = slice(step * tile, (step + 1) * tile)
        base = pair * 2 * head_dim
        stack = jnp.concatenate([values[base : base + 2 * head_dim, span], ones], axis=0)
        parts.append(blend(mm(stack, store.pop("weights")), head_dim))
        yield

    def finish(steps):
        mixed = jnp.concatenate(
            [
                jnp.concatenate(parts[step * pairs : (step + 1) * pairs], axis=0)
                for step in steps
            ],
            axis=1,
        )
        span = slice(steps[0] * tile, (steps[-1] + 1) * tile)
        result = (stream[span] + mm(mixed, out_weight[...], TN)).astype(jnp.bfloat16)
        for index, step in enumerate(steps):
            for slot in range(bins):
                start = index * tile + slot * ROWS
                target = passed.at[slot // 2] if slot % 2 else kept[slot // 2]
                target[step * ROWS : (step + 1) * ROWS] = result[start : start + ROWS]

    run_pipeline(
        units,
        len(units),
        first,
        lambda _, store: soften_steps(store),
        third,
        lambda _: iter(()),
    )
    finish(range(tiles))


def join_kernel(taken, *refs):
    half = len(refs) // 2
    for step in range(half):
        refs[half + step][0] = refs[step][...]
        refs[half + step][1] = taken[step]


def gather_kernel(plane, masks, *refs):
    half = len(masks) // 2
    got = refs[:half]
    residual, inner, outer = refs[half:]
    me = lax.axis_index("phase")
    chunk = got[0].shape[1]
    for slot, mask in enumerate(masks):
        start = pl.multiple_of((me ^ mask) * chunk, ROWS)
        residual[pl.ds(start, chunk)] = got[slot // 2][slot % 2]
    reach = inner.shape[0]
    extra = residual.shape[0] - reach
    odd = lax.axis_index("space") % 2
    inner[...] = residual[pl.ds(pl.multiple_of((1 - odd) * extra, plane), reach)]
    outer[...] = residual[pl.ds(pl.multiple_of(odd * extra, plane), reach)]


def frame_of(keys, pair, head_dim, group):
    frame = pair * 2 * head_dim // group * group
    return keys[:, frame : frame + group]


def table_tiles(table, corner, pair, at, members, plane, z_first, depth):
    tiles = []
    for index, member in enumerate(members):
        z = z_first + member - REACH
        halves = []
        for side in range(2):
            step = member - REACH - at - corner[0, 2 * pair + side]
            inside = (step >= 0) & (step < SPAN) & (z >= 0) & (z < depth)
            start = pl.multiple_of(jnp.where(inside, step, SPAN) * plane, plane)
            halves.append(table[pair, pl.ds(start, plane), side * plane : (side + 1) * plane])
        tiles.append((index * plane, (index + 1) * plane, jnp.concatenate(halves, axis=1)))
    return tiles


def inside_kernel(
    plane, corner, own, gain_second, qkv, table, queries_out, values_out,
    part_mixed, part_top, part_sum
):
    tokens, width = own.shape
    planes = tokens // plane
    heads = corner.shape[1]
    pairs = heads // 2
    head_dim = width // heads
    scale = LOG2E / math.sqrt(head_dim)
    group = 128
    members = list(range(REACH, REACH + planes))
    z_first = lax.axis_index("space") * planes
    depth = lax.axis_size("space") * planes
    normed = rms(own[...].astype(jnp.float32), gain_second[...])
    keys = mm(normed, qkv[:, width : 2 * width]).astype(jnp.bfloat16)
    value_weight = qkv[:, 2 * width :].T
    values_out[...] = value_weight
    values = mm(value_weight, normed, NT).astype(jnp.bfloat16)
    queries = (mm(qkv[:, :width].T, normed, NT) * scale).astype(jnp.bfloat16)
    queries_out[...] = queries
    ones = jnp.ones((ROWS, tokens), jnp.bfloat16)
    frames = [frame_of(keys, pair, head_dim, group) for pair in range(pairs)]
    stacks = [
        jnp.concatenate([values[pair * 2 * head_dim : (pair + 1) * 2 * head_dim], ones], axis=0)
        for pair in range(pairs)
    ]
    units = [(at, pair) for at in range(planes) for pair in range(pairs)]

    def first(unit, store):
        at, pair = unit
        return score_steps(
            frames[pair],
            block_diagonal(
                queries[:, at * plane : (at + 1) * plane],
                pair * 2 * head_dim,
                head_dim,
                group,
            ),
            table_tiles(table, corner, pair, at, members, plane, z_first, depth),
            store,
        )

    def third(unit, store):
        at, pair = unit
        mixed = mm(stacks[pair], store.pop("weights"))
        base = pair * 2 * head_dim
        part_mixed[at, base : base + head_dim] = mixed[:head_dim, :plane]
        part_mixed[at, base + head_dim : base + 2 * head_dim] = mixed[
            head_dim : 2 * head_dim, plane:
        ]
        part_top[at, pair : pair + 1] = store["top"]
        part_sum[at, pair : pair + 1] = mixed[2 * head_dim : 2 * head_dim + 1]
        yield

    run_pipeline(units, 2, first, lambda _, store: soften_steps(store), third, lambda _: iter(()))


def outside_kernel(
    plane,
    corner,
    own,
    inner,
    outer,
    gain_second,
    qkv,
    table,
    queries,
    value_weight,
    part_mixed,
    part_top,
    part_sum,
    out_weight,
    gain_third,
    mlp_up,
    mlp_down,
    out,
    key_store,
    value_store,
):
    tokens, width = own.shape
    planes = tokens // plane
    heads = corner.shape[1]
    pairs = heads // 2
    head_dim = width // heads
    reach = REACH * plane
    group = 128
    gain = gain_second[...]
    place = lax.axis_index("space")
    is_even = place % 2 == 0
    z_first = place * planes
    depth = lax.axis_size("space") * planes
    key_weight = qkv[:, width : 2 * width]
    for source, at_end in ((inner, is_even), (outer, jnp.logical_not(is_even))):
        normed = rms(source[...].astype(jnp.float32), gain)
        rows = pl.ds(pl.multiple_of(jnp.where(at_end, reach, 0), plane), reach)
        key_store[rows] = mm(normed, key_weight).astype(jnp.bfloat16)
        value_store[:, rows] = mm(value_weight[...], normed, NT).astype(jnp.bfloat16)
    rim = list(range(REACH)) + list(range(REACH + planes, 2 * REACH + planes))
    ones = jnp.ones((ROWS, 2 * reach), jnp.bfloat16)
    frames = [frame_of(key_store, pair, head_dim, group) for pair in range(pairs)]
    stacks = [
        jnp.concatenate([value_store[pair * 2 * head_dim : (pair + 1) * 2 * head_dim], ones], axis=0)
        for pair in range(pairs)
    ]
    units = [(at, pair) for at in range(planes) for pair in range(pairs)]

    def span(at):
        return min(at, REACH), REACH + max(0, at + SPAN - planes)

    def first(unit, store):
        at, pair = unit
        start, stop = span(at)
        return score_steps(
            frames[pair][start * plane : stop * plane],
            block_diagonal(
                queries[:, at * plane : (at + 1) * plane],
                pair * 2 * head_dim,
                head_dim,
                group,
            ),
            table_tiles(table, corner, pair, at, rim[start:stop], plane, z_first, depth),
            store,
        )

    def second(unit, store):
        at, pair = unit
        before = part_top[at, pair : pair + 1]
        store["top"] = jnp.maximum(store["top"], before)
        store["ratio"] = jnp.exp2(before - store["top"])
        return soften_steps(store)

    parts = []

    def third(unit, store):
        at, pair = unit
        start, stop = span(at)
        mixed = mm(stacks[pair][:, start * plane : stop * plane], store.pop("weights"))
        ratio = store["ratio"]
        total = mixed[2 * head_dim : 2 * head_dim + 1] + ratio * part_sum[at, pair : pair + 1]
        inverse = 1.0 / total
        ratio = ratio * inverse
        halves = []
        for side in range(2):
            rows = slice(side * head_dim, (side + 1) * head_dim)
            lanes = slice(side * plane, (side + 1) * plane)
            base = (pair * 2 + side) * head_dim
            halves.append(
                mixed[rows, lanes] * inverse[:, lanes]
                + part_mixed[at, base : base + head_dim] * ratio[:, lanes]
            )
        parts.append(jnp.concatenate(halves, axis=0).astype(jnp.bfloat16))
        yield

    run_pipeline(units, 2, first, second, third, lambda _: iter(()))
    mixed = [jnp.concatenate(parts[at * pairs : (at + 1) * pairs], axis=0) for at in range(planes)]
    columns = width
    block = 2 * plane

    def mlp_steps(start):
        here = slice(start * plane, start * plane + block)
        joined = jnp.concatenate(mixed[start : start + 2], axis=1) if 2 > 1 else mixed[start]
        residual = own[here].astype(jnp.float32) + mm(joined, out_weight[...], TN)
        normed = rms(residual, gain_third[...])
        yield
        hiddens = []
        for first_column in range(0, mlp_up.shape[1], columns):
            hidden = mm(normed, mlp_up[:, first_column : first_column + columns])
            hiddens.append(gelu(hidden.astype(jnp.bfloat16)))
            yield
        hidden = jnp.concatenate(hiddens, axis=1)
        out[here] = (residual + mm(hidden, mlp_down[...])).astype(out.dtype)

    interleave(*(mlp_steps(start) for start in range(0, planes, 2)))


def gelu(values):
    half = values * 0.5
    cubic = values * (GELU_LINEAR + GELU_CUBIC * (values * values))
    return half + half * jnp.tanh(cubic)


VMEM = pl.BlockSpec(memory_space=pltpu.VMEM)
SMEM = pl.BlockSpec(memory_space=pltpu.SMEM)
ANY = pl.BlockSpec(memory_space=pl.ANY)
HBM = pl.BlockSpec(memory_space=pltpu.HBM)


def call(kernel, specs, shapes, args, limit, scratch=(), flops=0, bytes_accessed=0):
    return pl.pallas_call(
        kernel,
        in_specs=specs,
        out_specs=[VMEM] * len(shapes),
        out_shape=[jax.ShapeDtypeStruct(shape, dtype) for shape, dtype in shapes],
        scratch_shapes=list(scratch),
        compiler_params=pltpu.CompilerParams(vmem_limit_bytes=limit * MIB),
        cost_estimate=pl.CostEstimate(
            flops=flops, bytes_accessed=bytes_accessed, transcendentals=0
        ),
    )(*args)


def local(
    volume,
    gain_first,
    phase_qkv,
    phase_out,
    bin_phase,
    phase_bias,
    gain_second,
    window_qkv,
    window_out,
    window_corner,
    window_bias,
    gain_third,
    mlp_up,
    mlp_down,
):
    planes, extent_x, extent_y, width = volume.shape[1:]
    plane = extent_x * extent_y
    tokens = planes * plane
    heads = window_corner.shape[0]
    bins = lax.axis_size("phase")
    half = bins // 2
    chunk = tokens // bins
    tile = ROWS * bins
    me = lax.axis_index("phase")
    bf16, f32 = jnp.bfloat16, jnp.float32

    def swap(block, mask):
        return lax.ppermute(block, "phase", [(i, i ^ mask) for i in range(bins)])

    own = volume.reshape(tokens, width)
    twin = swap(own, 1)

    def piece(mask):
        start = (me ^ mask) * chunk
        return jnp.stack(
            [lax.dynamic_slice_in_dim(source, start, chunk, axis=0) for source in (own, twin)]
        )

    masks = [0, 1] + [2 * step + part for step in range(half - 1, 0, -1) for part in range(2)]
    pieces = [piece(mask) for mask in masks[::2]]
    blocks = pieces[:1] + [swap(pieces[step], masks[2 * step]) for step in range(1, half)]
    corner = window_corner.T

    phase_weights, phase_table, window_table = call(
        functools.partial(prep_kernel, masks, extent_x, extent_y),
        [HBM] * 5 + [ANY],
        [
            ((3 * width, width), bf16),
            ((heads // 2, tile, 2 * tile), f32),
            ((heads // 2, (SPAN + 1) * plane, 2 * plane), f32),
        ],
        [
            *(
                pltpu.with_memory_space_constraint(array, pltpu.HBM)
                for array in (bin_phase, corner, window_bias, phase_bias, phase_qkv)
            ),
            pieces[-1],
        ],
        12,
        scratch=[
            pltpu.SMEM(bin_phase.shape, jnp.int32),
            pltpu.SMEM(corner.shape, jnp.int32),
            pltpu.SMEM(window_bias.shape, f32),
            pltpu.VMEM(phase_bias.shape, f32),
            pltpu.VMEM(phase_qkv.shape, bf16),
            pltpu.SemaphoreType.DMA((5,)),
        ],
        flops=2 * 10**9,
        bytes_accessed=4 * 2**20,
    )
    passed, *kept = call(
        functools.partial(phase_kernel, bins, heads),
        [VMEM] * (half + 4),
        [((half, chunk, width), bf16)] + [((chunk, width), bf16)] * half,
        [*blocks, gain_first.reshape(1, width), phase_weights, phase_table, phase_out],
        12,
        flops=2 * tokens * width * 5 * width,
        bytes_accessed=2**20,
    )
    results = call(
        join_kernel,
        [VMEM] * (half + 1),
        [((2, chunk, width), bf16)] * half,
        [swap(passed, 1), *kept],
        4,
    )
    got = [results[0]] + [swap(results[step], masks[2 * step]) for step in range(1, half)]
    reach = REACH * plane
    residual, inner, outer = call(
        functools.partial(gather_kernel, plane, masks),
        [VMEM] * half,
        [((tokens, width), bf16), ((reach, width), bf16), ((reach, width), bf16)],
        got,
        4,
    )
    count = lax.axis_size("space")

    def partners(shift):
        pairs = []
        for i in range(bins):
            for place in range(count):
                other = ((place + shift) ^ 1) - shift
                target = (i, other) if 0 <= other < count else (i ^ 1, place)
                pairs.append((i * count + place, target[0] * count + target[1]))
        return pairs

    inner = lax.ppermute(inner, ("phase", "space"), partners(0))
    outer = lax.ppermute(outer, ("phase", "space"), partners(1))
    gain = gain_second.reshape(1, width)
    pairs = heads // 2
    partial = call(
        functools.partial(inside_kernel, plane),
        [SMEM] + [VMEM] * 4,
        [
            ((width, tokens), bf16),
            ((width, width), bf16),
            ((planes, width, plane), f32),
            ((planes, pairs, 2 * plane), f32),
            ((planes, pairs, 2 * plane), f32),
        ],
        [corner, residual, gain, window_qkv, window_table],
        16,
        flops=2 * tokens * width * 14 * width,
        bytes_accessed=2**22,
    )
    (out,) = call(
        functools.partial(outside_kernel, plane),
        [SMEM] + [VMEM] * 15,
        [((tokens, width), bf16)],
        [
            corner,
            residual,
            inner,
            outer,
            gain,
            window_qkv,
            window_table,
            *partial,
            window_out,
            gain_third.reshape(1, width),
            mlp_up,
            mlp_down,
        ],
        20,
        scratch=[pltpu.VMEM((2 * reach, width), bf16), pltpu.VMEM((width, 2 * reach), bf16)],
        flops=2 * tokens * width * 14 * width,
        bytes_accessed=2**22,
    )
    return out.reshape(volume.shape)


def solution(mesh):
    split = P("phase", "space", None, None, None)
    in_specs = (split,) + (P(),) * 13
    return jax.shard_map(local, mesh=mesh, in_specs=in_specs, out_specs=split, check_vma=False)
```

```python
import functools
import math

import jax
import jax.numpy as jnp
from jax import lax
from jax.experimental import pallas as pl
from jax.experimental.pallas import tpu as pltpu
from jax.sharding import PartitionSpec as P

EPSILON = 1e-06
LOG2E = math.log2(math.e)
NEG = -1e30
SPAN = 4
REACH = SPAN - 1
ROWS = 16
MIB = 2**20
GELU_LINEAR = math.sqrt(2.0 / math.pi)
GELU_CUBIC = 0.044715 * GELU_LINEAR

NT = (((1,), (1,)), ((), ()))
TN = (((0,), (0,)), ((), ()))


def mm(a, b, dims=(((1,), (0,)), ((), ()))):
    return lax.dot_general(a, b, dims, preferred_element_type=jnp.float32)


def rms(values, gain):
    mean_sq = jnp.mean(values * values, axis=-1, keepdims=True)
    return (values * lax.rsqrt(mean_sq + EPSILON) * gain).astype(jnp.bfloat16)


def prep_kernel(
    masks,
    extent_x,
    extent_y,
    bin_phase_at,
    corner_at,
    window_bias_at,
    phase_bias_at,
    phase_qkv_at,
    _,
    phase_weights,
    phase_table,
    window_table,
    bin_phase,
    corner,
    window_bias,
    phase_bias,
    phase_qkv,
    sems,
):
    copies = [
        pltpu.make_async_copy(source, target, sems.at[index])
        for index, (source, target) in enumerate(
            (
                (bin_phase_at, bin_phase),
                (corner_at, corner),
                (window_bias_at, window_bias),
                (phase_bias_at, phase_bias),
                (phase_qkv_at, phase_qkv),
            )
        )
    ]
    for copy in copies:
        copy.start()
    for copy in copies:
        copy.wait()
    width = phase_qkv.shape[0]
    heads = phase_bias.shape[0]
    phase_weights[:width] = phase_qkv[:, :width].T
    phase_weights[width : 2 * width] = phase_qkv[:, 2 * width :].T
    phase_weights[2 * width :] = phase_qkv[:, width : 2 * width]
    me = lax.axis_index("phase")
    bins = len(masks)
    tile = ROWS * bins
    slot = lax.broadcasted_iota(jnp.int32, (heads, tile), 1) // ROWS
    query_phase = jnp.zeros((heads, tile), jnp.int32)
    for member, mask in enumerate(masks):
        query_phase = jnp.where(slot == member, bin_phase[me ^ mask], query_phase)
    same = (
        lax.broadcasted_iota(jnp.int32, (ROWS, tile), 0)
        == lax.broadcasted_iota(jnp.int32, (ROWS, tile), 1) % ROWS
    )
    bias = phase_bias[...] * LOG2E
    for member, mask in enumerate(masks):
        gap = bin_phase[me ^ mask] - query_phase
        gap = jnp.where(gap < 0, gap + bins, gap)
        value = jnp.zeros((heads, tile), jnp.float32)
        for step in range(bins):
            value = jnp.where(gap == step, bias[:, step : step + 1], value)
        for head in range(heads):
            phase_table[
                head // 2,
                member * ROWS : (member + 1) * ROWS,
                (head % 2) * tile : (head % 2 + 1) * tile,
            ] = jnp.where(same, value[head : head + 1], NEG)
    plane = extent_x * extent_y
    window_table[:, SPAN * plane :] = jnp.full(
        (heads // 2, plane, 2 * plane), NEG, window_table.dtype
    )
    shape = (extent_y, plane)
    lane = lax.broadcasted_iota(jnp.int32, shape, 1)
    lane_x = lane // extent_y
    delta_y = lax.broadcasted_iota(jnp.int32, shape, 0) - lane % extent_y
    for head in range(heads):
        first_x = corner[1, head]
        first_y = corner[2, head]
        y_masks = [delta_y == first_y + step for step in range(SPAN)]
        for step_z in range(SPAN):
            strips = []
            for step_x in range(SPAN):
                strip = jnp.full(shape, NEG, jnp.float32)
                for step_y in range(SPAN):
                    entry = window_bias[head, (step_z * SPAN + step_x) * SPAN + step_y] * LOG2E
                    strip = jnp.where(y_masks[step_y], entry, strip)
                strips.append(strip)
            for key_x in range(extent_x):
                block = jnp.full(shape, NEG, jnp.float32)
                for step_x in range(SPAN):
                    block = jnp.where(
                        lane_x == key_x - first_x - step_x, strips[step_x], block
                    )
                start = step_z * plane + key_x * extent_y
                window_table[
                    head // 2,
                    start : start + extent_y,
                    (head % 2) * plane : (head % 2 + 1) * plane,
                ] = block


def score_steps(keys, queries, tiles, store):
    pieces = []
    tops = []
    whole = mm(keys, queries)
    for start, stop, table in tiles:
        piece = whole[start:stop] + table
        pieces.append(piece)
        tops.append(jnp.max(piece.reshape(-1, 8, piece.shape[1]), axis=0))
        yield
    top = functools.reduce(jnp.maximum, tops)
    store["pieces"] = pieces
    store["top"] = jnp.max(top, axis=0, keepdims=True)


def soften_steps(store):
    weights = []
    for piece in store.pop("pieces"):
        weights.append(jnp.exp2((piece - store["top"]).astype(jnp.bfloat16)))
        yield
    store["weights"] = jnp.concatenate(weights, axis=0) if len(weights) > 1 else weights[0]


def blend(mixed, head_dim):
    count = mixed.shape[1] // 2
    inverse = 1.0 / mixed[2 * head_dim : 2 * head_dim + 1]
    return jnp.concatenate(
        [
            mixed[:head_dim, :count] * inverse[:, :count],
            mixed[head_dim : 2 * head_dim, count:] * inverse[:, count:],
        ],
        axis=0,
    ).astype(jnp.bfloat16)


def interleave(*steps):
    running = list(steps)
    while running:
        for step in list(running):
            try:
                next(step)
            except StopIteration:
                running.remove(step)


def run_pipeline(units, size, first, second, third, side):
    groups = [units[start : start + size] for start in range(0, len(units), size)]
    stores = {unit: {} for unit in units}

    def steps(action, index):
        if not 0 <= index < len(groups):
            return []
        return [action(unit, stores[unit]) for unit in groups[index]]

    interleave(*steps(first, 0))
    for index in range(len(groups)):
        interleave(
            *steps(first, index + 1),
            *steps(second, index),
            *steps(third, index - 1),
            side(index),
        )
    interleave(*steps(third, len(groups) - 1))


def block_diagonal(queries, base, head_dim, group):
    count = queries.shape[1]
    first = base % group
    left = queries[base : base + head_dim]
    right = queries[base + head_dim : base + 2 * head_dim]
    zero = jnp.zeros((head_dim, count), queries.dtype)
    body = jnp.concatenate(
        [jnp.concatenate([left, zero], axis=1), jnp.concatenate([zero, right], axis=1)], axis=0
    )
    pad = jnp.zeros((group - 2 * head_dim, 2 * count), queries.dtype)
    return jnp.concatenate([body, pad] if first == 0 else [pad, body], axis=0)


def phase_kernel(bins, heads, *refs):
    blocks = refs[: bins // 2]
    gain, weights_in, table, out_weight = refs[bins // 2 : bins // 2 + 4]
    passed, *kept = refs[bins // 2 + 4 :]
    chunk, width = blocks[0].shape[1:]
    head_dim = width // heads
    scale = LOG2E / math.sqrt(head_dim)
    tile = ROWS * bins
    tiles = chunk // ROWS
    pairs = heads // 2
    group = 128
    stream = jnp.concatenate(
        [
            blocks[slot // 2][slot % 2, step * ROWS : (step + 1) * ROWS]
            for step in range(tiles)
            for slot in range(bins)
        ],
        axis=0,
    ).astype(jnp.float32)
    normed = rms(stream, gain[...])
    keys = mm(normed, weights_in[2 * width :]).astype(jnp.bfloat16)
    both = mm(weights_in[: 2 * width], normed, NT)
    queries = (both[:width] * scale).astype(jnp.bfloat16)
    values = both[width:].astype(jnp.bfloat16)
    ones = jnp.ones((ROWS, tile), jnp.bfloat16)
    units = [(step, pair) for step in range(tiles) for pair in range(pairs)]
    parts = []

    def first(unit, store):
        step, pair = unit
        span = slice(step * tile, (step + 1) * tile)
        base = pair * 2 * head_dim
        frame = base // group * group
        return score_steps(
            keys[span, frame : frame + group],
            block_diagonal(queries[:, span], base, head_dim, group),
            [(0, tile, table[pair])],
            store,
        )

    def third(unit, store):
        step, pair = unit
        span = slice(step * tile, (step + 1) * tile)
        base = pair * 2 * head_dim
        stack = jnp.concatenate([values[base : base + 2 * head_dim, span], ones], axis=0)
        parts.append(blend(mm(stack, store.pop("weights")), head_dim))
        yield

    def finish(steps):
        mixed = jnp.concatenate(
            [
                jnp.concatenate(parts[step * pairs : (step + 1) * pairs], axis=0)
                for step in steps
            ],
            axis=1,
        )
        span = slice(steps[0] * tile, (steps[-1] + 1) * tile)
        result = (stream[span] + mm(mixed, out_weight[...], TN)).astype(jnp.bfloat16)
        for index, step in enumerate(steps):
            for slot in range(bins):
                start = index * tile + slot * ROWS
                target = passed.at[slot // 2] if slot % 2 else kept[slot // 2]
                target[step * ROWS : (step + 1) * ROWS] = result[start : start + ROWS]

    run_pipeline(
        units,
        len(units),
        first,
        lambda _, store: soften_steps(store),
        third,
        lambda _: iter(()),
    )
    finish(range(tiles))


def join_kernel(taken, *refs):
    half = len(refs) // 2
    for step in range(half):
        refs[half + step][0] = refs[step][...]
        refs[half + step][1] = taken[step]


def gather_kernel(plane, masks, *refs):
    half = len(masks) // 2
    got = refs[:half]
    residual, inner, outer = refs[half:]
    me = lax.axis_index("phase")
    chunk = got[0].shape[1]
    for slot, mask in enumerate(masks):
        start = pl.multiple_of((me ^ mask) * chunk, ROWS)
        residual[pl.ds(start, chunk)] = got[slot // 2][slot % 2]
    reach = inner.shape[0]
    extra = residual.shape[0] - reach
    odd = lax.axis_index("space") % 2
    inner[...] = residual[pl.ds(pl.multiple_of((1 - odd) * extra, plane), reach)]
    outer[...] = residual[pl.ds(pl.multiple_of(odd * extra, plane), reach)]


def frame_of(keys, pair, head_dim, group):
    frame = pair * 2 * head_dim // group * group
    return keys[:, frame : frame + group]


def table_tiles(table, corner, pair, at, members, plane, z_first, depth):
    tiles = []
    for index, member in enumerate(members):
        z = z_first + member - REACH
        halves = []
        for side in range(2):
            step = member - REACH - at - corner[0, 2 * pair + side]
            inside = (step >= 0) & (step < SPAN) & (z >= 0) & (z < depth)
            start = pl.multiple_of(jnp.where(inside, step, SPAN) * plane, plane)
            halves.append(table[pair, pl.ds(start, plane), side * plane : (side + 1) * plane])
        tiles.append((index * plane, (index + 1) * plane, jnp.concatenate(halves, axis=1)))
    return tiles


def inside_kernel(
    plane, corner, own, gain_second, qkv, table, queries_out, values_out,
    part_mixed, part_top, part_sum
):
    tokens, width = own.shape
    planes = tokens // plane
    heads = corner.shape[1]
    pairs = heads // 2
    head_dim = width // heads
    scale = LOG2E / math.sqrt(head_dim)
    group = 128
    members = list(range(REACH, REACH + planes))
    z_first = lax.axis_index("space") * planes
    depth = lax.axis_size("space") * planes
    normed = rms(own[...].astype(jnp.float32), gain_second[...])
    keys = mm(normed, qkv[:, width : 2 * width]).astype(jnp.bfloat16)
    value_weight = qkv[:, 2 * width :].T
    values_out[...] = value_weight
    values = mm(value_weight, normed, NT).astype(jnp.bfloat16)
    queries = (mm(qkv[:, :width].T, normed, NT) * scale).astype(jnp.bfloat16)
    queries_out[...] = queries
    ones = jnp.ones((ROWS, tokens), jnp.bfloat16)
    frames = [frame_of(keys, pair, head_dim, group) for pair in range(pairs)]
    stacks = [
        jnp.concatenate([values[pair * 2 * head_dim : (pair + 1) * 2 * head_dim], ones], axis=0)
        for pair in range(pairs)
    ]
    units = [(at, pair) for at in range(planes) for pair in range(pairs)]

    def first(unit, store):
        at, pair = unit
        return score_steps(
            frames[pair],
            block_diagonal(
                queries[:, at * plane : (at + 1) * plane],
                pair * 2 * head_dim,
                head_dim,
                group,
            ),
            table_tiles(table, corner, pair, at, members, plane, z_first, depth),
            store,
        )

    def third(unit, store):
        at, pair = unit
        mixed = mm(stacks[pair], store.pop("weights"))
        base = pair * 2 * head_dim
        part_mixed[at, base : base + head_dim] = mixed[:head_dim, :plane]
        part_mixed[at, base + head_dim : base + 2 * head_dim] = mixed[
            head_dim : 2 * head_dim, plane:
        ]
        part_top[at, pair : pair + 1] = store["top"]
        part_sum[at, pair : pair + 1] = mixed[2 * head_dim : 2 * head_dim + 1]
        yield

    run_pipeline(units, 2, first, lambda _, store: soften_steps(store), third, lambda _: iter(()))


def outside_kernel(
    plane,
    corner,
    own,
    inner,
    outer,
    gain_second,
    qkv,
    table,
    queries,
    value_weight,
    part_mixed,
    part_top,
    part_sum,
    out_weight,
    gain_third,
    mlp_up,
    mlp_down,
    out,
    key_store,
    value_store,
):
    tokens, width = own.shape
    planes = tokens // plane
    heads = corner.shape[1]
    pairs = heads // 2
    head_dim = width // heads
    reach = REACH * plane
    group = 128
    gain = gain_second[...]
    place = lax.axis_index("space")
    is_even = place % 2 == 0
    z_first = place * planes
    depth = lax.axis_size("space") * planes
    key_weight = qkv[:, width : 2 * width]
    normed = jnp.concatenate(
        [rms(source[...].astype(jnp.float32), gain) for source in (inner, outer)], axis=0
    )
    keys = mm(normed, key_weight).astype(jnp.bfloat16)
    values = mm(value_weight[...], normed, NT).astype(jnp.bfloat16)
    for index, at_end in enumerate((is_even, jnp.logical_not(is_even))):
        rows = pl.ds(pl.multiple_of(jnp.where(at_end, reach, 0), plane), reach)
        part = slice(index * reach, (index + 1) * reach)
        key_store[rows] = keys[part]
        value_store[:, rows] = values[:, part]
    rim = list(range(REACH)) + list(range(REACH + planes, 2 * REACH + planes))
    ones = jnp.ones((ROWS, 2 * reach), jnp.bfloat16)
    frames = [frame_of(key_store, pair, head_dim, group) for pair in range(pairs)]
    stacks = [
        jnp.concatenate([value_store[pair * 2 * head_dim : (pair + 1) * 2 * head_dim], ones], axis=0)
        for pair in range(pairs)
    ]
    units = [(at, pair) for at in range(planes) for pair in range(pairs)]

    def span(at):
        return min(at, REACH), REACH + max(0, at + SPAN - planes)

    def first(unit, store):
        at, pair = unit
        start, stop = span(at)
        return score_steps(
            frames[pair][start * plane : stop * plane],
            block_diagonal(
                queries[:, at * plane : (at + 1) * plane],
                pair * 2 * head_dim,
                head_dim,
                group,
            ),
            table_tiles(table, corner, pair, at, rim[start:stop], plane, z_first, depth),
            store,
        )

    def second(unit, store):
        at, pair = unit
        before = part_top[at, pair : pair + 1]
        store["top"] = jnp.maximum(store["top"], before)
        store["ratio"] = jnp.exp2(before - store["top"])
        return soften_steps(store)

    parts = []

    def third(unit, store):
        at, pair = unit
        start, stop = span(at)
        mixed = mm(stacks[pair][:, start * plane : stop * plane], store.pop("weights"))
        ratio = store["ratio"]
        total = mixed[2 * head_dim : 2 * head_dim + 1] + ratio * part_sum[at, pair : pair + 1]
        inverse = 1.0 / total
        ratio = ratio * inverse
        halves = []
        for side in range(2):
            rows = slice(side * head_dim, (side + 1) * head_dim)
            lanes = slice(side * plane, (side + 1) * plane)
            base = (pair * 2 + side) * head_dim
            halves.append(
                mixed[rows, lanes] * inverse[:, lanes]
                + part_mixed[at, base : base + head_dim] * ratio[:, lanes]
            )
        parts.append(jnp.concatenate(halves, axis=0).astype(jnp.bfloat16))
        yield

    run_pipeline(units, 2, first, second, third, lambda _: iter(()))
    mixed = [jnp.concatenate(parts[at * pairs : (at + 1) * pairs], axis=0) for at in range(planes)]
    block = 2 * plane

    def mlp_steps(start):
        here = slice(start * plane, start * plane + block)
        joined = jnp.concatenate(mixed[start : start + 2], axis=1)
        residual = own[here].astype(jnp.float32) + mm(joined, out_weight[...], TN)
        normed = rms(residual, gain_third[...])
        yield
        hidden = gelu(mm(normed, mlp_up[...]).astype(jnp.bfloat16))
        yield
        out[here] = (residual + mm(hidden, mlp_down[...])).astype(out.dtype)

    interleave(*(mlp_steps(start) for start in range(0, planes, 2)))


def gelu(values):
    half = values * 0.5
    cubic = values * (GELU_LINEAR + GELU_CUBIC * (values * values))
    return half + half * jnp.tanh(cubic)


VMEM = pl.BlockSpec(memory_space=pltpu.VMEM)
SMEM = pl.BlockSpec(memory_space=pltpu.SMEM)
ANY = pl.BlockSpec(memory_space=pl.ANY)
HBM = pl.BlockSpec(memory_space=pltpu.HBM)


def call(kernel, specs, shapes, args, limit, scratch=(), flops=0, bytes_accessed=0):
    return pl.pallas_call(
        kernel,
        in_specs=specs,
        out_specs=[VMEM] * len(shapes),
        out_shape=[jax.ShapeDtypeStruct(shape, dtype) for shape, dtype in shapes],
        scratch_shapes=list(scratch),
        compiler_params=pltpu.CompilerParams(vmem_limit_bytes=limit * MIB),
        cost_estimate=pl.CostEstimate(
            flops=flops, bytes_accessed=bytes_accessed, transcendentals=0
        ),
    )(*args)


def local(
    volume,
    gain_first,
    phase_qkv,
    phase_out,
    bin_phase,
    phase_bias,
    gain_second,
    window_qkv,
    window_out,
    window_corner,
    window_bias,
    gain_third,
    mlp_up,
    mlp_down,
):
    planes, extent_x, extent_y, width = volume.shape[1:]
    plane = extent_x * extent_y
    tokens = planes * plane
    heads = window_corner.shape[0]
    bins = lax.axis_size("phase")
    half = bins // 2
    chunk = tokens // bins
    tile = ROWS * bins
    me = lax.axis_index("phase")
    bf16, f32 = jnp.bfloat16, jnp.float32

    def swap(block, mask):
        return lax.ppermute(block, "phase", [(i, i ^ mask) for i in range(bins)])

    own = volume.reshape(tokens, width)
    twin = swap(own, 1)

    def piece(mask):
        start = (me ^ mask) * chunk
        return jnp.stack(
            [lax.dynamic_slice_in_dim(source, start, chunk, axis=0) for source in (own, twin)]
        )

    masks = [0, 1] + [2 * step + part for step in range(half - 1, 0, -1) for part in range(2)]
    pieces = [piece(mask) for mask in masks[::2]]
    blocks = pieces[:1] + [swap(pieces[step], masks[2 * step]) for step in range(1, half)]
    corner = window_corner.T

    phase_weights, phase_table, window_table = call(
        functools.partial(prep_kernel, masks, extent_x, extent_y),
        [HBM] * 5 + [ANY],
        [
            ((3 * width, width), bf16),
            ((heads // 2, tile, 2 * tile), f32),
            ((heads // 2, (SPAN + 1) * plane, 2 * plane), f32),
        ],
        [
            *(
                pltpu.with_memory_space_constraint(array, pltpu.HBM)
                for array in (bin_phase, corner, window_bias, phase_bias, phase_qkv)
            ),
            pieces[-1],
        ],
        12,
        scratch=[
            pltpu.SMEM(bin_phase.shape, jnp.int32),
            pltpu.SMEM(corner.shape, jnp.int32),
            pltpu.SMEM(window_bias.shape, f32),
            pltpu.VMEM(phase_bias.shape, f32),
            pltpu.VMEM(phase_qkv.shape, bf16),
            pltpu.SemaphoreType.DMA((5,)),
        ],
        flops=2 * 10**9,
        bytes_accessed=4 * 2**20,
    )
    passed, *kept = call(
        functools.partial(phase_kernel, bins, heads),
        [VMEM] * (half + 4),
        [((half, chunk, width), bf16)] + [((chunk, width), bf16)] * half,
        [*blocks, gain_first.reshape(1, width), phase_weights, phase_table, phase_out],
        12,
        flops=2 * tokens * width * 5 * width,
        bytes_accessed=2**20,
    )
    results = call(
        join_kernel,
        [VMEM] * (half + 1),
        [((2, chunk, width), bf16)] * half,
        [swap(passed, 1), *kept],
        4,
    )
    got = [results[0]] + [swap(results[step], masks[2 * step]) for step in range(1, half)]
    reach = REACH * plane
    residual, inner, outer = call(
        functools.partial(gather_kernel, plane, masks),
        [VMEM] * half,
        [((tokens, width), bf16), ((reach, width), bf16), ((reach, width), bf16)],
        got,
        4,
    )
    count = lax.axis_size("space")

    def partners(shift):
        pairs = []
        for i in range(bins):
            for place in range(count):
                other = ((place + shift) ^ 1) - shift
                target = (i, other) if 0 <= other < count else (i ^ 1, place)
                pairs.append((i * count + place, target[0] * count + target[1]))
        return pairs

    inner = lax.ppermute(inner, ("phase", "space"), partners(0))
    outer = lax.ppermute(outer, ("phase", "space"), partners(1))
    gain = gain_second.reshape(1, width)
    pairs = heads // 2
    partial = call(
        functools.partial(inside_kernel, plane),
        [SMEM] + [VMEM] * 4,
        [
            ((width, tokens), bf16),
            ((width, width), bf16),
            ((planes, width, plane), f32),
            ((planes, pairs, 2 * plane), f32),
            ((planes, pairs, 2 * plane), f32),
        ],
        [corner, residual, gain, window_qkv, window_table],
        16,
        flops=2 * tokens * width * 14 * width,
        bytes_accessed=2**22,
    )
    (out,) = call(
        functools.partial(outside_kernel, plane),
        [SMEM] + [VMEM] * 15,
        [((tokens, width), bf16)],
        [
            corner,
            residual,
            inner,
            outer,
            gain,
            window_qkv,
            window_table,
            *partial,
            window_out,
            gain_third.reshape(1, width),
            mlp_up,
            mlp_down,
        ],
        20,
        scratch=[pltpu.VMEM((2 * reach, width), bf16), pltpu.VMEM((width, 2 * reach), bf16)],
        flops=2 * tokens * width * 14 * width,
        bytes_accessed=2**22,
    )
    return out.reshape(volume.shape)


def solution(mesh):
    split = P("phase", "space", None, None, None)
    in_specs = (split,) + (P(),) * 13
    return jax.shard_map(local, mesh=mesh, in_specs=in_specs, out_specs=split, check_vma=False)
```

```python
import functools
import math

import jax
import jax.numpy as jnp
from jax import lax
from jax.experimental import pallas as pl
from jax.experimental.pallas import tpu as pltpu
from jax.sharding import PartitionSpec as P

EPSILON = 1e-06
LOG2E = math.log2(math.e)
NEG = -1e30
SPAN = 4
REACH = SPAN - 1
ROWS = 16
MIB = 2**20
GELU_LINEAR = math.sqrt(2.0 / math.pi)
GELU_CUBIC = 0.044715 * GELU_LINEAR

NT = (((1,), (1,)), ((), ()))
TN = (((0,), (0,)), ((), ()))


def mm(a, b, dims=(((1,), (0,)), ((), ()))):
    return lax.dot_general(a, b, dims, preferred_element_type=jnp.float32)


def rms(values, gain):
    mean_sq = jnp.mean(values * values, axis=-1, keepdims=True)
    return (values * lax.rsqrt(mean_sq + EPSILON) * gain).astype(jnp.bfloat16)


def prep_kernel(
    masks,
    extent_x,
    extent_y,
    bin_phase_at,
    corner_at,
    window_bias_at,
    phase_bias_at,
    phase_qkv_at,
    _,
    phase_weights,
    phase_table,
    window_table,
    bin_phase,
    corner,
    window_bias,
    phase_bias,
    phase_qkv,
    sems,
):
    copies = [
        pltpu.make_async_copy(source, target, sems.at[index])
        for index, (source, target) in enumerate(
            (
                (bin_phase_at, bin_phase),
                (corner_at, corner),
                (window_bias_at, window_bias),
                (phase_bias_at, phase_bias),
                (phase_qkv_at, phase_qkv),
            )
        )
    ]
    for copy in copies:
        copy.start()
    for copy in copies:
        copy.wait()
    width = phase_qkv.shape[0]
    heads = phase_bias.shape[0]
    phase_weights[:width] = phase_qkv[:, :width].T
    phase_weights[width : 2 * width] = phase_qkv[:, 2 * width :].T
    phase_weights[2 * width :] = phase_qkv[:, width : 2 * width]
    me = lax.axis_index("phase")
    bins = len(masks)
    tile = ROWS * bins
    slot = lax.broadcasted_iota(jnp.int32, (heads, tile), 1) // ROWS
    query_phase = jnp.zeros((heads, tile), jnp.int32)
    for member, mask in enumerate(masks):
        query_phase = jnp.where(slot == member, bin_phase[me ^ mask], query_phase)
    same = (
        lax.broadcasted_iota(jnp.int32, (ROWS, tile), 0)
        == lax.broadcasted_iota(jnp.int32, (ROWS, tile), 1) % ROWS
    )
    bias = phase_bias[...] * LOG2E
    for member, mask in enumerate(masks):
        gap = bin_phase[me ^ mask] - query_phase
        gap = jnp.where(gap < 0, gap + bins, gap)
        value = jnp.zeros((heads, tile), jnp.float32)
        for step in range(bins):
            value = jnp.where(gap == step, bias[:, step : step + 1], value)
        for head in range(heads):
            phase_table[
                head // 2,
                member * ROWS : (member + 1) * ROWS,
                (head % 2) * tile : (head % 2 + 1) * tile,
            ] = jnp.where(same, value[head : head + 1], NEG)
    plane = extent_x * extent_y
    window_table[:, SPAN * plane :] = jnp.full(
        (heads // 2, plane, 2 * plane), NEG, window_table.dtype
    )
    shape = (extent_y, plane)
    lane = lax.broadcasted_iota(jnp.int32, shape, 1)
    lane_x = lane // extent_y
    delta_y = lax.broadcasted_iota(jnp.int32, shape, 0) - lane % extent_y
    for head in range(heads):
        first_x = corner[1, head]
        first_y = corner[2, head]
        y_masks = [delta_y == first_y + step for step in range(SPAN)]
        for step_z in range(SPAN):
            strips = []
            for step_x in range(SPAN):
                strip = jnp.full(shape, NEG, jnp.float32)
                for step_y in range(SPAN):
                    entry = window_bias[head, (step_z * SPAN + step_x) * SPAN + step_y] * LOG2E
                    strip = jnp.where(y_masks[step_y], entry, strip)
                strips.append(strip)
            for key_x in range(extent_x):
                block = jnp.full(shape, NEG, jnp.float32)
                for step_x in range(SPAN):
                    block = jnp.where(
                        lane_x == key_x - first_x - step_x, strips[step_x], block
                    )
                start = step_z * plane + key_x * extent_y
                window_table[
                    head // 2,
                    start : start + extent_y,
                    (head % 2) * plane : (head % 2 + 1) * plane,
                ] = block


def score_steps(keys, queries, tiles, store):
    pieces = []
    tops = []
    whole = mm(keys, queries)
    for start, stop, table in tiles:
        piece = whole[start:stop] + table
        pieces.append(piece)
        tops.append(jnp.max(piece.reshape(-1, 8, piece.shape[1]), axis=0))
        yield
    top = functools.reduce(jnp.maximum, tops)
    store["pieces"] = pieces
    store["top"] = jnp.max(top, axis=0, keepdims=True)


def soften_steps(store):
    weights = []
    for piece in store.pop("pieces"):
        weights.append(jnp.exp2((piece - store["top"]).astype(jnp.bfloat16)))
        yield
    store["weights"] = jnp.concatenate(weights, axis=0) if len(weights) > 1 else weights[0]


def blend(mixed, head_dim):
    count = mixed.shape[1] // 2
    inverse = 1.0 / mixed[2 * head_dim : 2 * head_dim + 1]
    return jnp.concatenate(
        [
            mixed[:head_dim, :count] * inverse[:, :count],
            mixed[head_dim : 2 * head_dim, count:] * inverse[:, count:],
        ],
        axis=0,
    ).astype(jnp.bfloat16)


def interleave(*steps):
    running = list(steps)
    while running:
        for step in list(running):
            try:
                next(step)
            except StopIteration:
                running.remove(step)


def run_pipeline(units, size, first, second, third, side):
    groups = [units[start : start + size] for start in range(0, len(units), size)]
    stores = {unit: {} for unit in units}

    def steps(action, index):
        if not 0 <= index < len(groups):
            return []
        return [action(unit, stores[unit]) for unit in groups[index]]

    interleave(*steps(first, 0))
    for index in range(len(groups)):
        interleave(
            *steps(first, index + 1),
            *steps(second, index),
            *steps(third, index - 1),
            side(index),
        )
    interleave(*steps(third, len(groups) - 1))


def block_diagonal(queries, base, head_dim, group):
    count = queries.shape[1]
    first = base % group
    left = queries[base : base + head_dim]
    right = queries[base + head_dim : base + 2 * head_dim]
    zero = jnp.zeros((head_dim, count), queries.dtype)
    body = jnp.concatenate(
        [jnp.concatenate([left, zero], axis=1), jnp.concatenate([zero, right], axis=1)], axis=0
    )
    pad = jnp.zeros((group - 2 * head_dim, 2 * count), queries.dtype)
    return jnp.concatenate([body, pad] if first == 0 else [pad, body], axis=0)


def phase_kernel(bins, heads, *refs):
    blocks = refs[: bins // 2]
    gain, weights_in, table, out_weight = refs[bins // 2 : bins // 2 + 4]
    passed, *kept = refs[bins // 2 + 4 :]
    chunk, width = blocks[0].shape[1:]
    head_dim = width // heads
    scale = LOG2E / math.sqrt(head_dim)
    tile = ROWS * bins
    tiles = chunk // ROWS
    pairs = heads // 2
    group = 128
    stream = jnp.concatenate(
        [
            blocks[slot // 2][slot % 2, step * ROWS : (step + 1) * ROWS]
            for step in range(tiles)
            for slot in range(bins)
        ],
        axis=0,
    ).astype(jnp.float32)
    normed = rms(stream, gain[...])
    keys = mm(normed, weights_in[2 * width :]).astype(jnp.bfloat16)
    both = mm(weights_in[: 2 * width], normed, NT)
    queries = (both[:width] * scale).astype(jnp.bfloat16)
    values = both[width:].astype(jnp.bfloat16)
    ones = jnp.ones((ROWS, tile), jnp.bfloat16)
    units = [(step, pair) for step in range(tiles) for pair in range(pairs)]
    parts = []

    def first(unit, store):
        step, pair = unit
        span = slice(step * tile, (step + 1) * tile)
        base = pair * 2 * head_dim
        frame = base // group * group
        return score_steps(
            keys[span, frame : frame + group],
            block_diagonal(queries[:, span], base, head_dim, group),
            [(0, tile, table[pair])],
            store,
        )

    def third(unit, store):
        step, pair = unit
        span = slice(step * tile, (step + 1) * tile)
        base = pair * 2 * head_dim
        stack = jnp.concatenate([values[base : base + 2 * head_dim, span], ones], axis=0)
        parts.append(blend(mm(stack, store.pop("weights")), head_dim))
        yield

    def finish(steps):
        mixed = jnp.concatenate(
            [
                jnp.concatenate(parts[step * pairs : (step + 1) * pairs], axis=0)
                for step in steps
            ],
            axis=1,
        )
        span = slice(steps[0] * tile, (steps[-1] + 1) * tile)
        result = (stream[span] + mm(mixed, out_weight[...], TN)).astype(jnp.bfloat16)
        for index, step in enumerate(steps):
            for slot in range(bins):
                start = index * tile + slot * ROWS
                target = passed.at[slot // 2] if slot % 2 else kept[slot // 2]
                target[step * ROWS : (step + 1) * ROWS] = result[start : start + ROWS]

    run_pipeline(
        units,
        len(units),
        first,
        lambda _, store: soften_steps(store),
        third,
        lambda _: iter(()),
    )
    finish(range(tiles))


def join_kernel(taken, *refs):
    half = len(refs) // 2
    for step in range(half):
        refs[half + step][0] = refs[step][...]
        refs[half + step][1] = taken[step]


def gather_kernel(plane, masks, *refs):
    half = len(masks) // 2
    got = refs[:half]
    residual, inner, outer = refs[half:]
    me = lax.axis_index("phase")
    chunk = got[0].shape[1]
    for slot, mask in enumerate(masks):
        start = pl.multiple_of((me ^ mask) * chunk, ROWS)
        residual[pl.ds(start, chunk)] = got[slot // 2][slot % 2]
    reach = inner.shape[0]
    extra = residual.shape[0] - reach
    odd = lax.axis_index("space") % 2
    inner[...] = residual[pl.ds(pl.multiple_of((1 - odd) * extra, plane), reach)]
    outer[...] = residual[pl.ds(pl.multiple_of(odd * extra, plane), reach)]


def frame_of(keys, pair, head_dim, group):
    frame = pair * 2 * head_dim // group * group
    return keys[:, frame : frame + group]


def table_tiles(table, corner, pair, at, members, plane, z_first, depth):
    tiles = []
    for index, member in enumerate(members):
        z = z_first + member - REACH
        halves = []
        for side in range(2):
            step = member - REACH - at - corner[0, 2 * pair + side]
            inside = (step >= 0) & (step < SPAN) & (z >= 0) & (z < depth)
            start = pl.multiple_of(jnp.where(inside, step, SPAN) * plane, plane)
            halves.append(table[pair, pl.ds(start, plane), side * plane : (side + 1) * plane])
        tiles.append((index * plane, (index + 1) * plane, jnp.concatenate(halves, axis=1)))
    return tiles


def inside_kernel(
    plane, corner, own, gain_second, qkv, table, queries_out, values_out,
    part_mixed, part_top, part_sum
):
    tokens, width = own.shape
    planes = tokens // plane
    heads = corner.shape[1]
    pairs = heads // 2
    head_dim = width // heads
    scale = LOG2E / math.sqrt(head_dim)
    group = 128
    members = list(range(REACH, REACH + planes))
    z_first = lax.axis_index("space") * planes
    depth = lax.axis_size("space") * planes
    normed = rms(own[...].astype(jnp.float32), gain_second[...])
    keys = mm(normed, qkv[:, width : 2 * width]).astype(jnp.bfloat16)
    value_weight = qkv[:, 2 * width :].T
    values_out[...] = value_weight
    values = mm(value_weight, normed, NT).astype(jnp.bfloat16)
    queries = (mm(qkv[:, :width].T, normed, NT) * scale).astype(jnp.bfloat16)
    queries_out[...] = queries
    ones = jnp.ones((ROWS, tokens), jnp.bfloat16)
    frames = [frame_of(keys, pair, head_dim, group) for pair in range(pairs)]
    stacks = [
        jnp.concatenate([values[pair * 2 * head_dim : (pair + 1) * 2 * head_dim], ones], axis=0)
        for pair in range(pairs)
    ]
    units = [(at, pair) for at in range(planes) for pair in range(pairs)]

    def first(unit, store):
        at, pair = unit
        return score_steps(
            frames[pair],
            block_diagonal(
                queries[:, at * plane : (at + 1) * plane],
                pair * 2 * head_dim,
                head_dim,
                group,
            ),
            table_tiles(table, corner, pair, at, members, plane, z_first, depth),
            store,
        )

    def third(unit, store):
        at, pair = unit
        mixed = mm(stacks[pair], store.pop("weights"))
        base = pair * 2 * head_dim
        part_mixed[at, base : base + head_dim] = mixed[:head_dim, :plane]
        part_mixed[at, base + head_dim : base + 2 * head_dim] = mixed[
            head_dim : 2 * head_dim, plane:
        ]
        part_top[at, pair : pair + 1] = store["top"]
        part_sum[at, pair : pair + 1] = mixed[2 * head_dim : 2 * head_dim + 1]
        yield

    run_pipeline(units, 2, first, lambda _, store: soften_steps(store), third, lambda _: iter(()))


def outside_kernel(
    plane,
    corner,
    own,
    inner,
    outer,
    gain_second,
    qkv,
    table,
    queries,
    value_weight,
    part_mixed,
    part_top,
    part_sum,
    out_weight,
    gain_third,
    mlp_up,
    mlp_down,
    out,
    key_store,
    value_store,
):
    tokens, width = own.shape
    planes = tokens // plane
    heads = corner.shape[1]
    pairs = heads // 2
    head_dim = width // heads
    reach = REACH * plane
    group = 128
    gain = gain_second[...]
    place = lax.axis_index("space")
    is_even = place % 2 == 0
    z_first = place * planes
    depth = lax.axis_size("space") * planes
    key_weight = qkv[:, width : 2 * width]
    normed = jnp.concatenate(
        [rms(source[...].astype(jnp.float32), gain) for source in (inner, outer)], axis=0
    )
    keys = mm(normed, key_weight).astype(jnp.bfloat16)
    values = mm(value_weight[...], normed, NT).astype(jnp.bfloat16)
    for index, at_end in enumerate((is_even, jnp.logical_not(is_even))):
        rows = pl.ds(pl.multiple_of(jnp.where(at_end, reach, 0), plane), reach)
        part = slice(index * reach, (index + 1) * reach)
        key_store[rows] = keys[part]
        value_store[:, rows] = values[:, part]
    rim = list(range(REACH)) + list(range(REACH + planes, 2 * REACH + planes))
    ones = jnp.ones((ROWS, 2 * reach), jnp.bfloat16)
    frames = [frame_of(key_store, pair, head_dim, group) for pair in range(pairs)]
    stacks = [
        jnp.concatenate([value_store[pair * 2 * head_dim : (pair + 1) * 2 * head_dim], ones], axis=0)
        for pair in range(pairs)
    ]
    units = [(at, pair) for at in range(planes) for pair in range(pairs)]

    def span(at):
        return min(at, REACH), REACH + max(0, at + SPAN - planes)

    def first(unit, store):
        at, pair = unit
        start, stop = span(at)
        return score_steps(
            frames[pair][start * plane : stop * plane],
            block_diagonal(
                queries[:, at * plane : (at + 1) * plane],
                pair * 2 * head_dim,
                head_dim,
                group,
            ),
            table_tiles(table, corner, pair, at, rim[start:stop], plane, z_first, depth),
            store,
        )

    def second(unit, store):
        at, pair = unit
        before = part_top[at, pair : pair + 1]
        store["top"] = jnp.maximum(store["top"], before)
        store["ratio"] = jnp.exp2(before - store["top"])
        return soften_steps(store)

    parts = []

    def third(unit, store):
        at, pair = unit
        start, stop = span(at)
        mixed = mm(stacks[pair][:, start * plane : stop * plane], store.pop("weights"))
        ratio = store["ratio"]
        total = mixed[2 * head_dim : 2 * head_dim + 1] + ratio * part_sum[at, pair : pair + 1]
        inverse = 1.0 / total
        ratio = ratio * inverse
        halves = []
        for side in range(2):
            rows = slice(side * head_dim, (side + 1) * head_dim)
            lanes = slice(side * plane, (side + 1) * plane)
            base = (pair * 2 + side) * head_dim
            halves.append(
                mixed[rows, lanes] * inverse[:, lanes]
                + part_mixed[at, base : base + head_dim] * ratio[:, lanes]
            )
        parts.append(jnp.concatenate(halves, axis=0).astype(jnp.bfloat16))
        yield

    run_pipeline(units, 2, first, second, third, lambda _: iter(()))
    mixed = [jnp.concatenate(parts[at * pairs : (at + 1) * pairs], axis=0) for at in range(planes)]
    block = 2 * plane

    def mlp_steps(start):
        here = slice(start * plane, start * plane + block)
        joined = jnp.concatenate(mixed[start : start + 2], axis=1)
        residual = own[here].astype(jnp.float32) + mm(joined, out_weight[...], TN)
        normed = rms(residual, gain_third[...])
        yield
        hidden = gelu(mm(normed, mlp_up[...]).astype(jnp.bfloat16))
        yield
        out[here] = (residual + mm(hidden, mlp_down[...])).astype(out.dtype)

    interleave(*(mlp_steps(start) for start in range(0, planes, 2)))


def gelu(values):
    half = values * 0.5
    cubic = values * (GELU_LINEAR + GELU_CUBIC * (values * values))
    return half * (1.0 + jnp.tanh(cubic))


VMEM = pl.BlockSpec(memory_space=pltpu.VMEM)
SMEM = pl.BlockSpec(memory_space=pltpu.SMEM)
ANY = pl.BlockSpec(memory_space=pl.ANY)
HBM = pl.BlockSpec(memory_space=pltpu.HBM)


def call(kernel, specs, shapes, args, limit, scratch=(), flops=0, bytes_accessed=0):
    return pl.pallas_call(
        kernel,
        in_specs=specs,
        out_specs=[VMEM] * len(shapes),
        out_shape=[jax.ShapeDtypeStruct(shape, dtype) for shape, dtype in shapes],
        scratch_shapes=list(scratch),
        compiler_params=pltpu.CompilerParams(vmem_limit_bytes=limit * MIB),
        cost_estimate=pl.CostEstimate(
            flops=flops, bytes_accessed=bytes_accessed, transcendentals=0
        ),
    )(*args)


def local(
    volume,
    gain_first,
    phase_qkv,
    phase_out,
    bin_phase,
    phase_bias,
    gain_second,
    window_qkv,
    window_out,
    window_corner,
    window_bias,
    gain_third,
    mlp_up,
    mlp_down,
):
    planes, extent_x, extent_y, width = volume.shape[1:]
    plane = extent_x * extent_y
    tokens = planes * plane
    heads = window_corner.shape[0]
    bins = lax.axis_size("phase")
    half = bins // 2
    chunk = tokens // bins
    tile = ROWS * bins
    me = lax.axis_index("phase")
    bf16, f32 = jnp.bfloat16, jnp.float32

    def swap(block, mask):
        return lax.ppermute(block, "phase", [(i, i ^ mask) for i in range(bins)])

    own = volume.reshape(tokens, width)
    twin = swap(own, 1)

    def piece(mask):
        start = (me ^ mask) * chunk
        return jnp.stack(
            [lax.dynamic_slice_in_dim(source, start, chunk, axis=0) for source in (own, twin)]
        )

    masks = [0, 1] + [2 * step + part for step in [half - 1, *range(1, half - 1)] for part in range(2)]
    pieces = [piece(mask) for mask in masks[::2]]
    blocks = pieces[:1] + [swap(pieces[step], masks[2 * step]) for step in range(1, half)]
    corner = window_corner.T

    phase_weights, phase_table, window_table = call(
        functools.partial(prep_kernel, masks, extent_x, extent_y),
        [HBM] * 5 + [ANY],
        [
            ((3 * width, width), bf16),
            ((heads // 2, tile, 2 * tile), f32),
            ((heads // 2, (SPAN + 1) * plane, 2 * plane), f32),
        ],
        [
            *(
                pltpu.with_memory_space_constraint(array, pltpu.HBM)
                for array in (bin_phase, corner, window_bias, phase_bias, phase_qkv)
            ),
            pieces[-1],
        ],
        12,
        scratch=[
            pltpu.SMEM(bin_phase.shape, jnp.int32),
            pltpu.SMEM(corner.shape, jnp.int32),
            pltpu.SMEM(window_bias.shape, f32),
            pltpu.VMEM(phase_bias.shape, f32),
            pltpu.VMEM(phase_qkv.shape, bf16),
            pltpu.SemaphoreType.DMA((5,)),
        ],
        flops=2 * 10**9,
        bytes_accessed=4 * 2**20,
    )
    passed, *kept = call(
        functools.partial(phase_kernel, bins, heads),
        [VMEM] * (half + 4),
        [((half, chunk, width), bf16)] + [((chunk, width), bf16)] * half,
        [*blocks, gain_first.reshape(1, width), phase_weights, phase_table, phase_out],
        12,
        flops=2 * tokens * width * 5 * width,
        bytes_accessed=2**20,
    )
    results = call(
        join_kernel,
        [VMEM] * (half + 1),
        [((2, chunk, width), bf16)] * half,
        [swap(passed, 1), *kept],
        4,
    )
    got = [results[0]] + [swap(results[step], masks[2 * step]) for step in range(1, half)]
    reach = REACH * plane
    residual, inner, outer = call(
        functools.partial(gather_kernel, plane, masks),
        [VMEM] * half,
        [((tokens, width), bf16), ((reach, width), bf16), ((reach, width), bf16)],
        got,
        4,
    )
    count = lax.axis_size("space")

    def partners(shift):
        pairs = []
        for i in range(bins):
            for place in range(count):
                other = ((place + shift) ^ 1) - shift
                target = (i, other) if 0 <= other < count else (i ^ 1, place)
                pairs.append((i * count + place, target[0] * count + target[1]))
        return pairs

    inner = lax.ppermute(inner, ("phase", "space"), partners(0))
    outer = lax.ppermute(outer, ("phase", "space"), partners(1))
    gain = gain_second.reshape(1, width)
    pairs = heads // 2
    partial = call(
        functools.partial(inside_kernel, plane),
        [SMEM] + [VMEM] * 4,
        [
            ((width, tokens), bf16),
            ((width, width), bf16),
            ((planes, width, plane), f32),
            ((planes, pairs, 2 * plane), f32),
            ((planes, pairs, 2 * plane), f32),
        ],
        [corner, residual, gain, window_qkv, window_table],
        16,
        flops=2 * tokens * width * 14 * width,
        bytes_accessed=2**22,
    )
    (out,) = call(
        functools.partial(outside_kernel, plane),
        [SMEM] + [VMEM] * 15,
        [((tokens, width), bf16)],
        [
            corner,
            residual,
            inner,
            outer,
            gain,
            window_qkv,
            window_table,
            *partial,
            window_out,
            gain_third.reshape(1, width),
            mlp_up,
            mlp_down,
        ],
        20,
        scratch=[pltpu.VMEM((2 * reach, width), bf16), pltpu.VMEM((width, 2 * reach), bf16)],
        flops=2 * tokens * width * 14 * width,
        bytes_accessed=2**22,
    )
    return out.reshape(volume.shape)


def solution(mesh):
    split = P("phase", "space", None, None, None)
    in_specs = (split,) + (P(),) * 13
    return jax.shard_map(local, mesh=mesh, in_specs=in_specs, out_specs=split, check_vma=False)
```

```python
import functools
import math

import jax
import jax.numpy as jnp
from jax import lax
from jax.experimental import pallas as pl
from jax.experimental.pallas import tpu as pltpu
from jax.sharding import PartitionSpec as P

EPSILON = 1e-06
LOG2E = math.log2(math.e)
NEG = -1e30
SPAN = 4
REACH = SPAN - 1
ROWS = 16
MIB = 2**20
GELU_LINEAR = math.sqrt(2.0 / math.pi)
GELU_CUBIC = 0.044715 * GELU_LINEAR

NT = (((1,), (1,)), ((), ()))
TN = (((0,), (0,)), ((), ()))


def mm(a, b, dims=(((1,), (0,)), ((), ()))):
    return lax.dot_general(a, b, dims, preferred_element_type=jnp.float32)


def rms(values, gain):
    mean_sq = jnp.mean(values * values, axis=-1, keepdims=True)
    return (values * lax.rsqrt(mean_sq + EPSILON) * gain).astype(jnp.bfloat16)


def prep_kernel(
    masks,
    extent_x,
    extent_y,
    bin_phase_at,
    corner_at,
    window_bias_at,
    phase_bias_at,
    phase_qkv_at,
    _,
    phase_weights,
    phase_table,
    window_table,
    bin_phase,
    corner,
    window_bias,
    phase_bias,
    phase_qkv,
    sems,
):
    copies = [
        pltpu.make_async_copy(source, target, sems.at[index])
        for index, (source, target) in enumerate(
            (
                (bin_phase_at, bin_phase),
                (corner_at, corner),
                (window_bias_at, window_bias),
                (phase_bias_at, phase_bias),
                (phase_qkv_at, phase_qkv),
            )
        )
    ]
    for copy in copies:
        copy.start()
    for copy in copies:
        copy.wait()
    width = phase_qkv.shape[0]
    heads = phase_bias.shape[0]
    phase_weights[:width] = phase_qkv[:, :width].T
    phase_weights[width : 2 * width] = phase_qkv[:, 2 * width :].T
    phase_weights[2 * width :] = phase_qkv[:, width : 2 * width]
    me = lax.axis_index("phase")
    bins = len(masks)
    tile = ROWS * bins
    slot = lax.broadcasted_iota(jnp.int32, (heads, tile), 1) // ROWS
    query_phase = jnp.zeros((heads, tile), jnp.int32)
    for member, mask in enumerate(masks):
        query_phase = jnp.where(slot == member, bin_phase[me ^ mask], query_phase)
    same = (
        lax.broadcasted_iota(jnp.int32, (ROWS, tile), 0)
        == lax.broadcasted_iota(jnp.int32, (ROWS, tile), 1) % ROWS
    )
    bias = phase_bias[...] * LOG2E
    for member, mask in enumerate(masks):
        gap = bin_phase[me ^ mask] - query_phase
        gap = jnp.where(gap < 0, gap + bins, gap)
        value = jnp.zeros((heads, tile), jnp.float32)
        for step in range(bins):
            value = jnp.where(gap == step, bias[:, step : step + 1], value)
        for head in range(heads):
            phase_table[
                head // 2,
                member * ROWS : (member + 1) * ROWS,
                (head % 2) * tile : (head % 2 + 1) * tile,
            ] = jnp.where(same, value[head : head + 1], NEG)
    plane = extent_x * extent_y
    window_table[:, SPAN * plane :] = jnp.full(
        (heads // 2, plane, 2 * plane), NEG, window_table.dtype
    )
    shape = (extent_y, plane)
    lane = lax.broadcasted_iota(jnp.int32, shape, 1)
    lane_x = lane // extent_y
    delta_y = lax.broadcasted_iota(jnp.int32, shape, 0) - lane % extent_y
    for head in range(heads):
        first_x = corner[1, head]
        first_y = corner[2, head]
        y_masks = [delta_y == first_y + step for step in range(SPAN)]
        for step_z in range(SPAN):
            strips = []
            for step_x in range(SPAN):
                strip = jnp.full(shape, NEG, jnp.float32)
                for step_y in range(SPAN):
                    entry = window_bias[head, (step_z * SPAN + step_x) * SPAN + step_y] * LOG2E
                    strip = jnp.where(y_masks[step_y], entry, strip)
                strips.append(strip)
            for key_x in range(extent_x):
                block = jnp.full(shape, NEG, jnp.float32)
                for step_x in range(SPAN):
                    block = jnp.where(
                        lane_x == key_x - first_x - step_x, strips[step_x], block
                    )
                start = step_z * plane + key_x * extent_y
                window_table[
                    head // 2,
                    start : start + extent_y,
                    (head % 2) * plane : (head % 2 + 1) * plane,
                ] = block


def score_steps(keys, queries, tiles, store, whole=True):
    pieces = []
    tops = []
    joint = mm(keys, queries) if whole else None
    for start, stop, table in tiles:
        piece = (joint[start:stop] if whole else mm(keys[start:stop], queries)) + table
        pieces.append(piece)
        tops.append(jnp.max(piece.reshape(-1, 8, piece.shape[1]), axis=0))
        yield
    top = functools.reduce(jnp.maximum, tops)
    store["pieces"] = pieces
    store["top"] = jnp.max(top, axis=0, keepdims=True)


def soften_steps(store):
    weights = []
    for piece in store.pop("pieces"):
        weights.append(jnp.exp2((piece - store["top"]).astype(jnp.bfloat16)))
        yield
    store["weights"] = jnp.concatenate(weights, axis=0) if len(weights) > 1 else weights[0]


def blend(mixed, head_dim):
    count = mixed.shape[1] // 2
    inverse = 1.0 / mixed[2 * head_dim : 2 * head_dim + 1]
    return jnp.concatenate(
        [
            mixed[:head_dim, :count] * inverse[:, :count],
            mixed[head_dim : 2 * head_dim, count:] * inverse[:, count:],
        ],
        axis=0,
    ).astype(jnp.bfloat16)


def interleave(*steps):
    running = list(steps)
    while running:
        for step in list(running):
            try:
                next(step)
            except StopIteration:
                running.remove(step)


def run_pipeline(units, size, first, second, third, side):
    groups = [units[start : start + size] for start in range(0, len(units), size)]
    stores = {unit: {} for unit in units}

    def steps(action, index):
        if not 0 <= index < len(groups):
            return []
        return [action(unit, stores[unit]) for unit in groups[index]]

    interleave(*steps(first, 0))
    for index in range(len(groups)):
        interleave(
            *steps(first, index + 1),
            *steps(second, index),
            *steps(third, index - 1),
            side(index),
        )
    interleave(*steps(third, len(groups) - 1))


def block_diagonal(queries, base, head_dim, group):
    count = queries.shape[1]
    first = base % group
    left = queries[base : base + head_dim]
    right = queries[base + head_dim : base + 2 * head_dim]
    zero = jnp.zeros((head_dim, count), queries.dtype)
    body = jnp.concatenate(
        [jnp.concatenate([left, zero], axis=1), jnp.concatenate([zero, right], axis=1)], axis=0
    )
    pad = jnp.zeros((group - 2 * head_dim, 2 * count), queries.dtype)
    return jnp.concatenate([body, pad] if first == 0 else [pad, body], axis=0)


def phase_kernel(bins, heads, *refs):
    blocks = refs[: bins // 2]
    gain, weights_in, table, out_weight = refs[bins // 2 : bins // 2 + 4]
    passed, *kept = refs[bins // 2 + 4 :]
    chunk, width = blocks[0].shape[1:]
    head_dim = width // heads
    scale = LOG2E / math.sqrt(head_dim)
    tile = ROWS * bins
    tiles = chunk // ROWS
    pairs = heads // 2
    group = 128
    stream = jnp.concatenate(
        [
            blocks[slot // 2][slot % 2, step * ROWS : (step + 1) * ROWS]
            for step in range(tiles)
            for slot in range(bins)
        ],
        axis=0,
    ).astype(jnp.float32)
    normed = rms(stream, gain[...])
    keys = mm(normed, weights_in[2 * width :]).astype(jnp.bfloat16)
    both = mm(weights_in[: 2 * width], normed, NT)
    queries = (both[:width] * scale).astype(jnp.bfloat16)
    values = both[width:].astype(jnp.bfloat16)
    ones = jnp.ones((ROWS, tile), jnp.bfloat16)
    units = [(step, pair) for step in range(tiles) for pair in range(pairs)]
    parts = []

    def first(unit, store):
        step, pair = unit
        span = slice(step * tile, (step + 1) * tile)
        base = pair * 2 * head_dim
        frame = base // group * group
        return score_steps(
            keys[span, frame : frame + group],
            block_diagonal(queries[:, span], base, head_dim, group),
            [(0, tile, table[pair])],
            store,
        )

    def third(unit, store):
        step, pair = unit
        span = slice(step * tile, (step + 1) * tile)
        base = pair * 2 * head_dim
        stack = jnp.concatenate([values[base : base + 2 * head_dim, span], ones], axis=0)
        parts.append(blend(mm(stack, store.pop("weights")), head_dim))
        yield

    def finish(steps):
        mixed = jnp.concatenate(
            [
                jnp.concatenate(parts[step * pairs : (step + 1) * pairs], axis=0)
                for step in steps
            ],
            axis=1,
        )
        span = slice(steps[0] * tile, (steps[-1] + 1) * tile)
        result = (stream[span] + mm(mixed, out_weight[...], TN)).astype(jnp.bfloat16)
        for index, step in enumerate(steps):
            for slot in range(bins):
                start = index * tile + slot * ROWS
                target = passed.at[slot // 2] if slot % 2 else kept[slot // 2]
                target[step * ROWS : (step + 1) * ROWS] = result[start : start + ROWS]

    run_pipeline(
        units,
        len(units),
        first,
        lambda _, store: soften_steps(store),
        third,
        lambda _: iter(()),
    )
    finish(range(tiles))


def join_kernel(taken, *refs):
    half = len(refs) // 2
    for step in range(half):
        refs[half + step][0] = refs[step][...]
        refs[half + step][1] = taken[step]


def gather_kernel(plane, masks, *refs):
    half = len(masks) // 2
    got = refs[:half]
    residual, inner, outer = refs[half:]
    me = lax.axis_index("phase")
    chunk = got[0].shape[1]
    for slot, mask in enumerate(masks):
        start = pl.multiple_of((me ^ mask) * chunk, ROWS)
        residual[pl.ds(start, chunk)] = got[slot // 2][slot % 2]
    reach = inner.shape[0]
    extra = residual.shape[0] - reach
    odd = lax.axis_index("space") % 2
    inner[...] = residual[pl.ds(pl.multiple_of((1 - odd) * extra, plane), reach)]
    outer[...] = residual[pl.ds(pl.multiple_of(odd * extra, plane), reach)]


def frame_of(keys, pair, head_dim, group):
    frame = pair * 2 * head_dim // group * group
    return keys[:, frame : frame + group]


def table_tiles(table, corner, pair, at, members, plane, z_first, depth):
    tiles = []
    for index, member in enumerate(members):
        z = z_first + member - REACH
        halves = []
        for side in range(2):
            step = member - REACH - at - corner[0, 2 * pair + side]
            inside = (step >= 0) & (step < SPAN) & (z >= 0) & (z < depth)
            start = pl.multiple_of(jnp.where(inside, step, SPAN) * plane, plane)
            halves.append(table[pair, pl.ds(start, plane), side * plane : (side + 1) * plane])
        tiles.append((index * plane, (index + 1) * plane, jnp.concatenate(halves, axis=1)))
    return tiles


def inside_kernel(
    plane, corner, own, gain_second, qkv, table, queries_out, values_out,
    part_mixed, part_top, part_sum
):
    tokens, width = own.shape
    planes = tokens // plane
    heads = corner.shape[1]
    pairs = heads // 2
    head_dim = width // heads
    scale = LOG2E / math.sqrt(head_dim)
    group = 128
    members = list(range(REACH, REACH + planes))
    z_first = lax.axis_index("space") * planes
    depth = lax.axis_size("space") * planes
    normed = rms(own[...].astype(jnp.float32), gain_second[...])
    keys = mm(normed, qkv[:, width : 2 * width]).astype(jnp.bfloat16)
    value_weight = qkv[:, 2 * width :].T
    values_out[...] = value_weight
    values = mm(value_weight, normed, NT).astype(jnp.bfloat16)
    queries = (mm(qkv[:, :width].T, normed, NT) * scale).astype(jnp.bfloat16)
    queries_out[...] = queries
    ones = jnp.ones((ROWS, tokens), jnp.bfloat16)
    frames = [frame_of(keys, pair, head_dim, group) for pair in range(pairs)]
    stacks = [
        jnp.concatenate([values[pair * 2 * head_dim : (pair + 1) * 2 * head_dim], ones], axis=0)
        for pair in range(pairs)
    ]
    units = [(at, pair) for at in range(planes) for pair in range(pairs)]

    def first(unit, store):
        at, pair = unit
        return score_steps(
            frames[pair],
            block_diagonal(
                queries[:, at * plane : (at + 1) * plane],
                pair * 2 * head_dim,
                head_dim,
                group,
            ),
            table_tiles(table, corner, pair, at, members, plane, z_first, depth),
            store,
            whole=False,
        )

    def third(unit, store):
        at, pair = unit
        mixed = mm(stacks[pair], store.pop("weights"))
        base = pair * 2 * head_dim
        part_mixed[at, base : base + head_dim] = mixed[:head_dim, :plane]
        part_mixed[at, base + head_dim : base + 2 * head_dim] = mixed[
            head_dim : 2 * head_dim, plane:
        ]
        part_top[at, pair : pair + 1] = store["top"]
        part_sum[at, pair : pair + 1] = mixed[2 * head_dim : 2 * head_dim + 1]
        yield

    run_pipeline(units, 2, first, lambda _, store: soften_steps(store), third, lambda _: iter(()))


def outside_kernel(
    plane,
    corner,
    own,
    inner,
    outer,
    gain_second,
    qkv,
    table,
    queries,
    value_weight,
    part_mixed,
    part_top,
    part_sum,
    out_weight,
    gain_third,
    mlp_up,
    mlp_down,
    out,
    key_store,
    value_store,
):
    tokens, width = own.shape
    planes = tokens // plane
    heads = corner.shape[1]
    pairs = heads // 2
    head_dim = width // heads
    reach = REACH * plane
    group = 128
    gain = gain_second[...]
    place = lax.axis_index("space")
    is_even = place % 2 == 0
    z_first = place * planes
    depth = lax.axis_size("space") * planes
    key_weight = qkv[:, width : 2 * width]
    normed = jnp.concatenate(
        [rms(source[...].astype(jnp.float32), gain) for source in (inner, outer)], axis=0
    )
    keys = mm(normed, key_weight).astype(jnp.bfloat16)
    values = mm(value_weight[...], normed, NT).astype(jnp.bfloat16)
    for index, at_end in enumerate((is_even, jnp.logical_not(is_even))):
        rows = pl.ds(pl.multiple_of(jnp.where(at_end, reach, 0), plane), reach)
        part = slice(index * reach, (index + 1) * reach)
        key_store[rows] = keys[part]
        value_store[:, rows] = values[:, part]
    rim = list(range(REACH)) + list(range(REACH + planes, 2 * REACH + planes))
    ones = jnp.ones((ROWS, 2 * reach), jnp.bfloat16)
    frames = [frame_of(key_store, pair, head_dim, group) for pair in range(pairs)]
    stacks = [
        jnp.concatenate([value_store[pair * 2 * head_dim : (pair + 1) * 2 * head_dim], ones], axis=0)
        for pair in range(pairs)
    ]
    units = [(at, pair) for at in range(planes) for pair in range(pairs)]

    def span(at):
        return min(at, REACH), REACH + max(0, at + SPAN - planes)

    def first(unit, store):
        at, pair = unit
        start, stop = span(at)
        return score_steps(
            frames[pair][start * plane : stop * plane],
            block_diagonal(
                queries[:, at * plane : (at + 1) * plane],
                pair * 2 * head_dim,
                head_dim,
                group,
            ),
            table_tiles(table, corner, pair, at, rim[start:stop], plane, z_first, depth),
            store,
        )

    def second(unit, store):
        at, pair = unit
        before = part_top[at, pair : pair + 1]
        store["top"] = jnp.maximum(store["top"], before)
        store["ratio"] = jnp.exp2(before - store["top"])
        return soften_steps(store)

    parts = []

    def third(unit, store):
        at, pair = unit
        start, stop = span(at)
        mixed = mm(stacks[pair][:, start * plane : stop * plane], store.pop("weights"))
        ratio = store["ratio"]
        total = mixed[2 * head_dim : 2 * head_dim + 1] + ratio * part_sum[at, pair : pair + 1]
        inverse = 1.0 / total
        ratio = ratio * inverse
        halves = []
        for side in range(2):
            rows = slice(side * head_dim, (side + 1) * head_dim)
            lanes = slice(side * plane, (side + 1) * plane)
            base = (pair * 2 + side) * head_dim
            halves.append(
                mixed[rows, lanes] * inverse[:, lanes]
                + part_mixed[at, base : base + head_dim] * ratio[:, lanes]
            )
        parts.append(jnp.concatenate(halves, axis=0).astype(jnp.bfloat16))
        yield

    run_pipeline(units, 2, first, second, third, lambda _: iter(()))
    mixed = [jnp.concatenate(parts[at * pairs : (at + 1) * pairs], axis=0) for at in range(planes)]
    block = 2 * plane

    def mlp_steps(start):
        here = slice(start * plane, start * plane + block)
        joined = jnp.concatenate(mixed[start : start + 2], axis=1)
        residual = own[here].astype(jnp.float32) + mm(joined, out_weight[...], TN)
        normed = rms(residual, gain_third[...])
        yield
        hidden = gelu(mm(normed, mlp_up[...]).astype(jnp.bfloat16))
        yield
        out[here] = (residual + mm(hidden, mlp_down[...])).astype(out.dtype)

    interleave(*(mlp_steps(start) for start in range(0, planes, 2)))


def gelu(values):
    half = values * 0.5
    cubic = values * (GELU_LINEAR + GELU_CUBIC * (values * values))
    return half * (1.0 + jnp.tanh(cubic))


VMEM = pl.BlockSpec(memory_space=pltpu.VMEM)
SMEM = pl.BlockSpec(memory_space=pltpu.SMEM)
ANY = pl.BlockSpec(memory_space=pl.ANY)
HBM = pl.BlockSpec(memory_space=pltpu.HBM)


def call(kernel, specs, shapes, args, limit, scratch=(), flops=0, bytes_accessed=0):
    return pl.pallas_call(
        kernel,
        in_specs=specs,
        out_specs=[VMEM] * len(shapes),
        out_shape=[jax.ShapeDtypeStruct(shape, dtype) for shape, dtype in shapes],
        scratch_shapes=list(scratch),
        compiler_params=pltpu.CompilerParams(vmem_limit_bytes=limit * MIB),
        cost_estimate=pl.CostEstimate(
            flops=flops, bytes_accessed=bytes_accessed, transcendentals=0
        ),
    )(*args)


def local(
    volume,
    gain_first,
    phase_qkv,
    phase_out,
    bin_phase,
    phase_bias,
    gain_second,
    window_qkv,
    window_out,
    window_corner,
    window_bias,
    gain_third,
    mlp_up,
    mlp_down,
):
    planes, extent_x, extent_y, width = volume.shape[1:]
    plane = extent_x * extent_y
    tokens = planes * plane
    heads = window_corner.shape[0]
    bins = lax.axis_size("phase")
    half = bins // 2
    chunk = tokens // bins
    tile = ROWS * bins
    me = lax.axis_index("phase")
    bf16, f32 = jnp.bfloat16, jnp.float32

    def swap(block, mask):
        return lax.ppermute(block, "phase", [(i, i ^ mask) for i in range(bins)])

    own = volume.reshape(tokens, width)
    twin = swap(own, 1)

    def piece(mask):
        start = (me ^ mask) * chunk
        return jnp.stack(
            [lax.dynamic_slice_in_dim(source, start, chunk, axis=0) for source in (own, twin)]
        )

    masks = [0, 1] + [2 * step + part for step in [half - 1, *range(1, half - 1)] for part in range(2)]
    pieces = [piece(mask) for mask in masks[::2]]
    blocks = pieces[:1] + [swap(pieces[step], masks[2 * step]) for step in range(1, half)]
    corner = window_corner.T

    phase_weights, phase_table, window_table = call(
        functools.partial(prep_kernel, masks, extent_x, extent_y),
        [HBM] * 5 + [ANY],
        [
            ((3 * width, width), bf16),
            ((heads // 2, tile, 2 * tile), f32),
            ((heads // 2, (SPAN + 1) * plane, 2 * plane), f32),
        ],
        [
            *(
                pltpu.with_memory_space_constraint(array, pltpu.HBM)
                for array in (bin_phase, corner, window_bias, phase_bias, phase_qkv)
            ),
            pieces[-1],
        ],
        12,
        scratch=[
            pltpu.SMEM(bin_phase.shape, jnp.int32),
            pltpu.SMEM(corner.shape, jnp.int32),
            pltpu.SMEM(window_bias.shape, f32),
            pltpu.VMEM(phase_bias.shape, f32),
            pltpu.VMEM(phase_qkv.shape, bf16),
            pltpu.SemaphoreType.DMA((5,)),
        ],
        flops=2 * 10**9,
        bytes_accessed=4 * 2**20,
    )
    passed, *kept = call(
        functools.partial(phase_kernel, bins, heads),
        [VMEM] * (half + 4),
        [((half, chunk, width), bf16)] + [((chunk, width), bf16)] * half,
        [*blocks, gain_first.reshape(1, width), phase_weights, phase_table, phase_out],
        12,
        flops=2 * tokens * width * 5 * width,
        bytes_accessed=2**20,
    )
    results = call(
        join_kernel,
        [VMEM] * (half + 1),
        [((2, chunk, width), bf16)] * half,
        [swap(passed, 1), *kept],
        4,
    )
    got = [results[0]] + [swap(results[step], masks[2 * step]) for step in range(1, half)]
    reach = REACH * plane
    residual, inner, outer = call(
        functools.partial(gather_kernel, plane, masks),
        [VMEM] * half,
        [((tokens, width), bf16), ((reach, width), bf16), ((reach, width), bf16)],
        got,
        4,
    )
    count = lax.axis_size("space")

    def partners(shift):
        pairs = []
        for i in range(bins):
            for place in range(count):
                other = ((place + shift) ^ 1) - shift
                target = (i, other) if 0 <= other < count else (i ^ 1, place)
                pairs.append((i * count + place, target[0] * count + target[1]))
        return pairs

    inner = lax.ppermute(inner, ("phase", "space"), partners(0))
    outer = lax.ppermute(outer, ("phase", "space"), partners(1))
    gain = gain_second.reshape(1, width)
    pairs = heads // 2
    partial = call(
        functools.partial(inside_kernel, plane),
        [SMEM] + [VMEM] * 4,
        [
            ((width, tokens), bf16),
            ((width, width), bf16),
            ((planes, width, plane), f32),
            ((planes, pairs, 2 * plane), f32),
            ((planes, pairs, 2 * plane), f32),
        ],
        [corner, residual, gain, window_qkv, window_table],
        16,
        flops=2 * tokens * width * 14 * width,
        bytes_accessed=2**22,
    )
    (out,) = call(
        functools.partial(outside_kernel, plane),
        [SMEM] + [VMEM] * 15,
        [((tokens, width), bf16)],
        [
            corner,
            residual,
            inner,
            outer,
            gain,
            window_qkv,
            window_table,
            *partial,
            window_out,
            gain_third.reshape(1, width),
            mlp_up,
            mlp_down,
        ],
        20,
        scratch=[pltpu.VMEM((2 * reach, width), bf16), pltpu.VMEM((width, 2 * reach), bf16)],
        flops=2 * tokens * width * 14 * width,
        bytes_accessed=2**22,
    )
    return out.reshape(volume.shape)


def solution(mesh):
    split = P("phase", "space", None, None, None)
    in_specs = (split,) + (P(),) * 13
    return jax.shard_map(local, mesh=mesh, in_specs=in_specs, out_specs=split, check_vma=False)
```
